32 devices in a mesh: gx: 16 (over z, x, core), gy: 2 (over y).
Axes of the slice: x: 2, y: 2, z: 4, core: 2. Of those that a mesh axis runs over, the one named last changes fastest.
Arguments:
- features: bfloat16 [16, 2, 3, 64, 256], P('gx', 'gy'), may hold values from -6 to 6
- block_coords: int32 [16, 2, 3], P('gx', 'gy'), may hold values from 0 to 31, as said below
- block_counts: int32 [16, 2], P('gx', 'gy'), may hold values from 2 to 3, as said below
- first_weight: bfloat16 [6912, 256], replicated, may hold values from -0.078125 to 0.078125
- second_weight: bfloat16 [6912, 256], replicated, may hold values from -0.078125 to 0.078125
- cotangent: bfloat16 [16, 2, 3, 64, 256], P('gx', 'gy'), may hold values from -6 to 6
Outputs:
- output_features: float32 [16, 2, 3, 64, 256], P('gx', 'gy')
- input_grad: float32 [16, 2, 3, 64, 256], P('gx', 'gy')
- first_weight_grad: float32 [6912, 256], P('gx', 'gy')
- second_weight_grad: float32 [6912, 256], P('gx', 'gy')
The draws below stay inside these ranges and needn't reach their ends.
Inputs may be any that keep to these rules, and one draw needn't show every extreme that they name: `block_coords`: within a tile all 3 entries are distinct block positions, so slots at or past the tile's count name blocks that are not active. Slots 0 and 1 are always live and hold blocks of the lowest block layer in opposite corners of the tile's 2 x 2 block columns. `block_counts`: at least one tile holds 3 live slots in every draw.
All inputs are finite; a program needn't handle non-finite values.
Results may differ from the reference program's by a relative error of at most 0.0029.
Values may be sent and summed in bfloat16 or wider, within the bound.
No kernel may reach another device: no remote copies, remote signals or barrier semaphores. Data moves between devices by JAX's collectives and lax.ppermute only.
A program may use at most 128 MiB of HBM per device.

```python
import math
import jax
import jax.numpy as jnp
from jax import lax

C = 256
SLAB_BLOCKS = 8
MAX_BLOCKS = 3
TILE_ROWS = 16
TILE_COLS = 2


def draw_block_counts(key, part):
    key_base, key_busy, key_pick = jax.random.split(key, 3)
    upper_bound = max(4, MAX_BLOCKS // 2 + 2)
    base_count = jax.random.randint(key_base, (TILE_ROWS, TILE_COLS), 2, upper_bound)
    busy_tiles = jax.random.randint(key_busy, (TILE_ROWS, TILE_COLS), 0, 16) == 0
    counts_drawn = jnp.where(busy_tiles, MAX_BLOCKS, jnp.minimum(base_count, MAX_BLOCKS))
    pick_tile = jax.random.randint(key_pick, (), 0, TILE_ROWS * TILE_COLS)
    flat_counts = jnp.where(jnp.arange(TILE_ROWS * TILE_COLS) == pick_tile, MAX_BLOCKS, counts_drawn.reshape(-1))
    return flat_counts.reshape(TILE_ROWS, TILE_COLS).astype(jnp.int32)


def draw_block_coords(key, part):
    positions = 4 * SLAB_BLOCKS
    tile_total = TILE_ROWS * TILE_COLS
    key_ground, key_order = jax.random.split(key)
    corner = jax.random.randint(key_ground, (tile_total,), 0, 4)
    ground_first = corner * SLAB_BLOCKS
    ground_second = (3 - corner) * SLAB_BLOCKS
    orders = jax.vmap(lambda subkey: jax.random.permutation(subkey, positions))(jax.random.split(key_order, tile_total))
    taken_mask = (orders == ground_first[:, None]) | (orders == ground_second[:, None])
    order_rank = jnp.argsort(taken_mask.astype(jnp.int32), axis=1, stable=True)
    remaining = jnp.take_along_axis(orders, order_rank, axis=1)
    chosen = jnp.concatenate([ground_first[:, None], ground_second[:, None], remaining[:, :MAX_BLOCKS - 2]], axis=1)
    return chosen.reshape(TILE_ROWS, TILE_COLS, MAX_BLOCKS).astype(jnp.int32)


def steps_of(rng, shape, cuts, least, top_value):
    def one(position, shards_of):
        steps = jax.random.uniform(jax.random.fold_in(jax.random.fold_in(rng, 6), position), (shards_of,), jnp.float32, least / len(cuts), top_value / len(cuts))
        return jnp.repeat(jnp.exp(steps), shape[position] // shards_of).reshape((-1,) + (1,) * (len(shape) - position - 1))

    loudness = one(*cuts[0])
    for cut in cuts[1:]:
        loudness = loudness * one(*cut)
    return loudness


def scatter_about(rng, dims, deviation, limit, cuts=(), kind=jnp.bfloat16):
    array = jax.random.normal(rng, dims, jnp.float32) * deviation
    if len(cuts) > 0:
        array = steps_of(rng, dims, cuts, -0.22, 0.18) * array
    return jnp.clip(array, min=-limit, max=limit).astype(kind)


def setup_inputs(seed: int = 0) -> dict:
    seeds = jax.random.split(jax.random.key(seed), 7)
    return {
        "features": scatter_about(seeds[0], (TILE_ROWS, TILE_COLS, MAX_BLOCKS, 64, C), 1.0, 6.0, ((0, 16), (1, 2))),
        "block_coords": draw_block_coords(jax.random.fold_in(seeds[6], 71), 0),
        "block_counts": draw_block_counts(jax.random.fold_in(seeds[6], 71), 0),
        "first_weight": scatter_about(seeds[3], (27 * C, C), (27 * C) ** -0.5, 0.078125),
        "second_weight": scatter_about(seeds[4], (27 * C, C), (27 * C) ** -0.5, 0.078125),
        "cotangent": scatter_about(seeds[5], (TILE_ROWS, TILE_COLS, MAX_BLOCKS, 64, C), 1.0, 6.0, ((0, 16), (1, 2))),
    }


def tile_grid(field, slot_blocks, live_count):
    positions = jnp.arange(4 * SLAB_BLOCKS, dtype=jnp.int32)
    slot_index = jnp.arange(MAX_BLOCKS, dtype=jnp.int32)
    placing = (slot_blocks[:, None] == positions[None, :]) & (slot_index < live_count)[:, None]
    blocks = jnp.einsum('sp,svc->pvc', placing.astype(jnp.float32), field.astype(jnp.float32))
    blocks = blocks.reshape(2, 2, SLAB_BLOCKS, 4, 4, 4, C).transpose(0, 3, 1, 4, 2, 5, 6)
    return blocks.reshape(8, 8, 4 * SLAB_BLOCKS, C)

def padded_tile(field, block_coords, block_counts, tile_row, tile_col):
    strips = []
    for step_row in (-1, 0, 1):
        pieces = []
        for step_col in (-1, 0, 1):
            row_near = tile_row + step_row
            col_near = tile_col + step_col
            inside = (row_near >= 0) & (row_near < TILE_ROWS) & (col_near >= 0) & (col_near < TILE_COLS)
            row_safe = jnp.clip(row_near, 0, TILE_ROWS - 1)
            col_safe = jnp.clip(col_near, 0, TILE_COLS - 1)
            grid = tile_grid(field[row_safe, col_safe], block_coords[row_safe, col_safe], block_counts[row_safe, col_safe])
            pieces.append(jnp.where(inside, grid, jnp.zeros((), jnp.float32)))
        strips.append(jnp.concatenate(pieces, axis=1))
    whole = jnp.concatenate(strips, axis=0)
    return jnp.pad(whole[7:17, 7:17], ((0, 0), (0, 0), (1, 1), (0, 0)))

def columns(padded, slot_blocks):
    chan_width = padded.shape[3]
    start_x = slot_blocks // (2 * SLAB_BLOCKS)
    start_y = slot_blocks // SLAB_BLOCKS % 2
    start_z = slot_blocks % SLAB_BLOCKS

    def cut_cube(block_x, block_y, block_z):
        return lax.dynamic_slice(padded, (4 * block_x, 4 * block_y, 4 * block_z, block_x * 0), (6, 6, 6, chan_width))
    cubes = jax.vmap(cut_cube)(start_x, start_y, start_z)
    tap_list = []
    for tap_index in range(27):
        shift_x = tap_index // 9
        shift_y = tap_index // 3 % 3
        shift_z = tap_index % 3
        piece = cubes[:, shift_x:shift_x + 4, shift_y:shift_y + 4, shift_z:shift_z + 4, :]
        tap_list.append(piece.reshape(-1, chan_width))
    return jnp.concatenate(tap_list, axis=1)

def transposed(cols, weight):
    chan_width = weight.shape[1]
    stacked = cols.reshape(cols.shape[0], 27, chan_width).astype(jnp.float32)
    flipped = weight.reshape(27, chan_width, chan_width)[::-1].astype(jnp.float32)
    return jnp.einsum('rkc,kic->ri', stacked, flipped)

def reference(features, block_coords, block_counts, first_weight, second_weight, cotangent):
    tile_total = TILE_ROWS * TILE_COLS
    tile_ids = jnp.arange(tile_total, dtype=jnp.int32)
    grad_scale = 1.0 / math.sqrt(64 * MAX_BLOCKS * tile_total)

    def tile_columns(field, tile):
        tile_row = tile // TILE_COLS
        tile_col = tile % TILE_COLS
        padded = padded_tile(field, block_coords, block_counts, tile_row, tile_col)
        return columns(padded, block_coords[tile_row, tile_col]).astype(jnp.bfloat16)

    def row_live_of(tile):
        live_count = block_counts[tile // TILE_COLS, tile % TILE_COLS]
        return jnp.repeat(jnp.arange(MAX_BLOCKS, dtype=jnp.int32) < live_count, 64)[:, None]

    def rows_of(field, tile):
        return field[tile // TILE_COLS, tile % TILE_COLS].reshape(64 * MAX_BLOCKS, C)

    def forward_hidden(tile):
        pre_first = jnp.dot(tile_columns(features, tile), first_weight, preferred_element_type=jnp.float32)
        return jnp.where(row_live_of(tile), jax.nn.silu(pre_first), jnp.zeros((), jnp.float32)).astype(jnp.bfloat16)
    hidden_all = lax.map(forward_hidden, tile_ids).reshape(features.shape)

    def second_pass(grad_total, tile):
        row_live = row_live_of(tile)
        feature_cols = tile_columns(features, tile)
        pre_first = jnp.dot(feature_cols, first_weight, preferred_element_type=jnp.float32)
        hidden_cols = tile_columns(hidden_all, tile)
        output_rows = jnp.where(row_live, jnp.dot(hidden_cols, second_weight, preferred_element_type=jnp.float32), jnp.zeros((), jnp.float32))
        seed_rows = jnp.where(row_live, rows_of(cotangent, tile).astype(jnp.float32), jnp.zeros((), jnp.float32)).astype(jnp.bfloat16)
        grad_total = grad_total + jnp.dot(hidden_cols.T, seed_rows, preferred_element_type=jnp.float32)
        hidden_grad = transposed(tile_columns(cotangent, tile), second_weight)
        sigmoid_pre = jax.nn.sigmoid(pre_first)
        pre_grad = jnp.where(row_live, hidden_grad * sigmoid_pre * (1.0 + pre_first * (1.0 - sigmoid_pre)), jnp.zeros((), jnp.float32)).astype(jnp.bfloat16)
        return (grad_total, (output_rows, pre_grad))
    second_total, (output_all, pre_grad_all) = lax.scan(second_pass, jnp.zeros((27 * C, C), jnp.float32), tile_ids)
    pre_grad_all = pre_grad_all.reshape(features.shape)

    def third_pass(grad_total, tile):
        row_live = row_live_of(tile)
        feature_cols = tile_columns(features, tile)
        grad_total = grad_total + jnp.dot(feature_cols.T, rows_of(pre_grad_all, tile), preferred_element_type=jnp.float32)
        input_rows = jnp.where(row_live, transposed(tile_columns(pre_grad_all, tile), first_weight), jnp.zeros((), jnp.float32))
        return (grad_total, input_rows)
    first_total, input_all = lax.scan(third_pass, jnp.zeros((27 * C, C), jnp.float32), tile_ids)
    return (output_all.reshape(features.shape), input_all.reshape(features.shape), first_total * grad_scale, second_total * grad_scale)
```

```python
import functools
import math

import jax
import jax.numpy as jnp
import numpy as np
from jax import lax
from jax.experimental import pallas as pl
from jax.experimental.pallas import tpu as pltpu
from jax.sharding import PartitionSpec as P

C = 256
TAPS = 27
PLANE = 16
STEP_Y = 64.0
STEP_X = 4096.0
NOWHERE = -1.0e7
META_ROWS = 16
VMEM = pltpu.MemorySpace.VMEM
SMEM = pltpu.MemorySpace.SMEM


def params(mib):
    return pltpu.CompilerParams(vmem_limit_bytes=mib * 2**20)


def dot(lhs, rhs, dims=((1,), (0,))):
    return lax.dot_general(lhs, rhs, (dims, ((), ())), preferred_element_type=jnp.float32)


def source_codes(metas, offsets, width):
    lane = lax.broadcasted_iota(jnp.int32, (1, 512), 1)
    total = jnp.full((1, 512), NOWHERE, jnp.float32)
    for place, (meta, offset) in enumerate(zip(metas, offsets)):
        rows = meta.astype(jnp.float32)
        parts = []
        for half in range(2):
            x, y, z, live = (rows[4 * half + i : 4 * half + i + 1] for i in range(4))
            parts.append(
                jnp.where(live > 0.5, x * STEP_X + y * STEP_Y + z + offset, NOWHERE)
            )
        code = jnp.concatenate(parts, axis=1)
        inside = (lane >= place * width) & (lane < (place + 1) * width)
        total = jnp.where(inside, code, total)
    return total


def selectors(metas, where_ref, own_code, sides, width):
    near = where_ref[0].astype(jnp.float32) * (2 * STEP_X)
    side_offsets = [where_ref[1 + i].astype(jnp.float32) * (8 * STEP_Y) for i in range(sides)]
    offsets = [0.0] + side_offsets + [near, -near]
    for side_offset in side_offsets:
        offsets += [near + side_offset, side_offset - near]
    codes = source_codes(metas, offsets, width)
    edge = codes[:, : 3 * (1 + sides) * width]
    middle = codes[:, : (1 + sides) * width]
    return tuple(
        (source == own_code + step).astype(jnp.float32).astype(jnp.bfloat16)
        for source, step in ((edge, -STEP_X), (middle, 0.0), (edge, STEP_X))
    )


def fill(cols_ref, tiles, faces, chosen, width):
    for plane in range(6):
        if plane == 0:
            pieces = [tile[3 * width : 4 * width] for tile in tiles] + faces
            select = chosen[0]
        elif plane == 5:
            pieces = [tile[0:width] for tile in tiles] + faces
            select = chosen[2]
        else:
            pieces = [tile[(plane - 1) * width : plane * width] for tile in tiles]
            select = chosen[1]
        moved = dot(select, jnp.concatenate(pieces, axis=0)).astype(jnp.bfloat16)
        for shift in range(9):
            cols_ref[shift, plane * width : (plane + 1) * width, :] = moved[
                shift * width : (shift + 1) * width
            ]


def tap_rows(cols_ref, tap, width):
    start = tap // 9 * width
    return cols_ref[tap % 9, start : start + 4 * width, :]


def conv(cols_ref, weight_ref, width):
    total = None
    for tap in range(TAPS):
        term = dot(tap_rows(cols_ref, tap, width), weight_ref[tap * C : (tap + 1) * C, :])
        total = term if total is None else total + term
    return total


def conv_back(cols_ref, weight_ref, width):
    total = None
    for tap in range(TAPS):
        weight = weight_ref[(26 - tap) * C : (27 - tap) * C, :]
        term = dot(tap_rows(cols_ref, tap, width), weight, ((1,), (1,)))
        total = term if total is None else total + term
    return total


def live_rows(where_ref, sides, slots):
    row = lax.broadcasted_iota(jnp.int32, (4 * slots * PLANE, 1), 0)
    slot = (row // PLANE) % slots
    return slot < where_ref[1 + sides]


def neighbourhood(own_ref, side_refs, far_ref, fdiag_refs, near_ref, rows, width):
    sides = len(side_refs)
    faced = 2 * width
    near_at = faced + META_ROWS
    metas = [own_ref[rows : rows + 8, :]]
    metas += [ref[rows : rows + 8, :] for ref in side_refs]
    metas += [near_ref[faced : faced + 8, :], far_ref[faced : faced + 8, :]]
    for i, ref in enumerate(fdiag_refs):
        start = (i + 1) * near_at + faced
        metas += [near_ref[start : start + 8, :], ref[faced : faced + 8, :]]
    fields = []
    for field in range(2):
        top = field * (rows // 2)
        tiles = [own_ref.at[top : top + rows // 2]]
        tiles += [ref.at[top : top + rows // 2] for ref in side_refs]
        face = field * width
        faces = [near_ref[face : face + width, :], far_ref[face : face + width, :]]
        for i, ref in enumerate(fdiag_refs):
            start = (i + 1) * near_at + face
            faces += [near_ref[start : start + width, :], ref[face : face + width, :]]
        fields.append((tiles, faces))
    return metas, fields


def first_kernel(slots, sides, *refs):
    where_ref, code_ref, own_ref = refs[:3]
    side_refs, refs = refs[3 : 3 + sides], refs[3 + sides :]
    far_ref, fdiag_refs, near_ref = refs[0], refs[1 : 1 + sides], refs[1 + sides]
    refs = refs[2 + sides :]
    first_ref, second_ref, out_ref, feature_cols_ref, seed_cols_ref = refs
    width = slots * PLANE
    rows = 8 * width
    metas, fields = neighbourhood(own_ref, side_refs, far_ref, fdiag_refs, near_ref, rows, width)
    chosen = selectors(metas, where_ref, code_ref[...], sides, width)
    fill(feature_cols_ref, *fields[0], chosen, width)
    pre_first = conv(feature_cols_ref, first_ref, width)
    live = live_rows(where_ref, sides, slots)
    sigmoid = 1.0 / (1.0 + jnp.exp(-pre_first))
    hidden = jnp.where(live, pre_first * sigmoid, 0.0)
    slope = jnp.where(live, sigmoid * (1.0 + pre_first * (1.0 - sigmoid)), 0.0)
    out_ref[: rows // 2, :] = hidden.astype(jnp.bfloat16)
    fill(seed_cols_ref, *fields[1], chosen, width)
    hidden_grad = conv_back(seed_cols_ref, second_ref, width)
    out_ref[rows // 2 : rows, :] = (hidden_grad * slope).astype(jnp.bfloat16)
    out_ref[rows:, :] = own_ref[rows:, :]


def last_kernel(slots, sides, *refs):
    where_ref, code_ref, own_ref = refs[:3]
    side_refs, refs = refs[3 : 3 + sides], refs[3 + sides :]
    far_ref, fdiag_refs, near_ref = refs[0], refs[1 : 1 + sides], refs[1 + sides]
    refs = refs[2 + sides :]
    first_ref, second_ref, output_ref, input_ref, hidden_cols_ref, grad_cols_ref = refs
    width = slots * PLANE
    rows = 8 * width
    metas, fields = neighbourhood(own_ref, side_refs, far_ref, fdiag_refs, near_ref, rows, width)
    chosen = selectors(metas, where_ref, code_ref[...], sides, width)
    live = live_rows(where_ref, sides, slots)

    def put(ref, total):
        total = jnp.where(live, total, 0.0)
        for x in range(4):
            for slot in range(slots):
                start = x * width + slot * PLANE
                ref[slot, x * PLANE : (x + 1) * PLANE, :] = total[start : start + PLANE]

    fill(hidden_cols_ref, *fields[0], chosen, width)
    put(output_ref, conv(hidden_cols_ref, second_ref, width))
    fill(grad_cols_ref, *fields[1], chosen, width)
    put(input_ref, conv_back(grad_cols_ref, first_ref, width))


def store_terms(place_ref, keep_ref, send_ref, total_ref, chunks, rows):
    core = place_ref[0]
    for i in range(chunks // 2):
        keep_at = pl.multiple_of((2 * i + core) * rows, 8)
        send_at = pl.multiple_of((2 * i + 1 - core) * rows, 8)
        keep_ref[i] = total_ref[pl.ds(keep_at, rows), :]
        send_ref[i] = total_ref[pl.ds(send_at, rows), :].astype(jnp.bfloat16)


def second_terms_kernel(slots, scale, place_ref, both_ref, cols_ref, keep_ref, send_ref, total_ref):
    width = slots * PLANE
    hidden = both_ref[: 4 * width, :].astype(jnp.float32).T.astype(jnp.bfloat16)
    for tap in range(TAPS):
        total_ref[tap * C : (tap + 1) * C, :] = dot(hidden, tap_rows(cols_ref, 26 - tap, width)) * scale
    store_terms(place_ref, keep_ref, send_ref, total_ref, 2 * keep_ref.shape[0], keep_ref.shape[1])


def first_terms_kernel(slots, scale, place_ref, both_ref, cols_ref, keep_ref, send_ref, total_ref):
    width = slots * PLANE
    grad = both_ref[4 * width : 8 * width, :]
    for tap in range(TAPS):
        total_ref[tap * C : (tap + 1) * C, :] = (
            dot(tap_rows(cols_ref, tap, width), grad, ((0,), (0,))) * scale
        )
    store_terms(place_ref, keep_ref, send_ref, total_ref, 2 * keep_ref.shape[0], keep_ref.shape[1])


def swap(cells, axis, bit):
    count = lax.axis_size(axis)
    return lax.ppermute(cells, axis, [(i, i ^ bit) for i in range(count)])


def side_steps(count):
    if count == 2:
        return [[(0, 1), (1, 0)]]
    ends = count - 1
    return [
        [(i, i + 1) for i in range(ends)],
        [(i + 1, i) for i in range(ends)],
    ]


def far_steps(count):
    pairs = [(i, i + 1) for i in range(1, count - 1, 2)]
    return pairs + [(b, a) for a, b in pairs]


def exchanged(own, rows, width, core):
    gx, gy = lax.axis_size("gx"), lax.axis_size("gy")
    steps = side_steps(gy)

    def faces(tile, low):
        half = rows // 2
        starts = (0, half) if low else (3 * width, half + 3 * width)
        return [tile[start : start + width] for start in starts] + [tile[rows : rows + META_ROWS]]

    def face(tile, low_core):
        low, high = (jnp.concatenate(faces(tile, low), axis=0) for low in (True, False))
        return jnp.where(core == low_core, low, high)

    far_face = face(own, 0)
    side = [lax.ppermute(own, "gy", step) for step in steps]
    far = lax.ppermute(far_face, "gx", far_steps(gx))
    fdiag = [
        lax.ppermute(
            far_face,
            ("gx", "gy"),
            [(a * gy + c, b * gy + d) for a, b in far_steps(gx) for c, d in step],
        )
        for step in steps
    ]
    near = swap(jnp.concatenate([face(tile, 1) for tile in [own] + side], axis=0), "gx", 1)
    return (own, *side, far, *fdiag, near)


def halved(keep, got, index, axis):
    def part(i):
        return (
            lax.dynamic_index_in_dim(keep, i, axis, keepdims=False)
            + lax.dynamic_index_in_dim(got, i, axis, keepdims=False).astype(jnp.float32)
        )

    return part(index), part(1 - index).astype(jnp.bfloat16)


def spread(whole, index, count, axis):
    return [
        lax.dynamic_index_in_dim(whole, index ^ m, axis, keepdims=False).astype(jnp.bfloat16)
        for m in range(1, count)
    ]


def per_device(features, block_coords, block_counts, first_weight, second_weight, cotangent):
    gx, gy = lax.axis_size("gx"), lax.axis_size("gy")
    ix, iy = lax.axis_index("gx"), lax.axis_index("gy")
    slots = features.shape[2]
    width = slots * PLANE
    rows = 8 * width
    core, half, deep = ix % 2, ix // 2 % 2, ix // 4
    deeps = gx // 4
    sides = 1 if gy == 2 else 2

    coords = block_coords.reshape(slots)
    count = block_counts.reshape(())
    lanes = np.arange(512)
    lane_slot = (lanes // PLANE) % slots
    position = sum(jnp.where(lane_slot == s, coords[s], 0) for s in range(slots))
    meta = jnp.stack(
        [
            position // 16,
            4 * (position // 8 % 2) + lanes % PLANE // 4,
            4 * (position % 8) + lanes % 4,
            (lane_slot < count).astype(jnp.int32),
        ]
    )
    meta = meta.reshape(4, 2, C).transpose(1, 0, 2).reshape(8, C).astype(jnp.bfloat16)
    meta = jnp.concatenate([meta, jnp.zeros((META_ROWS - 8, C), jnp.bfloat16)], axis=0)
    cells = np.arange(9 * width)
    shift, cell = cells // width, cells % PLANE
    cell_slot = cells // PLANE % slots
    position = sum(jnp.where(cell_slot == s, coords[s], 0) for s in range(slots))
    code = (
        (position // 16) * int(STEP_X)
        + (4 * (position // 8 % 2) + (cell // 4 + shift // 3 - 1)) * int(STEP_Y)
        + 4 * (position % 8)
        + (cell % 4 + shift % 3 - 1)
    ).astype(jnp.float32)[:, None]
    side_signs = [1 - 2 * iy] if sides == 1 else [-1, 1]
    where = jnp.stack([jnp.asarray(v, jnp.int32) for v in [1 - 2 * core, *side_signs, count]])
    place = core.astype(jnp.int32).reshape(1)

    def planes(field):
        return field.reshape(slots, 4, PLANE, C).transpose(1, 0, 2, 3).reshape(4 * width, C)

    own = jnp.concatenate([planes(features), planes(cotangent), meta], axis=0)
    around = exchanged(own, rows, width, core)
    in_specs = [pl.BlockSpec(memory_space=SMEM)] + [pl.BlockSpec(memory_space=VMEM)] * (
        len(around) + 3
    )
    out = pl.BlockSpec(memory_space=VMEM)
    cols = jax.ShapeDtypeStruct((9, 6 * width, C), jnp.bfloat16)
    both, feature_cols, seed_cols = pl.pallas_call(
        functools.partial(first_kernel, slots, sides),
        out_shape=(jax.ShapeDtypeStruct(own.shape, jnp.bfloat16), cols, cols),
        in_specs=in_specs,
        out_specs=(out, out, out),
        compiler_params=params(48),
        name="first_layer",
    )(where, code, *around, first_weight, second_weight)

    grad_scale = 1.0 / math.sqrt(64 * slots * gx * gy)
    chunk = TAPS * C // gx

    def terms(kernel, name, cols):
        return pl.pallas_call(
            functools.partial(kernel, slots, grad_scale),
            out_shape=(
                jax.ShapeDtypeStruct((gx // 2, chunk, C), jnp.float32),
                jax.ShapeDtypeStruct((gx // 2, chunk, C), jnp.bfloat16),
            ),
            in_specs=[pl.BlockSpec(memory_space=SMEM), out, out],
            out_specs=(out, out),
            scratch_shapes=[pltpu.VMEM((TAPS * C, C), jnp.float32)],
            compiler_params=params(48),
            name=name,
        )(place, both, cols)

    second_keep, second_send = terms(second_terms_kernel, "second_terms", seed_cols)
    first_keep, first_send = terms(first_terms_kernel, "first_terms", feature_cols)

    def shaped(cells):
        return cells.reshape(deeps, 2, chunk, gy, C // gy)

    def over_y(keep, axis):
        sent = spread(keep, iy, gy, axis)
        got = [swap(piece, "gy", m) for m, piece in enumerate(sent, 1)]
        own = lax.dynamic_index_in_dim(keep, iy, axis, keepdims=False)
        return own + sum(piece.astype(jnp.float32) for piece in got)

    def over_z(keep):
        sent = spread(keep, deep, deeps, 0)
        got = [swap(piece, "gx", 4 * m) for m, piece in enumerate(sent, 1)]
        own = lax.dynamic_index_in_dim(keep, deep, 0, keepdims=False)
        return own + sum(piece.astype(jnp.float32) for piece in got)

    second_got = shaped(swap(second_send, "gx", 1))
    second_keep, second_sent = halved(shaped(second_keep), second_got, half, 1)
    second_sum = second_keep + swap(second_sent, "gx", 2).astype(jnp.float32)
    second_grad = over_z(over_y(second_sum, 2))

    first_got = shaped(swap(first_send, "gx", 1))
    first_sum = over_y(shaped(first_keep) + first_got.astype(jnp.float32), 3)
    first_keep, first_sent = (
        lax.dynamic_index_in_dim(first_sum, half, 1, keepdims=False),
        lax.dynamic_index_in_dim(first_sum, 1 - half, 1, keepdims=False).astype(jnp.bfloat16),
    )
    first_sum = first_keep + swap(first_sent, "gx", 2).astype(jnp.float32)
    first_grad = over_z(first_sum)

    around = exchanged(both, rows, width, core)
    result = jax.ShapeDtypeStruct((slots, 64, C), jnp.float32)
    output, input_grad = pl.pallas_call(
        functools.partial(last_kernel, slots, sides),
        out_shape=(result, result),
        in_specs=in_specs,
        out_specs=(out, out),
        scratch_shapes=[pltpu.VMEM(cols.shape, jnp.bfloat16)] * 2,
        compiler_params=params(48),
        name="last_layer",
    )(where, code, *around, first_weight, second_weight)
    return (
        output.reshape(features.shape),
        input_grad.reshape(features.shape),
        first_grad,
        second_grad,
    )


def solution(mesh):
    placed = (
        P("gx", "gy", None, None, None),
        P("gx", "gy", None),
        P("gx", "gy"),
        P(),
        P(),
        P("gx", "gy", None, None, None),
    )
    return jax.shard_map(
        per_device,
        mesh=mesh,
        in_specs=placed,
        out_specs=(
            P("gx", "gy", None, None, None),
            P("gx", "gy", None, None, None),
            P("gx", "gy"),
            P("gx", "gy"),
        ),
        check_vma=False,
    )
```

```python
import functools
import math

import jax
import jax.numpy as jnp
from jax import lax
from jax.experimental import pallas as pl
from jax.experimental.pallas import tpu as pltpu
from jax.sharding import PartitionSpec as P

C = 256
TAPS = 27
PLANE = 16
META = 16
LANES = 512
STEP_Y = 64.0
STEP_X = 4096.0
NOWHERE = -1.0e7
VMEM = pl.BlockSpec(memory_space=pltpu.MemorySpace.VMEM)
SMEM = pl.BlockSpec(memory_space=pltpu.MemorySpace.SMEM)


def params(mib):
    return pltpu.CompilerParams(vmem_limit_bytes=mib * 2**20)


def dot(lhs, rhs, dims=((1,), (0,))):
    return lax.dot_general(lhs, rhs, (dims, ((), ())), preferred_element_type=jnp.float32)


def iota(shape, dim):
    return lax.broadcasted_iota(jnp.int32, shape, dim)


def place_codes(meta, offset, absent=NOWHERE):
    rows = meta.astype(jnp.float32)
    parts = []
    for half in range(2):
        x, y, z, live = (rows[4 * half + i : 4 * half + i + 1] for i in range(4))
        parts.append(jnp.where(live > 0.5, x * STEP_X + y * STEP_Y + z + offset, absent))
    return jnp.concatenate(parts, axis=1)


def source_codes(metas, near, side_offsets, width):
    offsets = [0.0, *side_offsets, near, -near]
    for side_offset in side_offsets:
        offsets += [near + side_offset, side_offset - near]
    lane = iota((1, LANES), 1)
    total = jnp.full((1, LANES), NOWHERE, jnp.float32)
    for place, (meta, offset) in enumerate(zip(metas, offsets)):
        inside = (lane >= place * width) & (lane < (place + 1) * width)
        total = jnp.where(inside, place_codes(meta, offset), total)
    return total


def target_codes(meta, width):
    codes = place_codes(meta, 0.0, 3 * NOWHERE)
    own = iota((width, LANES), 0) == iota((width, LANES), 1)
    column = jnp.sum(jnp.where(own, codes, 0.0), axis=1, keepdims=True)
    return jnp.concatenate(
        [column + ((s // 3 - 1) * STEP_Y + (s % 3 - 1)) for s in range(9)], axis=0
    )


def selectors(source, target, sides, width):
    edge = source[:, : 3 * (1 + sides) * width]
    middle = source[:, : (1 + sides) * width]
    return tuple(
        (codes == target + step).astype(jnp.float32).astype(jnp.bfloat16)
        for codes, step in ((edge, -STEP_X), (middle, 0.0), (edge, STEP_X))
    )


def fill(cols_ref, tiles, faces, chosen, width, columns=slice(None)):
    def load(source, start):
        ref, first = source
        return ref[pl.ds(first + start, width), columns]

    for plane in range(6):
        if plane in (0, 5):
            near = 3 * width if plane == 0 else 0
            pieces = [load(tile, near) for tile in tiles] + [load(face, 0) for face in faces]
        else:
            pieces = [load(tile, (plane - 1) * width) for tile in tiles]
        select = chosen[0 if plane == 0 else 2 if plane == 5 else 1]
        moved = dot(select, jnp.concatenate(pieces, axis=0)).astype(jnp.bfloat16)
        for shift in range(9):
            cols_ref[shift, plane * width : (plane + 1) * width, :] = moved[
                shift * width : (shift + 1) * width
            ]


def tap_rows(cols_ref, tap, width, columns=slice(None)):
    start = tap // 9 * width
    return cols_ref[tap % 9, start : start + 4 * width, columns]


def conv(cols_ref, weight_ref, width):
    total = None
    for tap in range(TAPS):
        term = dot(tap_rows(cols_ref, tap, width), weight_ref[tap * C : (tap + 1) * C, :])
        total = term if total is None else total + term
    return total


def conv_back(cols_ref, weight_ref, width):
    total = None
    for tap in range(TAPS):
        weight = weight_ref[(26 - tap) * C : (27 - tap) * C, :]
        term = dot(tap_rows(cols_ref, tap, width), weight, ((1,), (1,)))
        total = term if total is None else total + term
    return total


def live_rows(meta, width):
    codes = place_codes(meta, 0.0)
    own = iota((width, LANES), 0) == iota((width, LANES), 1)
    column = jnp.sum(jnp.where(own, codes, 0.0), axis=1, keepdims=True)
    return jnp.concatenate([column] * 4, axis=0) > 0.5 * NOWHERE


def near_sign(axis="gx"):
    return (1 - 2 * (lax.axis_index(axis) % 2)).astype(jnp.float32)


def near_row(width):
    return pl.multiple_of((lax.axis_index("gx") % 2) * (3 * width), PLANE)


def side_offsets(sides):
    if sides == 2:
        return [-8 * STEP_Y, 8 * STEP_Y]
    return [(1 - 2 * lax.axis_index("gy")).astype(jnp.float32) * (8 * STEP_Y)]


def pack_kernel(features_ref, cotangent_ref, coords_ref, counts_ref, own_ref, face_ref):
    slots = features_ref.shape[2]
    width = slots * PLANE
    core = lax.axis_index("gx") % 2
    for field, ref in enumerate((features_ref, cotangent_ref)):
        for x in range(4):
            for slot in range(slots):
                start = field * 4 * width + x * width + slot * PLANE
                own_ref[start : start + PLANE, :] = ref[0, 0, slot, x * PLANE : (x + 1) * PLANE, :]
    lane = iota((1, LANES), 1)
    lane_slot = (lane // PLANE) % slots
    position = jnp.zeros((1, LANES), jnp.int32)
    for slot in range(slots):
        position = jnp.where(lane_slot == slot, coords_ref[0, 0, slot], position)
    values = [
        position // 16,
        4 * (position // 8 % 2) + lane % PLANE // 4,
        4 * (position % 8) + lane % 4,
        (lane_slot < counts_ref[0, 0]).astype(jnp.int32),
    ]
    rows = [v[:, h * C : (h + 1) * C] for h in range(2) for v in values]
    rows.append(jnp.zeros((META - 8, C), jnp.int32))
    meta = jnp.concatenate(rows, axis=0).astype(jnp.float32).astype(jnp.bfloat16)
    own_ref[8 * width :, :] = meta
    for field in range(2):
        at = pl.multiple_of(4 * width * field + 3 * width * core, PLANE)
        face_ref[field * width : (field + 1) * width, :] = own_ref[pl.ds(at, width), :]
    face_ref[2 * width :, :] = meta


def around(refs, sides):
    own, refs = refs[0], refs[1:]
    side, far, fdiag = refs[:sides], refs[sides], refs[sides + 1 : 2 * sides + 1]
    near, ndiag = refs[2 * sides + 1], refs[2 * sides + 2 :]
    return own, side, far, fdiag, near, ndiag


def own_sources(refs, sides, width, field):
    own, side, far, fdiag, near, ndiag = around(refs, sides)
    top, at = field * 4 * width, near_row(width)
    tiles = [(own, top)] + [(ref, top) for ref in side]
    faces = [(near, top + at), (far, field * width)]
    for n, f in zip(ndiag, fdiag):
        faces += [(n, top + at), (f, field * width)]
    return tiles, faces


def side_sources(refs, width, field):
    own, (side,), far, (fdiag,), near, (ndiag,) = around(refs, 1)
    return own_sources((side, own, fdiag, far, ndiag, near), 1, width, field)


def hidden_kernel(sides, count, *refs):
    early, refs = refs[:count], refs[count:]
    weight_ref, hidden_ref, slope_ref, cols_ref, source_ref, target_ref = refs
    own, side, far, fdiag, near, ndiag = around(early, sides)
    width = own.shape[0] // 8 // PLANE * PLANE
    rows, faced = 8 * width, 2 * width
    metas = [own[rows : rows + 8, :]] + [ref[rows : rows + 8, :] for ref in side]
    edges = [near[rows : rows + 8, :], far[faced : faced + 8, :]]
    for n, f in zip(ndiag, fdiag):
        edges += [n[rows : rows + 8, :], f[faced : faced + 8, :]]
    sign = near_sign() * (2 * STEP_X)
    offsets = side_offsets(sides)
    source = source_codes(metas + edges, sign, offsets, width)
    target = target_codes(metas[0], width)
    source_ref[...] = jnp.zeros(source_ref.shape, jnp.float32)
    source_ref[0:1, :] = source
    target_ref[:, 0:1] = target
    if sides == 1:
        mirrored = [metas[1], metas[0], edges[2], edges[3], edges[0], edges[1]]
        source_ref[1:2, :] = source_codes(mirrored, sign, [-offsets[0]], width)
        target_ref[:, 1:2] = target_codes(metas[1], width)
    else:
        target_ref[:, 1:2] = target
    chosen = selectors(source, target, sides, width)
    fill(cols_ref, *own_sources(early, sides, width, 0), chosen, width)
    pre_first = conv(cols_ref, weight_ref, width)
    live = live_rows(metas[0], width)
    sigmoid = 1.0 / (1.0 + jnp.exp(-pre_first))
    hidden_ref[...] = jnp.where(live, pre_first * sigmoid, 0.0).astype(jnp.bfloat16)
    slope_ref[...] = jnp.where(live, sigmoid * (1.0 + pre_first * (1.0 - sigmoid)), 0.0)


def grad_kernel(sides, count, *refs):
    early, refs = refs[:count], refs[count:]
    weight_ref, hidden_ref, slope_ref, source_ref, target_ref = refs[:5]
    grad_ref, face_ref, cols_ref = refs[5:]
    width = hidden_ref.shape[0] // 4
    chosen = selectors(source_ref[0:1, :], target_ref[:, 0:1], sides, width)
    fill(cols_ref, *own_sources(early, sides, width, 1), chosen, width)
    hidden_grad = conv_back(cols_ref, weight_ref, width)
    grad_ref[...] = (hidden_grad * slope_ref[...]).astype(jnp.bfloat16)
    at = pl.multiple_of(3 * width * (lax.axis_index("gx") % 2), PLANE)
    face_ref[:width, :] = hidden_ref[pl.ds(at, width), :]
    face_ref[width:, :] = grad_ref[pl.ds(at, width), :]


def store_terms(keep_ref, send_ref, total_ref):
    core = lax.axis_index("gx") % 2
    pairs, rows = keep_ref.shape[0], keep_ref.shape[1]
    for i in range(pairs):
        keep_at = pl.multiple_of((2 * i + core) * rows, 8)
        send_at = pl.multiple_of((2 * i + 1 - core) * rows, 8)
        keep_ref[i] = total_ref[pl.ds(keep_at, rows), :]
        send_ref[i] = total_ref[pl.ds(send_at, rows), :].astype(jnp.bfloat16)


def my_columns(cols):
    if cols == C:
        return slice(None)
    return pl.ds(pl.multiple_of(lax.axis_index("gy") * cols, 128), cols)


def second_terms_kernel(count, grouped, *refs):
    early, refs = refs[:count], refs[count:]
    hiddens, refs = refs[: 1 + grouped], refs[1 + grouped :]
    cols_ref, source_ref, target_ref, keep_ref, send_ref, total_ref, side_ref = refs
    cols = keep_ref.shape[2]
    columns = my_columns(cols)
    width = hiddens[0].shape[0] // 4
    hidden = jnp.concatenate([ref[...] for ref in hiddens], axis=0)
    hidden = hidden.astype(jnp.float32).T.astype(jnp.bfloat16)
    if grouped:
        chosen = selectors(source_ref[1:2, :], target_ref[:, 1:2], 1, width)
        fill(side_ref, *side_sources(early, width, 1), chosen, width, columns)

    def rows(tap):
        pieces = [tap_rows(cols_ref, 26 - tap, width, columns)]
        if grouped:
            pieces.append(tap_rows(side_ref, 26 - tap, width))
        return jnp.concatenate(pieces, axis=0)

    step = C // cols
    for first in range(0, TAPS, step):
        taps = range(first, min(first + step, TAPS))
        result = dot(hidden, jnp.concatenate([rows(tap) for tap in taps], axis=1))
        for i, tap in enumerate(taps):
            total_ref[tap * C : (tap + 1) * C, :] = result[:, i * cols : (i + 1) * cols]
    store_terms(keep_ref, send_ref, total_ref)


def first_terms_kernel(count, grouped, *refs):
    early, refs = refs[:count], refs[count:]
    grads, refs = refs[: 1 + grouped], refs[1 + grouped :]
    cols_ref, source_ref, target_ref, keep_ref, send_ref, total_ref, side_ref = refs
    columns = my_columns(keep_ref.shape[2])
    width = grads[0].shape[0] // 4
    if grouped:
        chosen = selectors(source_ref[1:2, :], target_ref[:, 1:2], 1, width)
        fill(side_ref, *side_sources(early, width, 0), chosen, width)
    grad = jnp.concatenate([ref[:, columns] for ref in grads], axis=0)
    for tap in range(TAPS):
        pieces = [tap_rows(cols_ref, tap, width)]
        if grouped:
            pieces.append(tap_rows(side_ref, tap, width))
        total_ref[tap * C : (tap + 1) * C, :] = dot(
            jnp.concatenate(pieces, axis=0), grad, ((0,), (0,))
        )
    store_terms(keep_ref, send_ref, total_ref)


def last_kernel(sides, count, *refs):
    own_ref, refs = refs[0], refs[1:]
    hidden_around, refs = refs[: 1 + sides], refs[1 + sides :]
    grad_around, refs = refs[: 1 + sides], refs[1 + sides :]
    fars, refs = refs[: 1 + sides], refs[1 + sides :]
    hidden_near, refs = refs[: 1 + sides], refs[1 + sides :]
    grad_near, refs = refs[: 1 + sides], refs[1 + sides :]
    first_ref, second_ref, source_ref, target_ref, output_ref, input_ref = refs[:6]
    hidden_cols_ref, grad_cols_ref = refs[6:]
    width = hidden_around[0].shape[0] // 4
    slots = output_ref.shape[0]
    chosen = selectors(source_ref[0:1, :], target_ref[:, 0:1], sides, width)
    live = live_rows(own_ref[8 * width : 8 * width + 8, :], width)
    at = near_row(width)

    def sources(field, tiles, nears):
        faces = []
        for near, far in zip(nears, fars):
            faces += [(near, at), (far, field * width)]
        return [(ref, 0) for ref in tiles], faces

    def put(ref, total):
        total = jnp.where(live, total, 0.0)
        for x in range(4):
            for slot in range(slots):
                start = x * width + slot * PLANE
                ref[slot, x * PLANE : (x + 1) * PLANE, :] = total[start : start + PLANE]

    fill(hidden_cols_ref, *sources(0, hidden_around, hidden_near), chosen, width)
    put(output_ref, conv(hidden_cols_ref, second_ref, width))
    fill(grad_cols_ref, *sources(1, grad_around, grad_near), chosen, width)
    put(input_ref, conv_back(grad_cols_ref, first_ref, width))


def swap(cells, axis, bit):
    return lax.ppermute(cells, axis, [(i, i ^ bit) for i in range(lax.axis_size(axis))])


def side_steps(count):
    if count == 2:
        return [[(0, 1), (1, 0)]]
    ends = count - 1
    return [[(i, i + 1) for i in range(ends)], [(i + 1, i) for i in range(ends)]]


def far_steps(count):
    pairs = [(i, i + 1) for i in range(1, count - 1, 2)]
    return pairs + [(b, a) for a, b in pairs]


def from_sides(cells):
    return [lax.ppermute(cells, "gy", step) for step in side_steps(lax.axis_size("gy"))]


def from_far(face):
    gx, gy = lax.axis_size("gx"), lax.axis_size("gy")
    far = lax.ppermute(face, "gx", far_steps(gx))
    return [far] + [
        lax.ppermute(
            face,
            ("gx", "gy"),
            [(a * gy + c, b * gy + d) for a, b in far_steps(gx) for c, d in step],
        )
        for step in side_steps(gy)
    ]


def piece(cells, index, axis):
    return lax.dynamic_index_in_dim(cells, index, axis, keepdims=False)


def over_core(keep, send):
    return lambda part: part(keep) + part(swap(send, "gx", 1)).astype(jnp.float32)


def per_device(features, block_coords, block_counts, first_weight, second_weight, cotangent):
    gx, gy = lax.axis_size("gx"), lax.axis_size("gy")
    ix, iy = lax.axis_index("gx"), lax.axis_index("gy")
    slots = features.shape[2]
    width = slots * PLANE
    rows = 8 * width
    half, deep = ix // 2 % 2, ix // 4
    deeps = gx // 4
    sides = 1 if gy == 2 else 2
    grouped = gy == 2
    cols = C // gy if grouped else C
    chunk = TAPS * C // gx

    def shape(dims, kind=jnp.bfloat16):
        return jax.ShapeDtypeStruct(dims, kind)

    own, face = pl.pallas_call(
        pack_kernel,
        out_shape=(shape((rows + META, C)), shape((2 * width + META, C))),
        in_specs=[VMEM, VMEM, SMEM, SMEM],
        out_specs=(VMEM, VMEM),
        compiler_params=params(8),
        name="pack",
    )(features, cotangent, block_coords, block_counts)
    side = from_sides(own)
    fars = from_far(face)
    nears = [swap(tile, "gx", 1) for tile in [own] + side]
    early = [own, *side, *fars, *nears]
    count = len(early)
    field = (4 * width, C)
    columns = shape((9, 6 * width, C))

    hidden, slope, feature_cols, source, target = pl.pallas_call(
        functools.partial(hidden_kernel, sides, count),
        out_shape=(
            shape(field),
            shape(field, jnp.float32),
            columns,
            shape((8, LANES), jnp.float32),
            shape((9 * width, 2), jnp.float32),
        ),
        in_specs=[VMEM] * (count + 1),
        out_specs=(VMEM,) * 5,
        compiler_params=params(16),
        name="hidden",
    )(*early, first_weight)
    side_hidden = from_sides(hidden)

    grad, late_face, seed_cols = pl.pallas_call(
        functools.partial(grad_kernel, sides, count),
        out_shape=(shape(field), shape((2 * width, C)), columns),
        in_specs=[VMEM] * (count + 5),
        out_specs=(VMEM,) * 3,
        compiler_params=params(16),
        name="pre_grad",
    )(*early, second_weight, hidden, slope, source, target)
    side_grad = from_sides(grad)

    def terms(kernel, name, fields, cells):
        return pl.pallas_call(
            functools.partial(kernel, count, int(grouped)),
            out_shape=(
                shape((gx // 2, chunk, cols), jnp.float32),
                shape((gx // 2, chunk, cols)),
            ),
            in_specs=[VMEM] * (count + len(fields) + 3),
            out_specs=(VMEM, VMEM),
            scratch_shapes=[
                pltpu.VMEM((TAPS * C, cols), jnp.float32),
                pltpu.VMEM((9, 6 * width, cols if name == "second_terms" else C), jnp.bfloat16),
            ],
            compiler_params=params(24),
            name=name,
        )(*early, *fields, cells, source, target)

    members = 1 + grouped
    second = terms(second_terms_kernel, "second_terms", ([hidden] + side_hidden)[:members], seed_cols)
    first = terms(first_terms_kernel, "first_terms", ([grad] + side_grad)[:members], feature_cols)

    grad_scale = 1.0 / math.sqrt(64 * slots * gx * gy)

    def summed(keep, send):
        keep = keep.reshape(deeps, 2, chunk, cols)
        got = swap(send, "gx", 1).reshape(keep.shape)

        def part(i):
            return piece(keep, i, 1) + piece(got, i, 1).astype(jnp.float32)

        sent = part(1 - half).astype(jnp.bfloat16)
        total = part(half) + swap(sent, "gx", 2).astype(jnp.float32)
        if not grouped:
            total = total.reshape(deeps, chunk, gy, cols // gy)
            total = piece(total, iy, 2) + sum(
                swap(piece(total, iy ^ m, 2).astype(jnp.bfloat16), "gy", m).astype(jnp.float32)
                for m in range(1, gy)
            )
        total = piece(total, deep, 0) + sum(
            swap(piece(total, deep ^ m, 0).astype(jnp.bfloat16), "gx", 4 * m).astype(jnp.float32)
            for m in range(1, deeps)
        )
        return total * grad_scale

    second_grad = summed(*second)
    first_grad = summed(*first)

    late_fars = from_far(late_face)
    hidden_near = [swap(tile, "gx", 1) for tile in [hidden] + side_hidden]
    grad_near = [swap(tile, "gx", 1) for tile in [grad] + side_grad]
    late = [own, hidden, *side_hidden, grad, *side_grad, *late_fars, *hidden_near, *grad_near]
    late += [first_weight, second_weight, source, target]
    result = shape((slots, 64, C), jnp.float32)
    output, input_grad = pl.pallas_call(
        functools.partial(last_kernel, sides, len(late)),
        out_shape=(result, result),
        in_specs=[VMEM] * len(late),
        out_specs=(VMEM, VMEM),
        scratch_shapes=[pltpu.VMEM(columns.shape, jnp.bfloat16)] * 2,
        compiler_params=params(24),
        name="last_layer",
    )(*late)
    return (
        output.reshape(features.shape),
        input_grad.reshape(features.shape),
        first_grad,
        second_grad,
    )


def solution(mesh):
    placed = (
        P("gx", "gy", None, None, None),
        P("gx", "gy", None),
        P("gx", "gy"),
        P(),
        P(),
        P("gx", "gy", None, None, None),
    )
    return jax.shard_map(
        per_device,
        mesh=mesh,
        in_specs=placed,
        out_specs=(
            P("gx", "gy", None, None, None),
            P("gx", "gy", None, None, None),
            P("gx", "gy"),
            P("gx", "gy"),
        ),
        check_vma=False,
    )
```

```python
import functools
import math

import jax
import jax.numpy as jnp
from jax import lax
from jax.experimental import pallas as pl
from jax.experimental.pallas import tpu as pltpu
from jax.sharding import PartitionSpec as P

C = 256
TAPS = 27
PLANE = 16
META = 16
LANES = 512
STEP_Y = 64.0
STEP_X = 4096.0
NOWHERE = -1.0e7
VMEM = pl.BlockSpec(memory_space=pltpu.MemorySpace.VMEM)
HBM = pl.BlockSpec(memory_space=pltpu.MemorySpace.HBM)
ANY = pl.BlockSpec(memory_space=pl.ANY)


def params(mib):
    return pltpu.CompilerParams(vmem_limit_bytes=mib * 2**20)


def dot(lhs, rhs, dims=((1,), (0,))):
    return lax.dot_general(lhs, rhs, (dims, ((), ())), preferred_element_type=jnp.float32)


def iota(shape, dim):
    return lax.broadcasted_iota(jnp.int32, shape, dim)


def place_codes(meta, offset, absent=NOWHERE):
    rows = meta.astype(jnp.float32)
    parts = []
    for half in range(2):
        x, y, z, live = (rows[4 * half + i : 4 * half + i + 1] for i in range(4))
        parts.append(jnp.where(live > 0.5, x * STEP_X + y * STEP_Y + z + offset, absent))
    return jnp.concatenate(parts, axis=1)


def source_codes(metas, near, side_offsets, width):
    offsets = [0.0, *side_offsets, near, -near]
    for side_offset in side_offsets:
        offsets += [near + side_offset, side_offset - near]
    lane = iota((1, LANES), 1)
    total = jnp.full((1, LANES), NOWHERE, jnp.float32)
    for place, (meta, offset) in enumerate(zip(metas, offsets)):
        inside = (lane >= place * width) & (lane < (place + 1) * width)
        total = jnp.where(inside, place_codes(meta, offset), total)
    return total


def target_codes(meta, width):
    codes = place_codes(meta, 0.0, 3 * NOWHERE)
    own = iota((width, LANES), 0) == iota((width, LANES), 1)
    column = jnp.sum(jnp.where(own, codes, 0.0), axis=1, keepdims=True)
    return jnp.concatenate(
        [column + ((s // 3 - 1) * STEP_Y + (s % 3 - 1)) for s in range(9)], axis=0
    )


def selectors(source, target, sides, width):
    edge = source[:, : 3 * (1 + sides) * width]
    middle = source[:, : (1 + sides) * width]
    return tuple(
        (codes == target + step).astype(jnp.float32).astype(jnp.bfloat16)
        for codes, step in ((edge, -STEP_X), (middle, 0.0), (edge, STEP_X))
    )


def fill(cols_ref, tiles, faces, chosen, width, columns=slice(None)):
    def load(source, start):
        ref, first = source
        return ref[pl.ds(first + start, width), columns]

    for plane in range(6):
        if plane in (0, 5):
            near = 3 * width if plane == 0 else 0
            pieces = [load(tile, near) for tile in tiles] + [load(face, 0) for face in faces]
        else:
            pieces = [load(tile, (plane - 1) * width) for tile in tiles]
        select = chosen[0 if plane == 0 else 2 if plane == 5 else 1]
        moved = dot(select, jnp.concatenate(pieces, axis=0)).astype(jnp.bfloat16)
        for shift in range(9):
            cols_ref[shift, plane * width : (plane + 1) * width, :] = moved[
                shift * width : (shift + 1) * width
            ]


def tap_rows(cols_ref, tap, width, columns=slice(None)):
    start = tap // 9 * width
    return cols_ref[tap % 9, start : start + 4 * width, columns]


def conv(cols_ref, weight, width):
    total = None
    for tap in range(TAPS):
        term = dot(tap_rows(cols_ref, tap, width), weight.tap(tap))
        total = term if total is None else total + term
    return total


def conv_back(cols_ref, weight, width):
    total = None
    for tap in range(TAPS):
        term = dot(tap_rows(cols_ref, tap, width), weight.tap(26 - tap), ((1,), (1,)))
        total = term if total is None else total + term
    return total


def live_rows(meta, width):
    codes = place_codes(meta, 0.0)
    own = iota((width, LANES), 0) == iota((width, LANES), 1)
    column = jnp.sum(jnp.where(own, codes, 0.0), axis=1, keepdims=True)
    return jnp.concatenate([column] * 4, axis=0) > 0.5 * NOWHERE


def near_row(width, flip=0):
    core = lax.axis_index("gx") % 2
    return pl.multiple_of((1 - core if flip else core) * (3 * width), PLANE)


def side_offsets(sides):
    if sides == 2:
        return [-8 * STEP_Y, 8 * STEP_Y]
    return [(1 - 2 * lax.axis_index("gy")).astype(jnp.float32) * (8 * STEP_Y)]


def pack_kernel(features, cotangent, coords, counts, own_ref, face_ref, place_ref, live_ref, sems):
    slots = features.shape[2]
    width = slots * PLANE
    copies = [
        pltpu.make_async_copy(coords.at[0], place_ref, sems.at[0]),
        pltpu.make_async_copy(counts, live_ref, sems.at[1]),
    ]
    for field, ref in enumerate((features, cotangent)):
        for x in range(4):
            for slot in range(slots):
                start = field * 4 * width + x * width + slot * PLANE
                copies.append(
                    pltpu.make_async_copy(
                        ref.at[0, 0, slot, pl.ds(x * PLANE, PLANE)],
                        own_ref.at[pl.ds(start, PLANE)],
                        sems.at[len(copies)],
                    )
                )
    for copy in copies:
        copy.start()
    for copy in copies:
        copy.wait()
    lane = iota((1, LANES), 1)
    lane_slot = (lane // PLANE) % slots
    position = jnp.zeros((1, LANES), jnp.int32)
    for slot in range(slots):
        position = jnp.where(lane_slot == slot, place_ref[0, slot], position)
    values = [
        position // 16,
        4 * (position // 8 % 2) + lane % PLANE // 4,
        4 * (position % 8) + lane % 4,
        (lane_slot < live_ref[0, 0]).astype(jnp.int32),
    ]
    rows = [v[:, h * C : (h + 1) * C] for h in range(2) for v in values]
    rows.append(jnp.zeros((META - 8, C), jnp.int32))
    meta = jnp.concatenate(rows, axis=0).astype(jnp.float32).astype(jnp.bfloat16)
    own_ref[8 * width :, :] = meta
    at = near_row(width)
    face_ref[:width, :] = own_ref[pl.ds(at, width), :]
    face_ref[width : 2 * width, :] = own_ref[pl.ds(pl.multiple_of(4 * width + at, PLANE), width), :]
    face_ref[2 * width :, :] = meta


def relay_kernel(*refs):
    refs, relay_ref = refs[:-2], refs[-1]
    at = 0
    for ref in refs:
        relay_ref[at : at + ref.shape[0], :] = ref[...]
        at += ref.shape[0]


def placed(j_refs, sides, rows):
    width = rows // 8
    tiles, fars = [], []
    for (own, own_at), (relay, relay_at) in j_refs:
        tiles.append([(own, own_at)])
        tiles[-1] += [(relay, relay_at + s * (rows + META)) for s in range(sides)]
        start = relay_at + sides * (rows + META)
        fars.append([(relay, start + s * (2 * width + META)) for s in range(1 + sides)])
    return tiles, fars


class Around:
    def __init__(self, tiles, fars, sides, rows):
        self.tiles, self.fars, self.sides = tiles, fars, sides
        self.rows, self.width = rows, rows // 8

    def tile(self, j, s):
        return self.tiles[j][s]

    def far(self, j, s):
        return self.fars[j][s]

    def order(self, s):
        return [s] + [other for other in range(1 + self.sides) if other != s]

    def codes(self, j, s):
        def meta(source, start):
            ref, first = source
            return ref[first + start : first + start + 8, :]

        order = self.order(s)
        metas = [meta(self.tile(j, o), self.rows) for o in order]
        for o in order:
            metas.append(meta(self.tile(j ^ 1, o), self.rows))
            metas.append(meta(self.far(j, o), 2 * self.width))
        sign = (1 - 2 * (lax.axis_index("gx") % 2)).astype(jnp.float32) * (2 * STEP_X)
        offsets = side_offsets(self.sides)
        source = source_codes(
            metas, -sign if j % 2 else sign, [-o for o in offsets] if s else offsets, self.width
        )
        return source, target_codes(metas[0], self.width)

    def sources(self, j, s, field):
        top = field * 4 * self.width
        at = near_row(self.width, j % 2)
        order = self.order(s)
        tiles = [(ref, first + top) for ref, first in (self.tile(j, o) for o in order)]
        faces = []
        for o in order:
            ref, first = self.tile(j ^ 1, o)
            faces.append((ref, first + top + at))
            ref, first = self.far(j, o)
            faces.append((ref, first + field * self.width))
        return tiles, faces


class Weight:
    def __init__(self, hbm_ref, ref, sems):
        third = 9 * C
        self.ref = ref
        self.copies = [
            pltpu.make_async_copy(
                hbm_ref.at[pl.ds(i * third, third)], ref.at[pl.ds(i * third, third)], sems.at[i]
            )
            for i in range(3)
        ]

    def start(self, order=(0, 1, 2)):
        for i in order:
            self.copies[i].start()

    def tap(self, tap):
        if self.copies[tap // 9] is not None:
            self.copies[tap // 9].wait()
            self.copies[tap // 9] = None
        return self.ref[tap * C : (tap + 1) * C, :]


def layer_kernel(sides, *refs):
    own, relay, near, near_relay, first_hbm, second_hbm = refs[:6]
    both_ref, slim_ref, face_ref, feature_cols, seed_cols, source_ref, target_ref = refs[6:13]
    first_ref, second_ref, sems = refs[13:]
    first = Weight(first_hbm, first_ref, sems.at[0])
    second = Weight(second_hbm, second_ref, sems.at[1])
    first.start()
    second.start((2, 1, 0))
    rows = own.shape[0] - META
    width = rows // 8
    pairs = [((own, 0), (relay, 0)), ((near, 0), (near_relay, 0))]
    around = Around(*placed(pairs, sides, rows), sides, rows)
    source, target = around.codes(0, 0)
    source_ref[...] = source
    target_ref[...] = target
    chosen = selectors(source, target, sides, width)
    fill(feature_cols, *around.sources(0, 0, 0), chosen, width)
    fill(seed_cols, *around.sources(0, 0, 1), chosen, width)
    pre_first = conv(feature_cols, first, width)
    live = live_rows(own[rows : rows + 8, :], width)
    sigmoid = 1.0 / (1.0 + jnp.exp(-pre_first))
    hidden = jnp.where(live, pre_first * sigmoid, 0.0)
    both_ref[: 4 * width, :] = hidden.astype(jnp.bfloat16)
    slope = jnp.where(live, sigmoid * (1.0 + pre_first * (1.0 - sigmoid)), 0.0)
    hidden_grad = conv_back(seed_cols, second, width)
    both_ref[4 * width :, :] = (hidden_grad * slope).astype(jnp.bfloat16)
    store_face(both_ref, face_ref)
    if sides == 1:
        slim(both_ref, slim_ref)
    else:
        slim_ref[...] = jnp.zeros(slim_ref.shape, slim_ref.dtype)


def slim(both_ref, slim_ref):
    rows = both_ref.shape[0] // 2
    columns = my_columns(C // 2)
    slim_ref[:rows, :] = both_ref[:rows, :]
    slim_ref[rows:, : C // 2] = both_ref[rows : rows + rows // 2, columns]
    slim_ref[rows:, C // 2 :] = both_ref[rows + rows // 2 :, columns]


def gather_kernel(own_ref, relay_ref, both_ref, *refs):
    packed_ref, slim_ref = refs[-2:]
    packed_ref[: own_ref.shape[0], :] = own_ref[...]
    packed_ref[own_ref.shape[0] :, :] = relay_ref[...]
    slim(both_ref, slim_ref)


def store_face(both_ref, face_ref):
    width = both_ref.shape[0] // 8
    at = near_row(width)
    face_ref[:width, :] = both_ref[pl.ds(at, width), :]
    face_ref[width:, :] = both_ref[pl.ds(pl.multiple_of(4 * width + at, PLANE), width), :]


def my_columns(cols):
    if cols == C:
        return slice(None)
    return pl.ds(pl.multiple_of(lax.axis_index("gy") * cols, 128), cols)


def store_terms(keep_ref, send_ref, total_ref):
    core = lax.axis_index("gx") % 2
    pairs, rows = keep_ref.shape[0], keep_ref.shape[1]
    for i in range(pairs):
        keep_at = pl.multiple_of((2 * i + core) * rows, 8)
        send_at = pl.multiple_of((2 * i + 1 - core) * rows, 8)
        keep_ref[i] = total_ref[pl.ds(keep_at, rows), :]
        send_ref[i] = total_ref[pl.ds(send_at, rows), :].astype(jnp.bfloat16)


def second_terms_kernel(both_ref, cols_ref, keep_ref, send_ref, total_ref):
    rows = both_ref.shape[0] // 2
    hidden = both_ref[:rows, :].astype(jnp.float32).T.astype(jnp.bfloat16)
    for tap in range(TAPS):
        total_ref[tap * C : (tap + 1) * C, :] = dot(hidden, tap_rows(cols_ref, 26 - tap, rows // 4))
    store_terms(keep_ref, send_ref, total_ref)


def first_terms_kernel(both_ref, cols_ref, keep_ref, send_ref, total_ref):
    rows = both_ref.shape[0] // 2
    grad = both_ref[rows:, :]
    for tap in range(TAPS):
        total_ref[tap * C : (tap + 1) * C, :] = dot(
            tap_rows(cols_ref, tap, rows // 4), grad, ((0,), (0,))
        )
    store_terms(keep_ref, send_ref, total_ref)


def group_cols(around, members, feature_ref, seed_ref):
    columns = my_columns(seed_ref.shape[3])
    for index, (j, s) in enumerate(members):
        chosen = selectors(*around.codes(j, s), 1, around.width)
        fill(feature_ref.at[index], *around.sources(j, s, 0), chosen, around.width)
        fill(seed_ref.at[index], *around.sources(j, s, 1), chosen, around.width, columns)


CHIP_MEMBERS = ((0, 1), (1, 0), (1, 1))
OTHER_MEMBERS = ((2, 0), (2, 1), (3, 0), (3, 1))


def chip_cols_kernel(own, relay, near, near_relay, feature_ref, seed_ref):
    rows = own.shape[0] - META
    pairs = [((own, 0), (relay, 0)), ((near, 0), (near_relay, 0))]
    around = Around(*placed(pairs, 1, rows), 1, rows)
    group_cols(around, CHIP_MEMBERS, feature_ref, seed_ref)


def other_cols_kernel(packed, near_packed, feature_ref, seed_ref):
    width = feature_ref.shape[2] // 6
    rows = 8 * width
    pairs = [((ref, 0), (ref, rows + META)) for ref in (packed, near_packed)]
    tiles, fars = placed(pairs, 1, rows)
    around = Around([None, None] + tiles, [None, None] + fars, 1, rows)
    group_cols(around, OTHER_MEMBERS, feature_ref, seed_ref)


def group_terms(cols_of, fields, first, top, out_refs, total_ref):
    own_ref, send_refs = out_refs[0], out_refs[1:]
    chunk, cols = own_ref.shape[0] // 2, own_ref.shape[1]
    deep = lax.axis_index("gx") // 4
    row = lax.axis_index("gx") % 4
    taps = total_ref.shape[1] // C
    width = fields[0].shape[0] // 4
    starts = [((deep ^ m) * 4 + row) * chunk for m in range(1 + len(send_refs))]

    def rows(tap):
        tap = jnp.minimum(tap, TAPS - 1)
        tap = tap if first else TAPS - 1 - tap
        at = pl.multiple_of(tap // 9 * width, PLANE)
        return jnp.concatenate(
            [cols_of(i, tap % 9, pl.ds(at, 4 * width)) for i in range(len(fields))], axis=0
        )

    operand = jnp.concatenate(fields, axis=0).astype(jnp.float32).T.astype(jnp.bfloat16)
    wanted = [(m, i) for m in range(len(starts)) for i in range(taps)]
    if first:
        for m, i in wanted:
            result = dot(operand, rows(starts[m] // C + i))
            total_ref[m, i * C : (i + 1) * C, :] = result.T
    else:
        step = max(1, C // cols)
        for at in range(0, len(wanted), step):
            part = wanted[at : at + step]
            result = dot(
                operand, jnp.concatenate([rows(starts[m] // C + i) for m, i in part], axis=1)
            )
            for place, (m, i) in enumerate(part):
                total_ref[m, i * C : (i + 1) * C, :] = result[:, place * cols : (place + 1) * cols]
    for m, start in enumerate(starts):
        at = pl.multiple_of(start % C, 16)
        if m == 0:
            own_ref[top : top + chunk, :] = total_ref[m, pl.ds(at, chunk), :]
        else:
            send_refs[m - 1][top : top + chunk, :] = total_ref[m, pl.ds(at, chunk), :].astype(
                jnp.bfloat16
            )


def group_terms_kernel(*refs):
    both, slims, refs = refs[:4], refs[4:8], refs[8:]
    (feature_cols, seed_cols, *groups), refs = refs[:6], refs[6:]
    out_refs, total_ref = refs[:-1], refs[-1]
    rows = both[0].shape[0] // 2
    chunk = out_refs[0].shape[0] // 2
    columns = my_columns(out_refs[0].shape[1])

    def group(part, tile, shift, at):
        ref, index = (groups[part], tile - 1) if tile < 4 else (groups[2 + part], tile - 4)
        return ref[index, shift, at, :]

    def seeds_of(tile, shift, at):
        return seed_cols[shift, at, columns] if tile == 0 else group(1, tile, shift, at)

    def features_of(tile, shift, at):
        return feature_cols[shift, at, :] if tile == 0 else group(0, tile, shift, at)

    grads = [ref[rows:, columns] for ref in both]
    grads += [
        jnp.concatenate([ref[rows:, : C // 2], ref[rows:, C // 2 :]], axis=0) for ref in slims
    ]
    hiddens = [ref[:rows, :] for ref in (*both, *slims)]
    group_terms(features_of, grads, True, 0, out_refs, total_ref)
    group_terms(seeds_of, hiddens, False, chunk, out_refs, total_ref)


def last_kernel(sides, *refs):
    own_ref, refs = refs[0], refs[1:]
    tiles, refs = refs[: 1 + sides], refs[1 + sides :]
    nears, refs = refs[: 1 + sides], refs[1 + sides :]
    fars, refs = refs[: 1 + sides], refs[1 + sides :]
    first_hbm, second_hbm, source_ref, target_ref, _, output_ref, input_ref = refs[:7]
    hidden_cols_ref, grad_cols_ref, first_ref, second_ref, sems = refs[7:]
    first = Weight(first_hbm, first_ref, sems.at[0])
    second = Weight(second_hbm, second_ref, sems.at[1])
    second.start()
    first.start((2, 1, 0))
    width = tiles[0].shape[0] // 8
    slots = output_ref.shape[0]
    chosen = selectors(source_ref[...], target_ref[...], sides, width)
    live = live_rows(own_ref[8 * width : 8 * width + 8, :], width)
    at = near_row(width)

    def sources(field):
        top = field * 4 * width
        faces = []
        for near, far in zip(nears, fars):
            faces += [(near, top + at), (far, field * width)]
        return [(ref, top) for ref in tiles], faces

    def put(ref, total):
        total = jnp.where(live, total, 0.0)
        for x in range(4):
            for slot in range(slots):
                start = x * width + slot * PLANE
                ref[slot, x * PLANE : (x + 1) * PLANE, :] = total[start : start + PLANE]

    fill(hidden_cols_ref, *sources(0), chosen, width)
    fill(grad_cols_ref, *sources(1), chosen, width)
    put(output_ref, conv(hidden_cols_ref, second, width))
    put(input_ref, conv_back(grad_cols_ref, first, width))


def swap(cells, axis, bit):
    return lax.ppermute(cells, axis, [(i, i ^ bit) for i in range(lax.axis_size(axis))])


def side_steps(count):
    if count == 2:
        return [[(0, 1), (1, 0)]]
    ends = count - 1
    return [[(i, i + 1) for i in range(ends)], [(i + 1, i) for i in range(ends)]]


def far_steps(count):
    pairs = [(i, i + 1) for i in range(1, count - 1, 2)]
    return pairs + [(b, a) for a, b in pairs]


def from_sides(cells):
    return [lax.ppermute(cells, "gy", step) for step in side_steps(lax.axis_size("gy"))]


def from_far(face):
    far = lax.ppermute(face, "gx", far_steps(lax.axis_size("gx")))
    return [far, *from_sides(far)]


def piece(cells, index, axis):
    return lax.dynamic_index_in_dim(cells, index, axis, keepdims=False)


def per_device(features, block_coords, block_counts, first_weight, second_weight, cotangent):
    gx, gy = lax.axis_size("gx"), lax.axis_size("gy")
    iy, ix = lax.axis_index("gy"), lax.axis_index("gx")
    slots = features.shape[2]
    width = slots * PLANE
    rows = 8 * width
    half, deep = ix // 2 % 2, ix // 4
    deeps = gx // 4
    grouped = gy == 2
    sides = 1 if grouped else 2
    chunk = TAPS * C // gx

    def shape(dims, kind=jnp.bfloat16):
        return jax.ShapeDtypeStruct(dims, kind)

    def call(kernel, name, outs, args, mib, micros, scratch=(), specs=None):
        return pl.pallas_call(
            kernel,
            out_shape=outs,
            in_specs=specs or [VMEM] * len(args),
            out_specs=(VMEM,) * len(outs),
            scratch_shapes=list(scratch),
            compiler_params=params(mib),
            cost_estimate=pl.CostEstimate(
                flops=int(micros * 1.1e9), bytes_accessed=2**20, transcendentals=0
            ),
            name=name,
        )(*args)

    own, face = call(
        pack_kernel,
        "pack",
        (shape((rows + META, C)), shape((2 * width + META, C))),
        (features, cotangent, block_coords, block_counts),
        60,
        0.1,
        [
            pltpu.SMEM((1, slots), jnp.int32),
            pltpu.SMEM((1, 1), jnp.int32),
            pltpu.SemaphoreType.DMA((2 + 8 * slots,)),
        ],
        [HBM] * 4,
    )
    side = from_sides(own)
    fars = from_far(face)
    near = swap(own, "gx", 1)
    other = swap(own, "gx", 2) if grouped else own
    parts = [*side, *fars]
    (relay,) = call(
        relay_kernel,
        "relay",
        (shape((sum(cells.shape[0] for cells in parts), C)),),
        (*parts, other),
        8,
        0.1,
        specs=[VMEM] * len(parts) + [ANY],
    )
    near_relay = swap(relay, "gx", 1)
    columns = shape((9, 6 * width, C))
    weights = [pltpu.VMEM(first_weight.shape, jnp.bfloat16)] * 2
    weights.append(pltpu.SemaphoreType.DMA((2, 3)))
    both, thin, late_face, feature_cols, seed_cols, source, target = call(
        functools.partial(layer_kernel, sides),
        "layer",
        (
            shape((rows, C)),
            shape((6 * width, C)),
            shape((2 * width, C)),
            columns,
            columns,
            shape((1, LANES), jnp.float32),
            shape((9 * width, 1), jnp.float32),
        ),
        (own, relay, near, near_relay, first_weight, second_weight),
        58,
        4,
        weights,
        [VMEM] * 4 + [HBM] * 2,
    )
    late_fars = from_far(late_face)
    both_side = from_sides(both)
    both_near = [swap(cells, "gx", 1) for cells in [both] + both_side]
    grad_scale = 1.0 / math.sqrt(64 * slots * gx * gy)

    def over_z(own_part, sent):
        got = [swap(cells, "gx", 4 * m) for m, cells in enumerate(sent, 1)]
        return (own_part + sum(cells.astype(jnp.float32) for cells in got)) * grad_scale

    if grouped:
        cols = C // 2
        far_relay = swap(relay, "gx", 2)

        def group_shapes(count):
            return shape((count, *columns.shape)), shape((count, *columns.shape[:2], cols))

        chip_features, chip_seeds = call(
            chip_cols_kernel,
            "chip_cols",
            group_shapes(len(CHIP_MEMBERS)),
            (own, relay, near, near_relay),
            8,
            3,
        )
        packed, side_thin = call(
            gather_kernel,
            "gather",
            (shape((own.shape[0] + relay.shape[0], C)), shape(thin.shape)),
            (other, far_relay, both_side[0], chip_seeds, late_fars[0]),
            8,
            0.5,
            specs=[VMEM] * 3 + [ANY] * 2,
        )
        near_packed = swap(packed, "gx", 1)
        other_features, other_seeds = call(
            other_cols_kernel,
            "other_cols",
            group_shapes(len(OTHER_MEMBERS)),
            (packed, near_packed),
            8,
            4,
        )
        others = [swap(cells, "gx", 2) for cells in (thin, side_thin)]
        others += [swap(cells, "gx", 1) for cells in others]
        members = [both, both_side[0], *both_near, *others]
        taps = 2 + (chunk - 2) // C
        own_part, *sent = call(
            group_terms_kernel,
            "group_terms",
            (
                shape((2 * chunk, cols), jnp.float32),
                *[shape((2 * chunk, cols))] * (deeps - 1),
            ),
            (
                *members,
                feature_cols,
                seed_cols,
                chip_features,
                chip_seeds,
                other_features,
                other_seeds,
            ),
            12,
            3.5,
            [pltpu.VMEM((deeps, taps * C, cols), jnp.float32)],
        )
        token = sent[0]
        grads = over_z(own_part, sent)
        first_grad, second_grad = grads[:chunk], grads[chunk:]
    else:

        def summed(kernel, name, cells):
            keep, send = call(
                kernel,
                name,
                (
                    shape((gx // 2, chunk, C), jnp.float32),
                    shape((gx // 2, chunk, C)),
                ),
                (both, cells),
                24,
                4,
                [pltpu.VMEM((TAPS * C, C), jnp.float32)],
            )
            keep = keep.reshape(deeps, 2, chunk, C)
            got = swap(send, "gx", 1).reshape(keep.shape)

            def part(i):
                return piece(keep, i, 1) + piece(got, i, 1).astype(jnp.float32)

            total = part(half) + swap(part(1 - half).astype(jnp.bfloat16), "gx", 2).astype(
                jnp.float32
            )
            total = total.reshape(deeps, chunk, gy, C // gy)
            total = piece(total, iy, 2) + sum(
                swap(piece(total, iy ^ m, 2).astype(jnp.bfloat16), "gy", m).astype(jnp.float32)
                for m in range(1, gy)
            )
            total = over_z(
                piece(total, deep, 0),
                [piece(total, deep ^ m, 0).astype(jnp.bfloat16) for m in range(1, deeps)],
            )
            return total, send

        second_grad, token = summed(second_terms_kernel, "second_terms", seed_cols)
        first_grad, _ = summed(first_terms_kernel, "first_terms", feature_cols)

    late = [own, both, *both_side, *both_near, *late_fars]
    result = shape((slots, 64, C), jnp.float32)
    output, input_grad = call(
        functools.partial(last_kernel, sides),
        "last_layer",
        (result, result),
        (*late, first_weight, second_weight, source, target, token),
        58,
        0.1,
        [pltpu.VMEM(columns.shape, jnp.bfloat16)] * 2 + weights,
        [VMEM] * len(late) + [HBM, HBM, VMEM, VMEM, ANY],
    )
    return (
        output.reshape(features.shape),
        input_grad.reshape(features.shape),
        first_grad,
        second_grad,
    )


def solution(mesh):
    placed = (
        P("gx", "gy", None, None, None),
        P("gx", "gy", None),
        P("gx", "gy"),
        P(),
        P(),
        P("gx", "gy", None, None, None),
    )
    return jax.shard_map(
        per_device,
        mesh=mesh,
        in_specs=placed,
        out_specs=(
            P("gx", "gy", None, None, None),
            P("gx", "gy", None, None, None),
            P("gx", "gy"),
            P("gx", "gy"),
        ),
        check_vma=False,
    )
```

```python
import functools
import math

import jax
import jax.numpy as jnp
from jax import lax
from jax.experimental import pallas as pl
from jax.experimental.pallas import tpu as pltpu
from jax.sharding import PartitionSpec as P

C = 256
TAPS = 27
PLANE = 16
META = 16
LANES = 512
STEP_Y = 64.0
STEP_X = 4096.0
NOWHERE = -1.0e7
VMEM = pl.BlockSpec(memory_space=pltpu.MemorySpace.VMEM)
HBM = pl.BlockSpec(memory_space=pltpu.MemorySpace.HBM)
ANY = pl.BlockSpec(memory_space=pl.ANY)


def params(mib):
    return pltpu.CompilerParams(vmem_limit_bytes=mib * 2**20)


def dot(lhs, rhs, dims=((1,), (0,))):
    return lax.dot_general(lhs, rhs, (dims, ((), ())), preferred_element_type=jnp.float32)


def iota(shape, dim):
    return lax.broadcasted_iota(jnp.int32, shape, dim)


def place_codes(meta, offset, absent=NOWHERE):
    rows = meta.astype(jnp.float32)
    parts = []
    for half in range(2):
        x, y, z, live = (rows[4 * half + i : 4 * half + i + 1] for i in range(4))
        parts.append(jnp.where(live > 0.5, x * STEP_X + y * STEP_Y + z + offset, absent))
    return jnp.concatenate(parts, axis=1)


def source_codes(metas, offsets, width):
    lane = iota((1, LANES), 1)
    total = jnp.full((1, LANES), NOWHERE, jnp.float32)
    for place, (meta, offset) in enumerate(zip(metas, offsets)):
        inside = (lane >= place * width) & (lane < (place + 1) * width)
        total = jnp.where(inside, place_codes(meta, offset), total)
    return total


def target_codes(meta, width):
    codes = place_codes(meta, 0.0, 3 * NOWHERE)
    own = iota((width, LANES), 0) == iota((width, LANES), 1)
    column = jnp.sum(jnp.where(own, codes, 0.0), axis=1, keepdims=True)
    return jnp.concatenate(
        [column + ((s // 3 - 1) * STEP_Y + (s % 3 - 1)) for s in range(9)], axis=0
    )


def selectors(before, after, target, sides, width):
    middle = (1 + sides) * width
    return tuple(
        (codes == target + step).astype(jnp.float32).astype(jnp.bfloat16)
        for codes, step in (
            (before[:, : 2 * middle], -STEP_X),
            (before[:, :middle], 0.0),
            (after[:, : 2 * middle], STEP_X),
        )
    )


def fill(cols_ref, tiles, faces, odd, chosen, width, columns=slice(None)):
    def load(source, plane):
        ref, first, paired = source
        if paired:
            at = first + plane % 2 * width
            return ref[at : at + width, plane // 2 * (C // 2) : (plane // 2 + 1) * (C // 2)]
        return ref[first + plane * width : first + (plane + 1) * width, columns]

    for plane in range(6):
        if plane in (0, 5):
            start = 3 if plane == 0 else 0
            pieces = [load(tile, start) for tile in tiles]
            for near, far in faces:
                near, far = load(near, start), load(far, 0)
                pieces.append(jnp.where(odd, near, far) if plane == 0 else jnp.where(odd, far, near))
        else:
            pieces = [load(tile, plane - 1) for tile in tiles]
        select = chosen[0 if plane == 0 else 2 if plane == 5 else 1]
        moved = dot(select, jnp.concatenate(pieces, axis=0)).astype(jnp.bfloat16)
        for shift in range(9):
            cols_ref[shift, plane * width : (plane + 1) * width, :] = moved[
                shift * width : (shift + 1) * width
            ]


def tap_rows(cols_ref, tap, width, columns=slice(None)):
    start = tap // 9 * width
    return cols_ref[tap % 9, start : start + 4 * width, columns]


def conv(cols_ref, weight_ref, width):
    total = None
    for tap in range(TAPS):
        term = dot(tap_rows(cols_ref, tap, width), weight_ref[tap * C : (tap + 1) * C, :])
        total = term if total is None else total + term
    return total


def conv_back(cols_ref, weight_ref, width):
    total = None
    for tap in range(TAPS):
        weight = weight_ref[(26 - tap) * C : (27 - tap) * C, :]
        term = dot(tap_rows(cols_ref, tap, width), weight, ((1,), (1,)))
        total = term if total is None else total + term
    return total


def live_rows(meta, width):
    codes = place_codes(meta, 0.0)
    own = iota((width, LANES), 0) == iota((width, LANES), 1)
    column = jnp.sum(jnp.where(own, codes, 0.0), axis=1, keepdims=True)
    return jnp.concatenate([column] * 4, axis=0) > 0.5 * NOWHERE


def near_row(width):
    return pl.multiple_of((lax.axis_index("gx") % 2) * (3 * width), PLANE)


def side_offsets(sides):
    if sides == 2:
        return [-8 * STEP_Y, 8 * STEP_Y]
    return [(1 - 2 * lax.axis_index("gy")).astype(jnp.float32) * (8 * STEP_Y)]


def pack_kernel(features, cotangent, coords, counts, *refs):
    own_ref, face_ref, thin_ref, cross_ref, place_ref, live_ref, sems = refs
    slots = features.shape[2]
    width = slots * PLANE
    copies = [
        pltpu.make_async_copy(coords.at[0], place_ref, sems.at[0]),
        pltpu.make_async_copy(counts, live_ref, sems.at[1]),
    ]
    for field, ref in enumerate((features, cotangent)):
        for x in range(4):
            for slot in range(slots):
                start = field * 4 * width + x * width + slot * PLANE
                copies.append(
                    pltpu.make_async_copy(
                        ref.at[0, 0, slot, pl.ds(x * PLANE, PLANE)],
                        own_ref.at[pl.ds(start, PLANE)],
                        sems.at[len(copies)],
                    )
                )
    for copy in copies:
        copy.start()
    for copy in copies:
        copy.wait()
    lane = iota((1, LANES), 1)
    lane_slot = (lane // PLANE) % slots
    position = jnp.zeros((1, LANES), jnp.int32)
    for slot in range(slots):
        position = jnp.where(lane_slot == slot, place_ref[0, slot], position)
    values = [
        position // 16,
        4 * (position // 8 % 2) + lane % PLANE // 4,
        4 * (position % 8) + lane % 4,
        (lane_slot < live_ref[0, 0]).astype(jnp.int32),
    ]
    rows = [v[:, h * C : (h + 1) * C] for h in range(2) for v in values]
    rows.append(jnp.zeros((META - 8, C), jnp.int32))
    meta = jnp.concatenate(rows, axis=0).astype(jnp.float32).astype(jnp.bfloat16)
    own_ref[8 * width :, :] = meta
    at = near_row(width)
    face_ref[:width, :] = own_ref[pl.ds(at, width), :]
    face_ref[width : 2 * width, :] = own_ref[pl.ds(pl.multiple_of(4 * width + at, PLANE), width), :]
    face_ref[2 * width :, :] = meta
    slim(own_ref, thin_ref, lax.axis_index("gy") % 2)
    slim(own_ref, cross_ref, 1 - lax.axis_index("gy") % 2)


def placed(relays, sides, rows):
    face = rows // 4 + META
    start = (1 + sides) * (rows + META)
    return (
        [[(relay, s * (rows + META), False) for s in range(1 + sides)] for relay in relays],
        [[(relay, start + s * face) for s in range(1 + sides)] for relay in relays],
    )


class Around:
    def __init__(self, tiles, fars, sides, rows):
        self.tiles, self.fars, self.sides = tiles, fars, sides
        self.rows, self.width = rows, rows // 8

    def order(self, s):
        return [s] + [other for other in range(1 + self.sides) if other != s]

    def odd(self, j):
        return (lax.axis_index("gx") + j) % 2 == 1

    def codes(self, j, s):
        def meta(ref, start):
            return ref[start : start + 8, :]

        def tile_meta(j, o):
            ref, first, thin = self.tiles[j][o]
            return meta(ref, first + (self.rows * 3 // 4 if thin else self.rows))

        order = self.order(s)
        metas = [tile_meta(j, o) for o in order]
        offsets = side_offsets(self.sides)
        offsets = [0.0] + ([-o for o in offsets] if s else offsets)
        befores, afters = [], []
        for o in order:
            near = tile_meta(j ^ 1, o)
            ref, first = self.fars[j][o]
            far = meta(ref, first + 2 * self.width)
            befores.append(jnp.where(self.odd(j), near, far))
            afters.append(jnp.where(self.odd(j), far, near))
        before, after = (
            source_codes(metas + beyond, offsets + [o + step for o in offsets], self.width)
            for beyond, step in ((befores, -2 * STEP_X), (afters, 2 * STEP_X))
        )
        return before, after, target_codes(metas[0], self.width)

    def sources(self, j, s, field):
        def tile(j, o):
            ref, first, thin = self.tiles[j][o]
            return ref, first + field * 4 * self.width, thin and field == 1

        order = self.order(s)
        faces = []
        for o in order:
            ref, first = self.fars[j][o]
            faces.append((tile(j ^ 1, o), (ref, first + field * self.width, False)))
        return [tile(j, o) for o in order], faces, self.odd(j)


def layer_kernel(sides, *refs):
    relay, near_relay, first, second = refs[:4]
    both_ref, slim_ref, cross_ref, feature_cols, seed_cols, source_ref, target_ref = refs[4:]
    rows = both_ref.shape[0]
    width = rows // 8
    around = Around(*placed([relay, near_relay], sides, rows), sides, rows)
    before, after, target = around.codes(0, 0)
    source_ref[0:1, :] = before
    source_ref[1:2, :] = after
    target_ref[...] = target
    chosen = selectors(before, after, target, sides, width)
    fill(feature_cols, *around.sources(0, 0, 0), chosen, width)
    fill(seed_cols, *around.sources(0, 0, 1), chosen, width)
    pre_first = conv(feature_cols, first, width)
    live = live_rows(relay[rows : rows + 8, :], width)
    sigmoid = 1.0 / (1.0 + jnp.exp(-pre_first))
    hidden = jnp.where(live, pre_first * sigmoid, 0.0)
    both_ref[: 4 * width, :] = hidden.astype(jnp.bfloat16)
    slope = jnp.where(live, sigmoid * (1.0 + pre_first * (1.0 - sigmoid)), 0.0)
    hidden_grad = conv_back(seed_cols, second, width)
    both_ref[4 * width :, :] = (hidden_grad * slope).astype(jnp.bfloat16)
    if sides == 1:
        slim(both_ref, slim_ref, lax.axis_index("gy"))
        slim(both_ref, cross_ref, 1 - lax.axis_index("gy"))
    else:
        slim_ref[...] = jnp.zeros(slim_ref.shape, slim_ref.dtype)
        cross_ref[...] = jnp.zeros(cross_ref.shape, cross_ref.dtype)


def slim(tile_ref, slim_ref, half):
    rows = tile_ref.shape[0] // (8 * PLANE) * 4 * PLANE
    columns = pl.ds(pl.multiple_of(half * (C // 2), 128), C // 2)
    slim_ref[:rows, :] = tile_ref[:rows, :]
    slim_ref[rows : rows + rows // 2, : C // 2] = tile_ref[rows : rows + rows // 2, columns]
    slim_ref[rows : rows + rows // 2, C // 2 :] = tile_ref[rows + rows // 2 : 2 * rows, columns]
    if slim_ref.shape[0] > rows + rows // 2:
        slim_ref[rows + rows // 2 :, :] = tile_ref[2 * rows :, :]


def relay_kernel(count, *refs):
    own_hbm, relay_ref, fars_ref, sem = refs[0], *refs[-3:]
    size = own_hbm.shape[0]
    copy = pltpu.make_async_copy(own_hbm, relay_ref.at[pl.ds(0, size)], sem)
    copy.start()
    gather_kernel(count - 1, *refs[1:count], relay_ref.at[pl.ds(size, relay_ref.shape[0] - size)])
    gather_kernel(count // 2, *refs[count // 2 : count], fars_ref)
    copy.wait()


def gather_kernel(count, *refs):
    packed_ref = refs[-1]
    at = 0
    for ref in refs[:count]:
        packed_ref[at : at + ref.shape[0], :] = ref[...]
        at += ref.shape[0]


def face_kernel(both_ref, *refs):
    face_ref = refs[-1]
    width = both_ref.shape[0] // 8
    at = near_row(width)
    face_ref[:width, :] = both_ref[pl.ds(at, width), :]
    face_ref[width:, :] = both_ref[pl.ds(pl.multiple_of(4 * width + at, PLANE), width), :]


def my_columns(cols):
    if cols == C:
        return slice(None)
    return pl.ds(pl.multiple_of(lax.axis_index("gy") * cols, 128), cols)


def store_terms(keep_ref, send_ref, total_ref):
    core = lax.axis_index("gx") % 2
    pairs, rows = keep_ref.shape[0], keep_ref.shape[1]
    for i in range(pairs):
        keep_at = pl.multiple_of((2 * i + core) * rows, 8)
        send_at = pl.multiple_of((2 * i + 1 - core) * rows, 8)
        keep_ref[i] = total_ref[pl.ds(keep_at, rows), :]
        send_ref[i] = total_ref[pl.ds(send_at, rows), :].astype(jnp.bfloat16)


def second_terms_kernel(both_ref, cols_ref, keep_ref, send_ref, total_ref):
    rows = both_ref.shape[0] // 2
    hidden = both_ref[:rows, :].astype(jnp.float32).T.astype(jnp.bfloat16)
    for tap in range(TAPS):
        total_ref[tap * C : (tap + 1) * C, :] = dot(hidden, tap_rows(cols_ref, 26 - tap, rows // 4))
    store_terms(keep_ref, send_ref, total_ref)


def first_terms_kernel(both_ref, cols_ref, keep_ref, send_ref, total_ref):
    rows = both_ref.shape[0] // 2
    grad = both_ref[rows:, :]
    for tap in range(TAPS):
        total_ref[tap * C : (tap + 1) * C, :] = dot(
            tap_rows(cols_ref, tap, rows // 4), grad, ((0,), (0,))
        )
    store_terms(keep_ref, send_ref, total_ref)


def group_cols(around, members, feature_ref, seed_ref):
    columns = my_columns(seed_ref.shape[3])
    for index, (j, s) in enumerate(members):
        chosen = selectors(*around.codes(j, s), 1, around.width)
        fill(feature_ref.at[index], *around.sources(j, s, 0), chosen, around.width)
        fill(seed_ref.at[index], *around.sources(j, s, 1), chosen, around.width, columns)


CHIP_MEMBERS = ((0, 1), (1, 0), (1, 1))
OTHER_MEMBERS = ((2, 0), (2, 1), (3, 0), (3, 1))


def chip_cols_kernel(relay, near_relay, feature_ref, seed_ref):
    rows = feature_ref.shape[2] // 6 * 8
    around = Around(*placed([relay, near_relay], 1, rows), 1, rows)
    group_cols(around, CHIP_MEMBERS, feature_ref, seed_ref)


def other_cols_kernel(packed, near_packed, _, feature_ref, seed_ref):
    width = feature_ref.shape[2] // 6
    rows = 8 * width
    thin, face = 6 * width + META, 2 * width + META
    tiles = [[(ref, s * thin, True) for s in range(2)] for ref in (packed, near_packed)]
    fars = [[(ref, 2 * thin + s * face) for s in range(2)] for ref in (packed, near_packed)]
    around = Around([None, None] + tiles, [None, None] + fars, 1, rows)
    group_cols(around, OTHER_MEMBERS, feature_ref, seed_ref)


def group_terms(cols_of, fields, first, top, out_refs, total_ref):
    own_ref, send_refs = out_refs[0], out_refs[1:]
    chunk, cols = own_ref.shape[0] // 2, own_ref.shape[1]
    deep = lax.axis_index("gx") // 4
    row = lax.axis_index("gx") % 4
    taps = total_ref.shape[1] // C
    width = fields[0].shape[0] // 4
    starts = [((deep ^ m) * 4 + row) * chunk for m in range(1 + len(send_refs))]

    def rows(tap):
        tap = jnp.minimum(tap, TAPS - 1)
        tap = tap if first else TAPS - 1 - tap
        at = pl.multiple_of(tap // 9 * width, PLANE)
        return jnp.concatenate(
            [cols_of(i, tap % 9, pl.ds(at, 4 * width)) for i in range(len(fields))], axis=0
        )

    operand = jnp.concatenate(fields, axis=0).astype(jnp.float32).T.astype(jnp.bfloat16)
    wanted = [(m, i) for m in range(len(starts)) for i in range(taps)]
    if first:
        for m, i in wanted:
            result = dot(operand, rows(starts[m] // C + i))
            total_ref[m, i * C : (i + 1) * C, :] = result.T
    else:
        step = max(1, C // cols)
        for at in range(0, len(wanted), step):
            part = wanted[at : at + step]
            result = dot(
                operand, jnp.concatenate([rows(starts[m] // C + i) for m, i in part], axis=1)
            )
            for place, (m, i) in enumerate(part):
                total_ref[m, i * C : (i + 1) * C, :] = result[:, place * cols : (place + 1) * cols]
    for m, start in enumerate(starts):
        at = pl.multiple_of(start % C, 16)
        if m == 0:
            own_ref[top : top + chunk, :] = total_ref[m, pl.ds(at, chunk), :]
        else:
            send_refs[m - 1][top : top + chunk, :] = total_ref[m, pl.ds(at, chunk), :].astype(
                jnp.bfloat16
            )


def group_terms_kernel(*refs):
    both, thins, packed, refs = refs[:2], refs[2:4], refs[4], refs[5:]
    (feature_cols, seed_cols, *groups), refs = refs[:6], refs[7:]
    out_refs, total_ref = refs[:-1], refs[-1]
    rows = both[0].shape[0] // 2
    chunk = out_refs[0].shape[0] // 2
    columns = my_columns(out_refs[0].shape[1])
    thin_rows = thins[0].shape[0]
    both = [(ref, 0) for ref in both]
    both += [(packed, 2 * thin_rows), (packed, 2 * thin_rows + 2 * rows)]
    thins = [(ref, 0) for ref in thins] + [(packed, 0), (packed, thin_rows)]

    def group(part, tile, shift, at):
        ref, index = (groups[part], tile - 1) if tile < 4 else (groups[2 + part], tile - 4)
        return ref[index, shift, at, :]

    def seeds_of(tile, shift, at):
        return seed_cols[shift, at, columns] if tile == 0 else group(1, tile, shift, at)

    def features_of(tile, shift, at):
        return feature_cols[shift, at, :] if tile == 0 else group(0, tile, shift, at)

    grads = [ref[at + rows : at + 2 * rows, columns] for ref, at in both]
    for ref, at in thins:
        halves = ref[at + rows : at + rows + rows // 2, :]
        grads.append(jnp.concatenate([halves[:, : C // 2], halves[:, C // 2 :]], axis=0))
    hiddens = [ref[at : at + rows, :] for ref, at in (*both, *thins)]
    group_terms(features_of, grads, True, 0, out_refs, total_ref)
    group_terms(seeds_of, hiddens, False, chunk, out_refs, total_ref)


def last_kernel(sides, *refs):
    own_ref, refs = refs[0], refs[1:]
    tiles, refs = refs[: 1 + sides], refs[1 + sides :]
    count = 1 if sides == 1 else 1 + sides
    nears, refs = refs[:count], refs[count:]
    fars, refs = refs[: 1 + sides], refs[1 + sides :]
    first, second, source_ref, target_ref, _, output_ref, input_ref = refs[:7]
    hidden_cols_ref, grad_cols_ref = refs[7:]
    width = tiles[0].shape[0] // 8
    slots = output_ref.shape[0]
    chosen = selectors(source_ref[0:1, :], source_ref[1:2, :], target_ref[...], sides, width)
    live = live_rows(own_ref[8 * width : 8 * width + 8, :], width)
    rows = tiles[0].shape[0]
    if sides == 1:
        near_at = nears[0].shape[0] - 2 * rows
        nears = [(nears[0], near_at, False), (nears[0], near_at + rows, False)]
    else:
        nears = [(ref, 0, False) for ref in nears]
    around = Around(
        [[(ref, 0, False) for ref in tiles], nears],
        [[(ref, 0) for ref in fars]],
        sides,
        rows,
    )

    def put(ref, total):
        total = jnp.where(live, total, 0.0)
        for x in range(4):
            for slot in range(slots):
                start = x * width + slot * PLANE
                ref[slot, x * PLANE : (x + 1) * PLANE, :] = total[start : start + PLANE]

    fill(hidden_cols_ref, *around.sources(0, 0, 0), chosen, width)
    fill(grad_cols_ref, *around.sources(0, 0, 1), chosen, width)
    put(output_ref, conv(hidden_cols_ref, second, width))
    put(input_ref, conv_back(grad_cols_ref, first, width))


def swap(cells, axis, bit):
    return lax.ppermute(cells, axis, [(i, i ^ bit) for i in range(lax.axis_size(axis))])


def side_steps(count):
    if count == 2:
        return [[(0, 1), (1, 0)]]
    ends = count - 1
    return [[(i, i + 1) for i in range(ends)], [(i + 1, i) for i in range(ends)]]


def far_steps(count):
    pairs = [(i, i + 1) for i in range(1, count - 1, 2)]
    return pairs + [(b, a) for a, b in pairs]


def from_sides(cells):
    return [lax.ppermute(cells, "gy", step) for step in side_steps(lax.axis_size("gy"))]


def across(face, gx_steps, gy_steps):
    gy = lax.axis_size("gy")
    return lax.ppermute(
        face, ("gx", "gy"), [(a * gy + c, b * gy + d) for a, b in gx_steps for c, d in gy_steps]
    )


def from_far(face, late):
    steps = far_steps(lax.axis_size("gx"))
    far = lax.ppermute(face, "gx", steps)
    if late:
        return [far, *from_sides(far)]
    return [far] + [across(face, steps, side) for side in side_steps(lax.axis_size("gy"))]


def piece(cells, index, axis):
    return lax.dynamic_index_in_dim(cells, index, axis, keepdims=False)


def per_device(features, block_coords, block_counts, first_weight, second_weight, cotangent):
    gx, gy = lax.axis_size("gx"), lax.axis_size("gy")
    iy, ix = lax.axis_index("gy"), lax.axis_index("gx")
    slots = features.shape[2]
    width = slots * PLANE
    rows = 8 * width
    half, deep = ix // 2 % 2, ix // 4
    deeps = gx // 4
    grouped = gy == 2
    sides = 1 if grouped else 2
    chunk = TAPS * C // gx

    def shape(dims, kind=jnp.bfloat16):
        return jax.ShapeDtypeStruct(dims, kind)

    def call(kernel, name, outs, args, mib, micros, scratch=(), specs=None):
        return pl.pallas_call(
            kernel,
            out_shape=outs,
            in_specs=specs or [VMEM] * len(args),
            out_specs=(VMEM,) * len(outs),
            scratch_shapes=list(scratch),
            compiler_params=params(mib),
            cost_estimate=pl.CostEstimate(
                flops=int(micros * 1.1e9), bytes_accessed=2**20, transcendentals=0
            ),
            name=name,
        )(*args)

    own, face, thin_own, cross_own = call(
        pack_kernel,
        "pack",
        (
            shape((rows + META, C)),
            shape((2 * width + META, C)),
            shape((6 * width + META, C)),
            shape((6 * width + META, C)),
        ),
        (features, cotangent, block_coords, block_counts),
        60,
        3,
        [
            pltpu.SMEM((1, slots), jnp.int32),
            pltpu.SMEM((1, 1), jnp.int32),
            pltpu.SemaphoreType.DMA((2 + 8 * slots,)),
        ],
        [HBM] * 4,
    )
    side = from_sides(own)
    fars = from_far(face, False)
    others = []
    if grouped:
        beside = [(i, i ^ 2) for i in range(gx)]
        others = [swap(thin_own, "gx", 2), across(cross_own, beside, side_steps(gy)[0])]
    parts = [own, *side, *fars]
    relay, far_faces = call(
        functools.partial(relay_kernel, len(parts)),
        "relay",
        (
            shape((sum(cells.shape[0] for cells in parts), C)),
            shape((sum(cells.shape[0] for cells in fars), C)),
        ),
        (*parts, *others),
        8,
        3,
        [pltpu.SemaphoreType.DMA],
        [ANY] + [VMEM] * (len(parts) - 1) + [ANY] * len(others),
    )
    near_relay = swap(relay, "gx", 1)
    columns = shape((9, 6 * width, C))
    both, thin, cross, feature_cols, seed_cols, source, target = call(
        functools.partial(layer_kernel, sides),
        "layer",
        (
            shape((rows, C)),
            shape((6 * width, C)),
            shape((6 * width, C)),
            columns,
            columns,
            shape((2, LANES), jnp.float32),
            shape((9 * width, 1), jnp.float32),
        ),
        (relay, near_relay, first_weight, second_weight),
        12,
        4,
    )
    both_side = from_sides(both)

    def faced(*after):
        return call(
            face_kernel,
            "face",
            (shape((2 * width, C)),),
            (both, *after),
            8,
            0.3,
            specs=[VMEM] + [ANY] * len(after),
        )[0]

    grad_scale = 1.0 / math.sqrt(64 * slots * gx * gy)

    def over_z(own_part, sent):
        got = [swap(cells, "gx", 4 * m) for m, cells in enumerate(sent, 1)]
        return (own_part + sum(cells.astype(jnp.float32) for cells in got)) * grad_scale

    if grouped:
        cols = C // 2

        def gathered(name, cells, after):
            return call(
                functools.partial(gather_kernel, len(cells)),
                name,
                (shape((sum(part.shape[0] for part in cells), C)),),
                (*cells, *after),
                8,
                0.5,
                specs=[VMEM] * len(cells) + [ANY] * len(after),
            )[0]

        def group_shapes(count):
            return shape((count, *columns.shape)), shape((count, *columns.shape[:2], cols))

        early = gathered("gather_early", (*others, swap(far_faces, "gx", 2)), (both,))
        near_early = swap(early, "gx", 1)
        chip_features, chip_seeds = call(
            chip_cols_kernel, "chip_cols", group_shapes(len(CHIP_MEMBERS)), (relay, near_relay), 8, 2.5
        )
        late_fars = from_far(faced(chip_seeds), True)
        thin_other = swap(thin, "gx", 2)
        cross_other = across(cross, beside, side_steps(gy)[0])
        packed = gathered(
            "gather_late",
            (thin_other, cross_other, both, both_side[0]),
            (chip_seeds, late_fars[0]),
        )
        near_packed = swap(packed, "gx", 1)
        nears = [near_packed]
        other_features, other_seeds = call(
            other_cols_kernel,
            "other_cols",
            group_shapes(len(OTHER_MEMBERS)),
            (early, near_early, packed),
            8,
            3,
            specs=[VMEM] * 2 + [ANY],
        )
        members = [both, both_side[0], thin_other, cross_other, near_packed]
        taps = 2 + (chunk - 2) // C
        own_part, *sent = call(
            group_terms_kernel,
            "group_terms",
            (
                shape((2 * chunk, cols), jnp.float32),
                *[shape((2 * chunk, cols))] * (deeps - 1),
            ),
            (
                *members,
                feature_cols,
                seed_cols,
                chip_features,
                chip_seeds,
                other_features,
                other_seeds,
                late_fars[0],
            ),
            12,
            3.5,
            [pltpu.VMEM((deeps, taps * C, cols), jnp.float32)],
            [VMEM] * (len(members) + 6) + [ANY],
        )
        token = sent[0]
        grads = over_z(own_part, sent)
        first_grad, second_grad = grads[:chunk], grads[chunk:]
    else:
        nears = [swap(cells, "gx", 1) for cells in (both, *both_side)]
        late_fars = from_far(faced(), True)

        def summed(kernel, name, cells):
            keep, send = call(
                kernel,
                name,
                (
                    shape((gx // 2, chunk, C), jnp.float32),
                    shape((gx // 2, chunk, C)),
                ),
                (both, cells),
                24,
                4,
                [pltpu.VMEM((TAPS * C, C), jnp.float32)],
            )
            keep = keep.reshape(deeps, 2, chunk, C)
            got = swap(send, "gx", 1).reshape(keep.shape)

            def part(i):
                return piece(keep, i, 1) + piece(got, i, 1).astype(jnp.float32)

            total = part(half) + swap(part(1 - half).astype(jnp.bfloat16), "gx", 2).astype(
                jnp.float32
            )
            total = total.reshape(deeps, chunk, gy, C // gy)
            total = piece(total, iy, 2) + sum(
                swap(piece(total, iy ^ m, 2).astype(jnp.bfloat16), "gy", m).astype(jnp.float32)
                for m in range(1, gy)
            )
            total = over_z(
                piece(total, deep, 0),
                [piece(total, deep ^ m, 0).astype(jnp.bfloat16) for m in range(1, deeps)],
            )
            return total, send

        second_grad, token = summed(second_terms_kernel, "second_terms", seed_cols)
        first_grad, _ = summed(first_terms_kernel, "first_terms", feature_cols)

    late = [own, both, *both_side, *nears, *late_fars]
    result = shape((slots, 64, C), jnp.float32)
    output, input_grad = call(
        functools.partial(last_kernel, sides),
        "last_layer",
        (result, result),
        (*late, first_weight, second_weight, source, target, token),
        12,
        0.1,
        [pltpu.VMEM(columns.shape, jnp.bfloat16)] * 2,
        [VMEM] * (len(late) + 4) + [ANY],
    )
    return (
        output.reshape(features.shape),
        input_grad.reshape(features.shape),
        first_grad,
        second_grad,
    )


def solution(mesh):
    placed = (
        P("gx", "gy", None, None, None),
        P("gx", "gy", None),
        P("gx", "gy"),
        P(),
        P(),
        P("gx", "gy", None, None, None),
    )
    return jax.shard_map(
        per_device,
        mesh=mesh,
        in_specs=placed,
        out_specs=(
            P("gx", "gy", None, None, None),
            P("gx", "gy", None, None, None),
            P("gx", "gy"),
            P("gx", "gy"),
        ),
        check_vma=False,
    )
```

```python
import functools
import math

import jax
import jax.numpy as jnp
from jax import lax
from jax.experimental import pallas as pl
from jax.experimental.pallas import tpu as pltpu
from jax.sharding import PartitionSpec as P

C = 256
TAPS = 27
PLANE = 16
META = 16
LANES = 512
STEP_Y = 64.0
STEP_X = 4096.0
NOWHERE = -1.0e7
VMEM = pl.BlockSpec(memory_space=pltpu.MemorySpace.VMEM)
HBM = pl.BlockSpec(memory_space=pltpu.MemorySpace.HBM)
ANY = pl.BlockSpec(memory_space=pl.ANY)


def params(mib):
    return pltpu.CompilerParams(vmem_limit_bytes=mib * 2**20)


def dot(lhs, rhs, dims=((1,), (0,))):
    return lax.dot_general(lhs, rhs, (dims, ((), ())), preferred_element_type=jnp.float32)


def iota(shape, dim):
    return lax.broadcasted_iota(jnp.int32, shape, dim)


def place_codes(meta, offset, absent=NOWHERE):
    rows = meta.astype(jnp.float32)
    parts = []
    for half in range(2):
        x, y, z, live = (rows[4 * half + i : 4 * half + i + 1] for i in range(4))
        parts.append(jnp.where(live > 0.5, x * STEP_X + y * STEP_Y + z + offset, absent))
    return jnp.concatenate(parts, axis=1)


def source_codes(metas, offsets, width):
    lane = iota((1, LANES), 1)
    total = jnp.full((1, LANES), NOWHERE, jnp.float32)
    for place, (meta, offset) in enumerate(zip(metas, offsets)):
        inside = (lane >= place * width) & (lane < (place + 1) * width)
        total = jnp.where(inside, place_codes(meta, offset), total)
    return total


def target_codes(meta, width):
    codes = place_codes(meta, 0.0, 3 * NOWHERE)
    own = iota((width, LANES), 0) == iota((width, LANES), 1)
    column = jnp.sum(jnp.where(own, codes, 0.0), axis=1, keepdims=True)
    return jnp.concatenate(
        [column + ((s // 3 - 1) * STEP_Y + (s % 3 - 1)) for s in range(9)], axis=0
    )


def selectors(before, after, target, sides, width):
    middle = (1 + sides) * width
    return tuple(
        (codes == target + step).astype(jnp.float32).astype(jnp.bfloat16)
        for codes, step in (
            (before[:, : 2 * middle], -STEP_X),
            (before[:, :middle], 0.0),
            (after[:, : 2 * middle], STEP_X),
        )
    )


def fill(cols_ref, tiles, faces, odd, chosen, width, columns=slice(None)):
    def load(source, plane):
        ref, first, paired = source
        if paired:
            at = first + plane % 2 * width
            return ref[at : at + width, plane // 2 * (C // 2) : (plane // 2 + 1) * (C // 2)]
        return ref[first + plane * width : first + (plane + 1) * width, columns]

    for plane in range(6):
        if plane in (0, 5):
            start = 3 if plane == 0 else 0
            pieces = [load(tile, start) for tile in tiles]
            for near, far in faces:
                if far is None:
                    pieces.append(load(near, start))
                    continue
                near, far = load(near, start), load(far, 0)
                pieces.append(jnp.where(odd, near, far) if plane == 0 else jnp.where(odd, far, near))
        else:
            pieces = [load(tile, plane - 1) for tile in tiles]
        select = chosen[0 if plane == 0 else 2 if plane == 5 else 1]
        moved = dot(select, jnp.concatenate(pieces, axis=0)).astype(jnp.bfloat16)
        for shift in range(9):
            cols_ref[shift, plane * width : (plane + 1) * width, :] = moved[
                shift * width : (shift + 1) * width
            ]


def tap_rows(cols_ref, tap, width, columns=slice(None)):
    start = tap // 9 * width
    return cols_ref[tap % 9, start : start + 4 * width, columns]


def conv(cols_ref, weight_ref, width):
    total = None
    for tap in range(TAPS):
        term = dot(tap_rows(cols_ref, tap, width), weight_ref[tap * C : (tap + 1) * C, :])
        total = term if total is None else total + term
    return total


def conv_back(cols_ref, weight_ref, width):
    total = None
    for tap in range(TAPS):
        weight = weight_ref[(26 - tap) * C : (27 - tap) * C, :]
        term = dot(tap_rows(cols_ref, tap, width), weight, ((1,), (1,)))
        total = term if total is None else total + term
    return total


def live_rows(meta, width):
    codes = place_codes(meta, 0.0)
    own = iota((width, LANES), 0) == iota((width, LANES), 1)
    column = jnp.sum(jnp.where(own, codes, 0.0), axis=1, keepdims=True)
    return jnp.concatenate([column] * 4, axis=0) > 0.5 * NOWHERE


def near_row(width):
    return pl.multiple_of((lax.axis_index("gx") % 2) * (3 * width), PLANE)


def side_offsets(sides):
    if sides == 2:
        return [-8 * STEP_Y, 8 * STEP_Y]
    return [(1 - 2 * lax.axis_index("gy")).astype(jnp.float32) * (8 * STEP_Y)]


def pack_kernel(features, cotangent, coords, counts, *refs):
    own_ref, face_ref, place_ref, live_ref, sems = refs
    slots = features.shape[2]
    width = slots * PLANE
    copies = [
        pltpu.make_async_copy(coords.at[0], place_ref, sems.at[0]),
        pltpu.make_async_copy(counts, live_ref, sems.at[1]),
    ]
    for field, ref in enumerate((features, cotangent)):
        for x in range(4):
            for slot in range(slots):
                start = field * 4 * width + x * width + slot * PLANE
                copies.append(
                    pltpu.make_async_copy(
                        ref.at[0, 0, slot, pl.ds(x * PLANE, PLANE)],
                        own_ref.at[pl.ds(start, PLANE)],
                        sems.at[len(copies)],
                    )
                )
    for copy in copies:
        copy.start()
    for copy in copies:
        copy.wait()
    lane = iota((1, LANES), 1)
    lane_slot = (lane // PLANE) % slots
    position = jnp.zeros((1, LANES), jnp.int32)
    for slot in range(slots):
        position = jnp.where(lane_slot == slot, place_ref[0, slot], position)
    values = [
        position // 16,
        4 * (position // 8 % 2) + lane % PLANE // 4,
        4 * (position % 8) + lane % 4,
        (lane_slot < live_ref[0, 0]).astype(jnp.int32),
    ]
    rows = [v[:, h * C : (h + 1) * C] for h in range(2) for v in values]
    rows.append(jnp.zeros((META - 8, C), jnp.int32))
    meta = jnp.concatenate(rows, axis=0).astype(jnp.float32).astype(jnp.bfloat16)
    own_ref[8 * width :, :] = meta
    at = near_row(width)
    face_ref[:width, :] = own_ref[pl.ds(at, width), :]
    face_ref[width : 2 * width, :] = own_ref[pl.ds(pl.multiple_of(4 * width + at, PLANE), width), :]
    face_ref[2 * width :, :] = meta


class Around:
    def __init__(self, tiles, fars, sides, rows):
        self.tiles, self.fars, self.sides = tiles, fars, sides
        self.rows, self.width = rows, rows // 8

    def order(self, s):
        return [s] + [other for other in range(1 + self.sides) if other != s]

    def odd(self, j):
        return (lax.axis_index("gx") + j) % 2 == 1

    def codes(self, j, s):
        def meta(ref, start):
            return ref[start : start + 8, :]

        def tile_meta(j, o):
            ref, first, thin = self.tiles[j][o]
            return meta(ref, first + (self.rows * 3 // 4 if thin else self.rows))

        order = self.order(s)
        metas = [tile_meta(j, o) for o in order]
        offsets = side_offsets(self.sides)
        offsets = [0.0] + ([-o for o in offsets] if s else offsets)
        befores, afters = [], []
        for o in order:
            near = tile_meta(j ^ 1, o)
            if self.fars is None:
                far = jnp.zeros_like(near)
            else:
                ref, first = self.fars[j][o]
                far = meta(ref, first + 2 * self.width)
            befores.append(jnp.where(self.odd(j), near, far))
            afters.append(jnp.where(self.odd(j), far, near))
        before, after = (
            source_codes(metas + beyond, offsets + [o + step for o in offsets], self.width)
            for beyond, step in ((befores, -2 * STEP_X), (afters, 2 * STEP_X))
        )
        return before, after, target_codes(metas[0], self.width)

    def sources(self, j, s, field):
        def tile(j, o):
            ref, first, thin = self.tiles[j][o]
            return ref, first + field * 4 * self.width, thin and field == 1

        order = self.order(s)
        faces = []
        for o in order:
            far = None
            if self.fars is not None:
                ref, first = self.fars[j][o]
                far = (ref, first + field * self.width, False)
            faces.append((tile(j ^ 1, o), far))
        return [tile(j, o) for o in order], faces, self.odd(j)


def chip_places(refs, sides, rows):
    return [[(ref, s * (rows + META), False) for s in range(1 + sides)] for ref in refs]


def main_kernel(sides, *refs):
    tiles, refs = refs[:2], refs[2:]
    first, second, pre_ref, back_ref, feature_cols, seed_cols = refs
    rows = 2 * pre_ref.shape[0]
    width = rows // 8
    around = Around(chip_places(tiles, sides, rows), None, sides, rows)
    chosen = selectors(*around.codes(0, 0), sides, width)
    fill(feature_cols, *around.sources(0, 0, 0), chosen, width)
    fill(seed_cols, *around.sources(0, 0, 1), chosen, width)
    pre_ref[...] = conv(feature_cols, first, width)
    back_ref[...] = conv_back(seed_cols, second, width)


def layer_kernel(sides, *refs):
    tiles, refs = refs[:2], refs[2:]
    fars, refs = refs[: 1 + sides], refs[1 + sides :]
    first, second, pre_main, back_main = refs[:4]
    both_ref, slim_ref, cross_ref, source_ref, target_ref, pre_ref, back_ref = refs[-7:]
    rows = both_ref.shape[0]
    width = rows // 8
    around = Around(chip_places(tiles, sides, rows), [[(ref, 0) for ref in fars]], sides, rows)
    before, after, target = around.codes(0, 0)
    source_ref[0:1, :] = before
    source_ref[1:2, :] = after
    target_ref[...] = target
    odd = around.odd(0)
    codes = jnp.where(odd, after, before)[:, : 2 * (1 + sides) * width]
    chosen = (codes == target + jnp.where(odd, STEP_X, -STEP_X)).astype(jnp.float32)
    chosen = chosen.astype(jnp.bfloat16)
    nothing = jnp.zeros(((1 + sides) * width, C), jnp.bfloat16)
    at = near_row(width)

    def add(total_ref, main_ref, field, weight):
        pieces = [nothing] + [ref[field * width : (field + 1) * width, :] for ref in fars]
        moved = dot(chosen, jnp.concatenate(pieces, axis=0)).astype(jnp.bfloat16)
        more = sum(weight(shift, moved[shift * width : (shift + 1) * width]) for shift in range(9))
        total_ref[...] = main_ref[...]
        total_ref[pl.ds(at, width), :] = total_ref[pl.ds(at, width), :] + more

    def tap(weight_ref, index):
        return weight_ref[pl.ds(pl.multiple_of(index * C, C), C), :]

    add(
        pre_ref,
        pre_main,
        0,
        lambda shift, cells: dot(cells, tap(first, jnp.where(odd, 18, 0) + shift)),
    )
    add(
        back_ref,
        back_main,
        1,
        lambda shift, cells: dot(cells, tap(second, jnp.where(odd, 8, 26) - shift), ((1,), (1,))),
    )
    pre_first = pre_ref[...]
    live = live_rows(tiles[0][rows : rows + 8, :], width)
    sigmoid = 1.0 / (1.0 + jnp.exp(-pre_first))
    hidden = jnp.where(live, pre_first * sigmoid, 0.0)
    both_ref[: 4 * width, :] = hidden.astype(jnp.bfloat16)
    slope = jnp.where(live, sigmoid * (1.0 + pre_first * (1.0 - sigmoid)), 0.0)
    both_ref[4 * width :, :] = (back_ref[...] * slope).astype(jnp.bfloat16)
    if sides == 1:
        slim(both_ref, slim_ref, lax.axis_index("gy"))
        slim(both_ref, cross_ref, 1 - lax.axis_index("gy"))
    else:
        slim_ref[...] = jnp.zeros(slim_ref.shape, slim_ref.dtype)
        cross_ref[...] = jnp.zeros(cross_ref.shape, cross_ref.dtype)


def join_kernel(count, *refs):
    joined_ref, slim_ref = refs[-2:]
    gather_kernel(count, *refs[:count], joined_ref)
    if count == 2:
        size = slim_ref.shape[0] // 2
        for i in range(2):
            slim(refs[i], slim_ref.at[pl.ds(i * size, size)], lax.axis_index("gy"))
    else:
        slim_ref[...] = jnp.zeros(slim_ref.shape, slim_ref.dtype)


def slim(tile_ref, slim_ref, half):
    rows = tile_ref.shape[0] // (8 * PLANE) * 4 * PLANE
    columns = pl.ds(pl.multiple_of(half * (C // 2), 128), C // 2)
    slim_ref[:rows, :] = tile_ref[:rows, :]
    slim_ref[rows : rows + rows // 2, : C // 2] = tile_ref[rows : rows + rows // 2, columns]
    slim_ref[rows : rows + rows // 2, C // 2 :] = tile_ref[rows + rows // 2 : 2 * rows, columns]
    if slim_ref.shape[0] > rows + rows // 2:
        slim_ref[rows + rows // 2 :, :] = tile_ref[2 * rows :, :]


def gather_kernel(count, *refs):
    packed_ref = refs[-1]
    at = 0
    for ref in refs[:count]:
        packed_ref[at : at + ref.shape[0], :] = ref[...]
        at += ref.shape[0]


def face_kernel(both_ref, *refs):
    face_ref = refs[-1]
    width = both_ref.shape[0] // 8
    at = near_row(width)
    face_ref[:width, :] = both_ref[pl.ds(at, width), :]
    face_ref[width:, :] = both_ref[pl.ds(pl.multiple_of(4 * width + at, PLANE), width), :]


def my_columns(cols):
    if cols == C:
        return slice(None)
    return pl.ds(pl.multiple_of(lax.axis_index("gy") * cols, 128), cols)


def store_terms(keep_ref, send_ref, total_ref):
    core = lax.axis_index("gx") % 2
    pairs, rows = keep_ref.shape[0], keep_ref.shape[1]
    for i in range(pairs):
        keep_at = pl.multiple_of((2 * i + core) * rows, 8)
        send_at = pl.multiple_of((2 * i + 1 - core) * rows, 8)
        keep_ref[i] = total_ref[pl.ds(keep_at, rows), :]
        send_ref[i] = total_ref[pl.ds(send_at, rows), :]


def second_terms_kernel(both_ref, cols_ref, keep_ref, send_ref, total_ref):
    rows = both_ref.shape[0] // 2
    hidden = both_ref[:rows, :].astype(jnp.float32).T.astype(jnp.bfloat16)
    for tap in range(TAPS):
        total_ref[tap * C : (tap + 1) * C, :] = dot(hidden, tap_rows(cols_ref, 26 - tap, rows // 4))
    store_terms(keep_ref, send_ref, total_ref)


def first_terms_kernel(both_ref, cols_ref, keep_ref, send_ref, total_ref):
    rows = both_ref.shape[0] // 2
    grad = both_ref[rows:, :]
    for tap in range(TAPS):
        total_ref[tap * C : (tap + 1) * C, :] = dot(
            tap_rows(cols_ref, tap, rows // 4), grad, ((0,), (0,))
        )
    store_terms(keep_ref, send_ref, total_ref)


def group_cols(around, members, feature_ref, seed_ref):
    columns = my_columns(seed_ref.shape[3])
    for index, (j, s) in enumerate(members):
        chosen = selectors(*around.codes(j, s), around.sides, around.width)
        fill(feature_ref.at[index], *around.sources(j, s, 0), chosen, around.width)
        fill(seed_ref.at[index], *around.sources(j, s, 1), chosen, around.width, columns)


CHIP_MEMBERS = (((0, 0), (0, 1)), ((1, 0), (1, 1)))
OTHER_MEMBERS = ((2, 0), (2, 1), (3, 0), (3, 1))


def chip_cols_kernel(sides, members, *refs):
    tiles, (far, near_far), (feature_ref, seed_ref) = refs[:2], refs[2:4], refs[-2:]
    rows = feature_ref.shape[2] // 6 * 8
    face = rows // 4 + META
    fars = [[(ref, s * face) for s in range(1 + sides)] for ref in (far, near_far)]
    around = Around(chip_places(tiles, sides, rows), fars, sides, rows)
    group_cols(around, members, feature_ref, seed_ref)


def other_cols_kernel(packed, near_packed, _, feature_ref, seed_ref):
    width = feature_ref.shape[2] // 6
    rows = 8 * width
    thin, face = 6 * width + META, 2 * width + META
    tiles = [[(ref, s * thin, True) for s in range(2)] for ref in (packed, near_packed)]
    fars = [[(ref, 2 * thin + s * face) for s in range(2)] for ref in (packed, near_packed)]
    around = Around([None, None] + tiles, [None, None] + fars, 1, rows)
    group_cols(around, OTHER_MEMBERS, feature_ref, seed_ref)


def group_terms(cols_of, fields, first, top, out_refs, total_ref):
    own_ref, send_refs = out_refs[0], out_refs[1:]
    chunk, cols = own_ref.shape[0] // 2, own_ref.shape[1]
    deep = lax.axis_index("gx") // 4
    row = lax.axis_index("gx") % 4
    taps = total_ref.shape[1] // C
    width = fields[0].shape[0] // 4
    starts = [((deep ^ m) * 4 + row) * chunk for m in range(1 + len(send_refs))]

    def rows(tap):
        tap = jnp.minimum(tap, TAPS - 1)
        tap = tap if first else TAPS - 1 - tap
        at = pl.multiple_of(tap // 9 * width, PLANE)
        return jnp.concatenate(
            [cols_of(i, tap % 9, pl.ds(at, 4 * width)) for i in range(len(fields))], axis=0
        )

    operand = jnp.concatenate(fields, axis=0).astype(jnp.float32).T.astype(jnp.bfloat16)
    wanted = [(m, i) for m in range(len(starts)) for i in range(taps)]
    if first:
        for m, i in wanted:
            result = dot(operand, rows(starts[m] // C + i))
            total_ref[m, i * C : (i + 1) * C, :] = result.T
    else:
        step = max(1, C // cols)
        for at in range(0, len(wanted), step):
            part = wanted[at : at + step]
            result = dot(
                operand, jnp.concatenate([rows(starts[m] // C + i) for m, i in part], axis=1)
            )
            for place, (m, i) in enumerate(part):
                total_ref[m, i * C : (i + 1) * C, :] = result[:, place * cols : (place + 1) * cols]
    for m, start in enumerate(starts):
        at = pl.multiple_of(start % C, 16)
        if m == 0:
            own_ref[top : top + chunk, :] = total_ref[m, pl.ds(at, chunk), :]
        else:
            send_refs[m - 1][top : top + chunk, :] = total_ref[m, pl.ds(at, chunk), :].astype(
                jnp.bfloat16
            )


def group_terms_kernel(*refs):
    both, thins, packed, refs = refs[:2], refs[2:4], refs[4], refs[5:]
    groups, refs = refs[:6], refs[6:]
    out_refs, total_ref = refs[:-1], refs[-1]
    rows = both[0].shape[0] // 2
    chunk = out_refs[0].shape[0] // 2
    columns = my_columns(out_refs[0].shape[1])
    thin_rows = thins[0].shape[0]
    both = [(ref, 0) for ref in both]
    both += [(packed, 2 * thin_rows), (packed, 2 * thin_rows + 2 * rows)]
    thins = [(ref, 0) for ref in thins] + [(packed, 0), (packed, thin_rows)]

    def group(part, tile, shift, at):
        place, index = (tile // 2, tile % 2) if tile < 4 else (2, tile - 4)
        return groups[part + 2 * place][index, shift, at, :]

    features_of, seeds_of = functools.partial(group, 0), functools.partial(group, 1)
    grads = [ref[at + rows : at + 2 * rows, columns] for ref, at in both]
    for ref, at in thins:
        halves = ref[at + rows : at + rows + rows // 2, :]
        grads.append(jnp.concatenate([halves[:, : C // 2], halves[:, C // 2 :]], axis=0))
    hiddens = [ref[at : at + rows, :] for ref, at in (*both, *thins)]
    group_terms(features_of, grads, True, 0, out_refs, total_ref)
    group_terms(seeds_of, hiddens, False, chunk, out_refs, total_ref)


def last_kernel(sides, *refs):
    own_ref, refs = refs[0], refs[1:]
    tiles, refs = refs[: 1 + sides], refs[1 + sides :]
    count = 1 if sides == 1 else 1 + sides
    nears, refs = refs[:count], refs[count:]
    fars, refs = refs[: 1 + sides], refs[1 + sides :]
    first, second, source_ref, target_ref, _, output_ref, input_ref = refs[:7]
    hidden_cols_ref, grad_cols_ref = refs[7:]
    width = tiles[0].shape[0] // 8
    slots = output_ref.shape[0]
    chosen = selectors(source_ref[0:1, :], source_ref[1:2, :], target_ref[...], sides, width)
    live = live_rows(own_ref[8 * width : 8 * width + 8, :], width)
    rows = tiles[0].shape[0]
    if sides == 1:
        near_at = nears[0].shape[0] - 2 * rows
        nears = [(nears[0], near_at, False), (nears[0], near_at + rows, False)]
    else:
        nears = [(ref, 0, False) for ref in nears]
    around = Around(
        [[(ref, 0, False) for ref in tiles], nears],
        [[(ref, 0) for ref in fars]],
        sides,
        rows,
    )

    def put(ref, total):
        total = jnp.where(live, total, 0.0)
        for x in range(4):
            for slot in range(slots):
                start = x * width + slot * PLANE
                ref[slot, x * PLANE : (x + 1) * PLANE, :] = total[start : start + PLANE]

    fill(hidden_cols_ref, *around.sources(0, 0, 0), chosen, width)
    fill(grad_cols_ref, *around.sources(0, 0, 1), chosen, width)
    put(output_ref, conv(hidden_cols_ref, second, width))
    put(input_ref, conv_back(grad_cols_ref, first, width))


def swap(cells, axis, bit):
    return lax.ppermute(cells, axis, [(i, i ^ bit) for i in range(lax.axis_size(axis))])


def side_steps(count):
    if count == 2:
        return [[(0, 1), (1, 0)]]
    ends = count - 1
    return [[(i, i + 1) for i in range(ends)], [(i + 1, i) for i in range(ends)]]


def far_steps(count):
    pairs = [(i, i + 1) for i in range(1, count - 1, 2)]
    return pairs + [(b, a) for a, b in pairs]


def from_sides(cells):
    return [lax.ppermute(cells, "gy", step) for step in side_steps(lax.axis_size("gy"))]


def across(face, gx_steps, gy_steps):
    gy = lax.axis_size("gy")
    return lax.ppermute(
        face, ("gx", "gy"), [(a * gy + c, b * gy + d) for a, b in gx_steps for c, d in gy_steps]
    )


def from_far(face):
    far = lax.ppermute(face, "gx", far_steps(lax.axis_size("gx")))
    return [far, *from_sides(far)]


def piece(cells, index, axis):
    return lax.dynamic_index_in_dim(cells, index, axis, keepdims=False)


def per_device(features, block_coords, block_counts, first_weight, second_weight, cotangent):
    gx, gy = lax.axis_size("gx"), lax.axis_size("gy")
    iy, ix = lax.axis_index("gy"), lax.axis_index("gx")
    slots = features.shape[2]
    width = slots * PLANE
    rows = 8 * width
    half, deep = ix // 2 % 2, ix // 4
    deeps = gx // 4
    grouped = gy == 2
    sides = 1 if grouped else 2
    chunk = TAPS * C // gx

    def shape(dims, kind=jnp.bfloat16):
        return jax.ShapeDtypeStruct(dims, kind)

    def call(kernel, name, outs, args, mib, micros, scratch=(), specs=None):
        return pl.pallas_call(
            kernel,
            out_shape=outs,
            in_specs=specs or [VMEM] * len(args),
            out_specs=(VMEM,) * len(outs),
            scratch_shapes=list(scratch),
            compiler_params=params(mib),
            cost_estimate=pl.CostEstimate(
                flops=int(micros * 1.1e9), bytes_accessed=2**20, transcendentals=0
            ),
            name=name,
        )(*args)

    own, face = call(
        pack_kernel,
        "pack",
        (
            shape((rows + META, C)),
            shape((2 * width + META, C)),
        ),
        (features, cotangent, block_coords, block_counts),
        60,
        3,
        [
            pltpu.SMEM((1, slots), jnp.int32),
            pltpu.SMEM((1, 1), jnp.int32),
            pltpu.SemaphoreType.DMA((2 + 8 * slots,)),
        ],
        [HBM] * 4,
    )
    side = from_sides(own)
    field = (4 * width, C)
    fars = from_far(face)
    def gathered(name, cells, after, micros=0.5):
        return call(
            functools.partial(gather_kernel, len(cells)),
            name,
            (shape((sum(part.shape[0] for part in cells), C)),),
            (*cells, *after),
            8,
            micros,
            specs=[VMEM] * len(cells) + [ANY] * len(after),
        )[0]

    parts = [own, *side]
    chip, thins = call(
        functools.partial(join_kernel, len(parts)),
        "join",
        (
            shape((len(parts) * (rows + META), C)),
            shape((2 * (6 * width + META), C)),
        ),
        (*parts, fars[0]),
        8,
        3,
        specs=[VMEM] * len(parts) + [ANY],
    )
    chip = [chip, swap(chip, "gx", 1)]
    columns = shape((9, 6 * width, C))
    main = call(
        functools.partial(main_kernel, sides),
        "first_convs",
        (shape(field, jnp.float32),) * 2,
        (*chip, first_weight, second_weight),
        12,
        3,
        [pltpu.VMEM(columns.shape, jnp.bfloat16)] * 2,
    )
    both, thin, cross, source, target = call(
        functools.partial(layer_kernel, sides),
        "layer",
        (
            shape((rows, C)),
            shape((6 * width, C)),
            shape((6 * width, C)),
            shape((2, LANES), jnp.float32),
            shape((9 * width, 1), jnp.float32),
        ),
        (*chip, *fars, first_weight, second_weight, *main),
        8,
        1,
        [pltpu.VMEM(field, jnp.float32)] * 2,
    )
    both_side = from_sides(both)

    def late_far(after):
        (late_face,) = call(
            face_kernel,
            "face",
            (shape((2 * width, C)),),
            (both, *after),
            8,
            0.3,
            specs=[VMEM] + [ANY] * len(after),
        )
        return from_far(late_face)

    grad_scale = 1.0 / math.sqrt(64 * slots * gx * gy)

    def over_z(own_part, sent):
        got = [swap(cells, "gx", 4 * m) for m, cells in enumerate(sent, 1)]
        return (own_part + sum(cells.astype(jnp.float32) for cells in got)) * grad_scale

    if grouped:
        cols = C // 2

        def group_shapes(count):
            return shape((count, *columns.shape)), shape((count, *columns.shape[:2], cols))

        far_faces = gathered("far_faces", fars, main[:1])
        near_faces = swap(far_faces, "gx", 1)
        beside = [swap(thins, "gx", 2), swap(far_faces, "gx", 2)]
        early = gathered("gather_early", beside, (both,))
        near_early = swap(early, "gx", 1)
        chip_cols = [
            call(
                functools.partial(chip_cols_kernel, 1, members),
                "chip_cols",
                group_shapes(len(members)),
                (*chip, far_faces, near_faces, *after),
                8,
                1.6,
                specs=[VMEM] * 4 + [ANY] * len(after),
            )
            for members, after in zip(CHIP_MEMBERS, ((), beside))
        ]
        late_fars = late_far(chip_cols[0][1:])
        thin_other = swap(thin, "gx", 2)
        cross_other = across(cross, [(i, i ^ 2) for i in range(gx)], side_steps(gy)[0])
        packed = gathered(
            "gather_late",
            (thin_other, cross_other, both, both_side[0]),
            (chip_cols[1][1], late_fars[0]),
        )
        near_packed = swap(packed, "gx", 1)
        nears = [near_packed]
        other_features, other_seeds = call(
            other_cols_kernel,
            "other_cols",
            group_shapes(len(OTHER_MEMBERS)),
            (early, near_early, packed),
            8,
            3,
            specs=[VMEM] * 2 + [ANY],
        )
        members = [both, both_side[0], thin_other, cross_other, near_packed]
        taps = 2 + (chunk - 2) // C
        own_part, *sent = call(
            group_terms_kernel,
            "group_terms",
            (
                shape((2 * chunk, cols), jnp.float32),
                *[shape((2 * chunk, cols))] * (deeps - 1),
            ),
            (
                *members,
                *chip_cols[0],
                *chip_cols[1],
                other_features,
                other_seeds,
            ),
            12,
            3.5,
            [pltpu.VMEM((deeps, taps * C, cols), jnp.float32)],
        )
        token = sent[0]
        grads = over_z(own_part, sent)
        first_grad, second_grad = grads[:chunk], grads[chunk:]
    else:
        far_faces = jnp.concatenate(fars, axis=0)
        nears = [swap(cells, "gx", 1) for cells in (both, *both_side)]
        late_fars = late_far(())

        def summed(kernel, name, cells):
            keep, send = call(
                kernel,
                name,
                (
                    shape((gx // 2, chunk, C), jnp.float32),
                    shape((gx // 2, chunk, C), jnp.float32),
                ),
                (both, cells),
                24,
                4,
                [pltpu.VMEM((TAPS * C, C), jnp.float32)],
            )
            keep = keep.reshape(deeps, 2, chunk, C)
            got = swap(send, "gx", 1).reshape(keep.shape)

            def part(i):
                return piece(keep, i, 1) + piece(got, i, 1)

            total = part(half) + swap(part(1 - half).astype(jnp.bfloat16), "gx", 2).astype(
                jnp.float32
            )
            total = total.reshape(deeps, chunk, gy, C // gy)
            total = piece(total, iy, 2) + sum(
                swap(piece(total, iy ^ m, 2).astype(jnp.bfloat16), "gy", m).astype(jnp.float32)
                for m in range(1, gy)
            )
            total = over_z(
                piece(total, deep, 0),
                [piece(total, deep ^ m, 0).astype(jnp.bfloat16) for m in range(1, deeps)],
            )
            return total, send

        feature_cols, seed_cols = call(
            functools.partial(chip_cols_kernel, sides, ((0, 0),)),
            "own_cols",
            (shape((1, *columns.shape)),) * 2,
            (*chip, far_faces, far_faces),
            8,
            1,
        )
        feature_cols, seed_cols = feature_cols[0], seed_cols[0]
        second_grad, token = summed(second_terms_kernel, "second_terms", seed_cols)
        first_grad, _ = summed(first_terms_kernel, "first_terms", feature_cols)

    late = [chip[0], both, *both_side, *nears, *late_fars]
    result = shape((slots, 64, C), jnp.float32)
    output, input_grad = call(
        functools.partial(last_kernel, sides),
        "last_layer",
        (result, result),
        (*late, first_weight, second_weight, source, target, token),
        12,
        0.1,
        [pltpu.VMEM(columns.shape, jnp.bfloat16)] * 2,
        [VMEM] * (len(late) + 4) + [ANY],
    )
    return (
        output.reshape(features.shape),
        input_grad.reshape(features.shape),
        first_grad,
        second_grad,
    )


def solution(mesh):
    placed = (
        P("gx", "gy", None, None, None),
        P("gx", "gy", None),
        P("gx", "gy"),
        P(),
        P(),
        P("gx", "gy", None, None, None),
    )
    return jax.shard_map(
        per_device,
        mesh=mesh,
        in_specs=placed,
        out_specs=(
            P("gx", "gy", None, None, None),
            P("gx", "gy", None, None, None),
            P("gx", "gy"),
            P("gx", "gy"),
        ),
        check_vma=False,
    )
```

```python
import functools
import math

import jax
import jax.numpy as jnp
from jax import lax
from jax.experimental import pallas as pl
from jax.experimental.pallas import tpu as pltpu
from jax.sharding import PartitionSpec as P

C = 256
TAPS = 27
PLANE = 16
META = 16
LANES = 512
STEP_Y = 64.0
STEP_X = 4096.0
NOWHERE = -1.0e7
VMEM = pl.BlockSpec(memory_space=pltpu.MemorySpace.VMEM)
HBM = pl.BlockSpec(memory_space=pltpu.MemorySpace.HBM)
ANY = pl.BlockSpec(memory_space=pl.ANY)


def params(mib):
    return pltpu.CompilerParams(vmem_limit_bytes=mib * 2**20)


def dot(lhs, rhs, dims=((1,), (0,))):
    return lax.dot_general(lhs, rhs, (dims, ((), ())), preferred_element_type=jnp.float32)


def iota(shape, dim):
    return lax.broadcasted_iota(jnp.int32, shape, dim)


def place_codes(meta, offset, absent=NOWHERE):
    rows = meta.astype(jnp.float32)
    parts = []
    for half in range(2):
        x, y, z, live = (rows[4 * half + i : 4 * half + i + 1] for i in range(4))
        parts.append(jnp.where(live > 0.5, x * STEP_X + y * STEP_Y + z + offset, absent))
    return jnp.concatenate(parts, axis=1)


def source_codes(metas, offsets, width):
    lane = iota((1, LANES), 1)
    total = jnp.full((1, LANES), NOWHERE, jnp.float32)
    for place, (meta, offset) in enumerate(zip(metas, offsets)):
        inside = (lane >= place * width) & (lane < (place + 1) * width)
        total = jnp.where(inside, place_codes(meta, offset), total)
    return total


def target_codes(meta, width):
    codes = place_codes(meta, 0.0, 3 * NOWHERE)
    own = iota((width, LANES), 0) == iota((width, LANES), 1)
    column = jnp.sum(jnp.where(own, codes, 0.0), axis=1, keepdims=True)
    return jnp.concatenate(
        [column + ((s // 3 - 1) * STEP_Y + (s % 3 - 1)) for s in range(9)], axis=0
    )


def selectors(before, after, target, sides, width):
    middle = (1 + sides) * width
    return tuple(
        (codes == target + step).astype(jnp.float32).astype(jnp.bfloat16)
        for codes, step in (
            (before[:, : 2 * middle], -STEP_X),
            (before[:, :middle], 0.0),
            (after[:, : 2 * middle], STEP_X),
        )
    )


def fill(cols_ref, tiles, faces, odd, chosen, width, columns=slice(None)):
    def load(source, plane):
        ref, first, paired = source
        if paired:
            at = first + plane % 2 * width
            return ref[at : at + width, plane // 2 * (C // 2) : (plane // 2 + 1) * (C // 2)]
        return ref[first + plane * width : first + (plane + 1) * width, columns]

    for plane in range(6):
        if plane in (0, 5):
            start = 3 if plane == 0 else 0
            pieces = [load(tile, start) for tile in tiles]
            for near, far in faces:
                if far is None:
                    pieces.append(load(near, start))
                    continue
                near, far = load(near, start), load(far, 0)
                pieces.append(jnp.where(odd, near, far) if plane == 0 else jnp.where(odd, far, near))
        else:
            pieces = [load(tile, plane - 1) for tile in tiles]
        select = chosen[0 if plane == 0 else 2 if plane == 5 else 1]
        moved = dot(select, jnp.concatenate(pieces, axis=0)).astype(jnp.bfloat16)
        for shift in range(9):
            cols_ref[shift, plane * width : (plane + 1) * width, :] = moved[
                shift * width : (shift + 1) * width
            ]


def tap_rows(cols_ref, tap, width, columns=slice(None)):
    start = tap // 9 * width
    return cols_ref[tap % 9, start : start + 4 * width, columns]


def conv(cols_ref, weight_ref, width):
    total = None
    for tap in range(TAPS):
        term = dot(tap_rows(cols_ref, tap, width), weight_ref[tap * C : (tap + 1) * C, :])
        total = term if total is None else total + term
    return total


def conv_back(cols_ref, weight_ref, width):
    total = None
    for tap in range(TAPS):
        weight = weight_ref[(26 - tap) * C : (27 - tap) * C, :]
        term = dot(tap_rows(cols_ref, tap, width), weight, ((1,), (1,)))
        total = term if total is None else total + term
    return total


def live_rows(meta, width):
    codes = place_codes(meta, 0.0)
    own = iota((width, LANES), 0) == iota((width, LANES), 1)
    column = jnp.sum(jnp.where(own, codes, 0.0), axis=1, keepdims=True)
    return jnp.concatenate([column] * 4, axis=0) > 0.5 * NOWHERE


def near_row(width):
    return pl.multiple_of((lax.axis_index("gx") % 2) * (3 * width), PLANE)


def side_offsets(sides):
    if sides == 2:
        return [-8 * STEP_Y, 8 * STEP_Y]
    return [(1 - 2 * lax.axis_index("gy")).astype(jnp.float32) * (8 * STEP_Y)]


def pack_kernel(features, cotangent, coords, counts, *refs):
    own_ref, face_ref, place_ref, live_ref, sems = refs
    slots = features.shape[2]
    width = slots * PLANE
    copies = [
        pltpu.make_async_copy(coords.at[0], place_ref, sems.at[0]),
        pltpu.make_async_copy(counts, live_ref, sems.at[1]),
    ]
    for field, ref in enumerate((features, cotangent)):
        planes = own_ref.at[pl.ds(field * 4 * width, 4 * width)].reshape(4, slots, PLANE, C)
        for slot in range(slots):
            copies.append(
                pltpu.make_async_copy(
                    ref.at[0, 0, slot].reshape(4, PLANE, C),
                    planes.at[:, slot],
                    sems.at[len(copies)],
                )
            )
    for copy in copies:
        copy.start()
    for copy in copies:
        copy.wait()
    lane = iota((1, LANES), 1)
    lane_slot = (lane // PLANE) % slots
    position = jnp.zeros((1, LANES), jnp.int32)
    for slot in range(slots):
        position = jnp.where(lane_slot == slot, place_ref[0, slot], position)
    values = [
        position // 16,
        4 * (position // 8 % 2) + lane % PLANE // 4,
        4 * (position % 8) + lane % 4,
        (lane_slot < live_ref[0, 0]).astype(jnp.int32),
    ]
    rows = [v[:, h * C : (h + 1) * C] for h in range(2) for v in values]
    rows.append(jnp.zeros((META - 8, C), jnp.int32))
    meta = jnp.concatenate(rows, axis=0).astype(jnp.float32).astype(jnp.bfloat16)
    own_ref[8 * width :, :] = meta
    at = near_row(width)
    face_ref[:width, :] = own_ref[pl.ds(at, width), :]
    face_ref[width : 2 * width, :] = own_ref[pl.ds(pl.multiple_of(4 * width + at, PLANE), width), :]
    face_ref[2 * width :, :] = meta


class Around:
    def __init__(self, tiles, fars, sides, rows):
        self.tiles, self.fars, self.sides = tiles, fars, sides
        self.rows, self.width = rows, rows // 8

    def order(self, s):
        return [s] + [other for other in range(1 + self.sides) if other != s]

    def odd(self, j):
        return (lax.axis_index("gx") + j) % 2 == 1

    def codes(self, j, s):
        def meta(ref, start):
            return ref[start : start + 8, :]

        def tile_meta(j, o):
            ref, first, thin = self.tiles[j][o]
            return meta(ref, first + (self.rows * 3 // 4 if thin else self.rows))

        order = self.order(s)
        metas = [tile_meta(j, o) for o in order]
        offsets = side_offsets(self.sides)
        offsets = [0.0] + ([-o for o in offsets] if s else offsets)
        befores, afters = [], []
        for o in order:
            near = tile_meta(j ^ 1, o)
            if self.fars is None:
                far = jnp.zeros_like(near)
            else:
                ref, first = self.fars[j][o]
                far = meta(ref, first + 2 * self.width)
            befores.append(jnp.where(self.odd(j), near, far))
            afters.append(jnp.where(self.odd(j), far, near))
        before, after = (
            source_codes(metas + beyond, offsets + [o + step for o in offsets], self.width)
            for beyond, step in ((befores, -2 * STEP_X), (afters, 2 * STEP_X))
        )
        return before, after, target_codes(metas[0], self.width)

    def sources(self, j, s, field):
        def tile(j, o):
            ref, first, thin = self.tiles[j][o]
            return ref, first + field * 4 * self.width, thin and field == 1

        order = self.order(s)
        faces = []
        for o in order:
            far = None
            if self.fars is not None:
                ref, first = self.fars[j][o]
                far = (ref, first + field * self.width, False)
            faces.append((tile(j ^ 1, o), far))
        return [tile(j, o) for o in order], faces, self.odd(j)


def chip_places(refs, sides, rows):
    return [[(ref, s * (rows + META), False) for s in range(1 + sides)] for ref in refs]


def main_kernel(sides, *refs):
    tiles, refs = refs[:2], refs[2:]
    first, second, pre_ref, back_ref, feature_cols, seed_cols = refs
    rows = 2 * pre_ref.shape[0]
    width = rows // 8
    around = Around(chip_places(tiles, sides, rows), None, sides, rows)
    chosen = selectors(*around.codes(0, 0), sides, width)
    fill(feature_cols, *around.sources(0, 0, 0), chosen, width)
    fill(seed_cols, *around.sources(0, 0, 1), chosen, width)
    pre_ref[...] = conv(feature_cols, first, width)
    back_ref[...] = conv_back(seed_cols, second, width)


def layer_kernel(sides, *refs):
    tiles, refs = refs[:2], refs[2:]
    fars, refs = refs[: 1 + sides], refs[1 + sides :]
    first, second, pre_main, back_main = refs[:4]
    both_ref, slim_ref, cross_ref, source_ref, target_ref, pre_ref, back_ref = refs[-7:]
    rows = both_ref.shape[0]
    width = rows // 8
    around = Around(chip_places(tiles, sides, rows), [[(ref, 0) for ref in fars]], sides, rows)
    before, after, target = around.codes(0, 0)
    source_ref[0:1, :] = before
    source_ref[1:2, :] = after
    target_ref[...] = target
    odd = around.odd(0)
    codes = jnp.where(odd, after, before)[:, : 2 * (1 + sides) * width]
    chosen = (codes == target + jnp.where(odd, STEP_X, -STEP_X)).astype(jnp.float32)
    chosen = chosen.astype(jnp.bfloat16)
    nothing = jnp.zeros(((1 + sides) * width, C), jnp.bfloat16)
    at = near_row(width)

    def add(total_ref, main_ref, field, weight):
        pieces = [nothing] + [ref[field * width : (field + 1) * width, :] for ref in fars]
        moved = dot(chosen, jnp.concatenate(pieces, axis=0)).astype(jnp.bfloat16)
        more = sum(weight(shift, moved[shift * width : (shift + 1) * width]) for shift in range(9))
        total_ref[...] = main_ref[...]
        total_ref[pl.ds(at, width), :] = total_ref[pl.ds(at, width), :] + more

    def tap(weight_ref, index):
        return weight_ref[pl.ds(pl.multiple_of(index * C, C), C), :]

    add(
        pre_ref,
        pre_main,
        0,
        lambda shift, cells: dot(cells, tap(first, jnp.where(odd, 18, 0) + shift)),
    )
    add(
        back_ref,
        back_main,
        1,
        lambda shift, cells: dot(cells, tap(second, jnp.where(odd, 8, 26) - shift), ((1,), (1,))),
    )
    pre_first = pre_ref[...]
    live = live_rows(tiles[0][rows : rows + 8, :], width)
    sigmoid = 1.0 / (1.0 + jnp.exp(-pre_first))
    hidden = jnp.where(live, pre_first * sigmoid, 0.0)
    both_ref[: 4 * width, :] = hidden.astype(jnp.bfloat16)
    slope = jnp.where(live, sigmoid * (1.0 + pre_first * (1.0 - sigmoid)), 0.0)
    both_ref[4 * width :, :] = (back_ref[...] * slope).astype(jnp.bfloat16)
    if sides == 1:
        slim(both_ref, slim_ref, lax.axis_index("gy"))
        slim(both_ref, cross_ref, 1 - lax.axis_index("gy"))
    else:
        slim_ref[...] = jnp.zeros(slim_ref.shape, slim_ref.dtype)
        cross_ref[...] = jnp.zeros(cross_ref.shape, cross_ref.dtype)


def join_kernel(count, *refs):
    joined_ref, slim_ref = refs[-2:]
    gather_kernel(count, *refs[:count], joined_ref)
    if count == 2:
        size = slim_ref.shape[0] // 2
        for i in range(2):
            slim(refs[i], slim_ref.at[pl.ds(i * size, size)], lax.axis_index("gy"))
    else:
        slim_ref[...] = jnp.zeros(slim_ref.shape, slim_ref.dtype)


def slim(tile_ref, slim_ref, half):
    rows = tile_ref.shape[0] // (8 * PLANE) * 4 * PLANE
    columns = pl.ds(pl.multiple_of(half * (C // 2), 128), C // 2)
    slim_ref[:rows, :] = tile_ref[:rows, :]
    slim_ref[rows : rows + rows // 2, : C // 2] = tile_ref[rows : rows + rows // 2, columns]
    slim_ref[rows : rows + rows // 2, C // 2 :] = tile_ref[rows + rows // 2 : 2 * rows, columns]
    if slim_ref.shape[0] > rows + rows // 2:
        slim_ref[rows + rows // 2 :, :] = tile_ref[2 * rows :, :]


def gather_kernel(count, *refs):
    packed_ref = refs[-1]
    at = 0
    for ref in refs[:count]:
        packed_ref[at : at + ref.shape[0], :] = ref[...]
        at += ref.shape[0]


def face_kernel(both_ref, *refs):
    face_ref = refs[-1]
    width = both_ref.shape[0] // 8
    at = near_row(width)
    face_ref[:width, :] = both_ref[pl.ds(at, width), :]
    face_ref[width:, :] = both_ref[pl.ds(pl.multiple_of(4 * width + at, PLANE), width), :]


def my_columns(cols):
    if cols == C:
        return slice(None)
    return pl.ds(pl.multiple_of(lax.axis_index("gy") * cols, 128), cols)


def store_terms(keep_ref, send_ref, total_ref):
    core = lax.axis_index("gx") % 2
    pairs, rows = keep_ref.shape[0], keep_ref.shape[1]
    for i in range(pairs):
        keep_at = pl.multiple_of((2 * i + core) * rows, 8)
        send_at = pl.multiple_of((2 * i + 1 - core) * rows, 8)
        keep_ref[i] = total_ref[pl.ds(keep_at, rows), :]
        send_ref[i] = total_ref[pl.ds(send_at, rows), :]


def second_terms_kernel(both_ref, cols_ref, keep_ref, send_ref, total_ref):
    rows = both_ref.shape[0] // 2
    hidden = both_ref[:rows, :].astype(jnp.float32).T.astype(jnp.bfloat16)
    for tap in range(TAPS):
        total_ref[tap * C : (tap + 1) * C, :] = dot(hidden, tap_rows(cols_ref, 26 - tap, rows // 4))
    store_terms(keep_ref, send_ref, total_ref)


def first_terms_kernel(both_ref, cols_ref, keep_ref, send_ref, total_ref):
    rows = both_ref.shape[0] // 2
    grad = both_ref[rows:, :]
    for tap in range(TAPS):
        total_ref[tap * C : (tap + 1) * C, :] = dot(
            tap_rows(cols_ref, tap, rows // 4), grad, ((0,), (0,))
        )
    store_terms(keep_ref, send_ref, total_ref)


def group_cols(around, members, feature_ref, seed_ref):
    columns = my_columns(seed_ref.shape[3])
    for index, (j, s) in enumerate(members):
        chosen = selectors(*around.codes(j, s), around.sides, around.width)
        fill(feature_ref.at[index], *around.sources(j, s, 0), chosen, around.width)
        fill(seed_ref.at[index], *around.sources(j, s, 1), chosen, around.width, columns)


CHIP_MEMBERS = (((0, 0), (0, 1)), ((1, 0), (1, 1)))
OTHER_MEMBERS = ((2, 0), (2, 1), (3, 0), (3, 1))


def chip_cols_kernel(sides, members, *refs):
    tiles, (far, near_far), (feature_ref, seed_ref) = refs[:2], refs[2:4], refs[-2:]
    rows = feature_ref.shape[2] // 6 * 8
    face = rows // 4 + META
    fars = [[(ref, s * face) for s in range(1 + sides)] for ref in (far, near_far)]
    around = Around(chip_places(tiles, sides, rows), fars, sides, rows)
    group_cols(around, members, feature_ref, seed_ref)


def other_cols_kernel(packed, near_packed, _, feature_ref, seed_ref):
    width = feature_ref.shape[2] // 6
    rows = 8 * width
    thin, face = 6 * width + META, 2 * width + META
    tiles = [[(ref, s * thin, True) for s in range(2)] for ref in (packed, near_packed)]
    fars = [[(ref, 2 * thin + s * face) for s in range(2)] for ref in (packed, near_packed)]
    around = Around([None, None] + tiles, [None, None] + fars, 1, rows)
    group_cols(around, OTHER_MEMBERS, feature_ref, seed_ref)


def group_terms(cols_of, fields, first, top, out_refs, total_ref):
    own_ref, send_refs = out_refs[0], out_refs[1:]
    chunk, cols = own_ref.shape[0] // 2, own_ref.shape[1]
    deep = lax.axis_index("gx") // 4
    row = lax.axis_index("gx") % 4
    taps = total_ref.shape[1] // C
    width = fields[0].shape[0] // 4
    starts = [((deep ^ m) * 4 + row) * chunk for m in range(1 + len(send_refs))]

    def rows(tap):
        tap = jnp.minimum(tap, TAPS - 1)
        tap = tap if first else TAPS - 1 - tap
        at = pl.multiple_of(tap // 9 * width, PLANE)
        return jnp.concatenate(
            [cols_of(i, tap % 9, pl.ds(at, 4 * width)) for i in range(len(fields))], axis=0
        )

    operand = jnp.concatenate(fields, axis=0).astype(jnp.float32).T.astype(jnp.bfloat16)
    wanted = [(m, i) for m in range(len(starts)) for i in range(taps)]
    if first:
        for m, i in wanted:
            result = dot(operand, rows(starts[m] // C + i))
            total_ref[m, i * C : (i + 1) * C, :] = result.T
    else:
        step = max(1, C // cols)
        for at in range(0, len(wanted), step):
            part = wanted[at : at + step]
            result = dot(
                operand, jnp.concatenate([rows(starts[m] // C + i) for m, i in part], axis=1)
            )
            for place, (m, i) in enumerate(part):
                total_ref[m, i * C : (i + 1) * C, :] = result[:, place * cols : (place + 1) * cols]
    for m, start in enumerate(starts):
        at = pl.multiple_of(start % C, 16)
        if m == 0:
            own_ref[top : top + chunk, :] = total_ref[m, pl.ds(at, chunk), :]
        else:
            send_refs[m - 1][top : top + chunk, :] = total_ref[m, pl.ds(at, chunk), :].astype(
                jnp.bfloat16
            )


def group_terms_kernel(*refs):
    both, thins, packed, refs = refs[:2], refs[2:4], refs[4], refs[5:]
    groups, refs = refs[:6], refs[6:]
    out_refs, total_ref = refs[:-1], refs[-1]
    rows = both[0].shape[0] // 2
    chunk = out_refs[0].shape[0] // 2
    columns = my_columns(out_refs[0].shape[1])
    thin_rows = thins[0].shape[0]
    both = [(ref, 0) for ref in both]
    both += [(packed, 2 * thin_rows), (packed, 2 * thin_rows + 2 * rows)]
    thins = [(ref, 0) for ref in thins] + [(packed, 0), (packed, thin_rows)]

    def group(part, tile, shift, at):
        place, index = (tile // 2, tile % 2) if tile < 4 else (2, tile - 4)
        return groups[part + 2 * place][index, shift, at, :]

    features_of, seeds_of = functools.partial(group, 0), functools.partial(group, 1)
    grads = [ref[at + rows : at + 2 * rows, columns] for ref, at in both]
    for ref, at in thins:
        halves = ref[at + rows : at + rows + rows // 2, :]
        grads.append(jnp.concatenate([halves[:, : C // 2], halves[:, C // 2 :]], axis=0))
    hiddens = [ref[at : at + rows, :] for ref, at in (*both, *thins)]
    group_terms(features_of, grads, True, 0, out_refs, total_ref)
    group_terms(seeds_of, hiddens, False, chunk, out_refs, total_ref)


def last_kernel(sides, *refs):
    own_ref, refs = refs[0], refs[1:]
    tiles, refs = refs[: 1 + sides], refs[1 + sides :]
    count = 1 if sides == 1 else 1 + sides
    nears, refs = refs[:count], refs[count:]
    fars, refs = refs[: 1 + sides], refs[1 + sides :]
    first, second, source_ref, target_ref, _, output_ref, input_ref = refs[:7]
    hidden_cols_ref, grad_cols_ref = refs[7:]
    width = tiles[0].shape[0] // 8
    slots = output_ref.shape[0]
    chosen = selectors(source_ref[0:1, :], source_ref[1:2, :], target_ref[...], sides, width)
    live = live_rows(own_ref[8 * width : 8 * width + 8, :], width)
    rows = tiles[0].shape[0]
    if sides == 1:
        near_at = nears[0].shape[0] - 2 * rows
        nears = [(nears[0], near_at, False), (nears[0], near_at + rows, False)]
    else:
        nears = [(ref, 0, False) for ref in nears]
    around = Around(
        [[(ref, 0, False) for ref in tiles], nears],
        [[(ref, 0) for ref in fars]],
        sides,
        rows,
    )

    def put(ref, total):
        total = jnp.where(live, total, 0.0)
        for x in range(4):
            for slot in range(slots):
                start = x * width + slot * PLANE
                ref[slot, x * PLANE : (x + 1) * PLANE, :] = total[start : start + PLANE]

    fill(hidden_cols_ref, *around.sources(0, 0, 0), chosen, width)
    fill(grad_cols_ref, *around.sources(0, 0, 1), chosen, width)
    put(output_ref, conv(hidden_cols_ref, second, width))
    put(input_ref, conv_back(grad_cols_ref, first, width))


def swap(cells, axis, bit):
    return lax.ppermute(cells, axis, [(i, i ^ bit) for i in range(lax.axis_size(axis))])


def side_steps(count):
    if count == 2:
        return [[(0, 1), (1, 0)]]
    ends = count - 1
    return [[(i, i + 1) for i in range(ends)], [(i + 1, i) for i in range(ends)]]


def far_steps(count):
    pairs = [(i, i + 1) for i in range(1, count - 1, 2)]
    return pairs + [(b, a) for a, b in pairs]


def from_sides(cells):
    return [lax.ppermute(cells, "gy", step) for step in side_steps(lax.axis_size("gy"))]


def across(face, gx_steps, gy_steps):
    gy = lax.axis_size("gy")
    return lax.ppermute(
        face, ("gx", "gy"), [(a * gy + c, b * gy + d) for a, b in gx_steps for c, d in gy_steps]
    )


def from_far(face):
    far = lax.ppermute(face, "gx", far_steps(lax.axis_size("gx")))
    return [far, *from_sides(far)]


def piece(cells, index, axis):
    return lax.dynamic_index_in_dim(cells, index, axis, keepdims=False)


def per_device(features, block_coords, block_counts, first_weight, second_weight, cotangent):
    gx, gy = lax.axis_size("gx"), lax.axis_size("gy")
    iy, ix = lax.axis_index("gy"), lax.axis_index("gx")
    slots = features.shape[2]
    width = slots * PLANE
    rows = 8 * width
    half, deep = ix // 2 % 2, ix // 4
    deeps = gx // 4
    grouped = gy == 2
    sides = 1 if grouped else 2
    chunk = TAPS * C // gx

    def shape(dims, kind=jnp.bfloat16):
        return jax.ShapeDtypeStruct(dims, kind)

    def call(kernel, name, outs, args, mib, micros, scratch=(), specs=None):
        return pl.pallas_call(
            kernel,
            out_shape=outs,
            in_specs=specs or [VMEM] * len(args),
            out_specs=(VMEM,) * len(outs),
            scratch_shapes=list(scratch),
            compiler_params=params(mib),
            cost_estimate=pl.CostEstimate(
                flops=int(micros * 1.1e9), bytes_accessed=2**20, transcendentals=0
            ),
            name=name,
        )(*args)

    own, face = call(
        pack_kernel,
        "pack",
        (
            shape((rows + META, C)),
            shape((2 * width + META, C)),
        ),
        (features, cotangent, block_coords, block_counts),
        60,
        3,
        [
            pltpu.SMEM((1, slots), jnp.int32),
            pltpu.SMEM((1, 1), jnp.int32),
            pltpu.SemaphoreType.DMA((2 + 2 * slots,)),
        ],
        [HBM] * 4,
    )
    side = from_sides(own)
    field = (4 * width, C)
    fars = from_far(face)
    def gathered(name, cells, after, micros=0.5):
        return call(
            functools.partial(gather_kernel, len(cells)),
            name,
            (shape((sum(part.shape[0] for part in cells), C)),),
            (*cells, *after),
            8,
            micros,
            specs=[VMEM] * len(cells) + [ANY] * len(after),
        )[0]

    parts = [own, *side]
    chip, thins = call(
        functools.partial(join_kernel, len(parts)),
        "join",
        (
            shape((len(parts) * (rows + META), C)),
            shape((2 * (6 * width + META), C)),
        ),
        (*parts, fars[0]),
        8,
        3,
        specs=[VMEM] * len(parts) + [ANY],
    )
    chip = [chip, swap(chip, "gx", 1)]
    columns = shape((9, 6 * width, C))
    main = call(
        functools.partial(main_kernel, sides),
        "first_convs",
        (shape(field, jnp.float32),) * 2,
        (*chip, first_weight, second_weight),
        12,
        3,
        [pltpu.VMEM(columns.shape, jnp.bfloat16)] * 2,
    )
    both, thin, cross, source, target = call(
        functools.partial(layer_kernel, sides),
        "layer",
        (
            shape((rows, C)),
            shape((6 * width, C)),
            shape((6 * width, C)),
            shape((2, LANES), jnp.float32),
            shape((9 * width, 1), jnp.float32),
        ),
        (*chip, *fars, first_weight, second_weight, *main),
        8,
        1,
        [pltpu.VMEM(field, jnp.float32)] * 2,
    )
    both_side = from_sides(both)

    def late_far(after):
        (late_face,) = call(
            face_kernel,
            "face",
            (shape((2 * width, C)),),
            (both, *after),
            8,
            0.3,
            specs=[VMEM] + [ANY] * len(after),
        )
        return from_far(late_face)

    grad_scale = 1.0 / math.sqrt(64 * slots * gx * gy)

    def over_z(own_part, sent):
        got = [swap(cells, "gx", 4 * m) for m, cells in enumerate(sent, 1)]
        return (own_part + sum(cells.astype(jnp.float32) for cells in got)) * grad_scale

    if grouped:
        cols = C // 2

        def group_shapes(count):
            return shape((count, *columns.shape)), shape((count, *columns.shape[:2], cols))

        far_faces = gathered("far_faces", fars, main[:1])
        near_faces = swap(far_faces, "gx", 1)
        beside = [swap(thins, "gx", 2), swap(far_faces, "gx", 2)]
        early = gathered("gather_early", beside, (both,))
        near_early = swap(early, "gx", 1)
        chip_cols = [
            call(
                functools.partial(chip_cols_kernel, 1, members),
                "chip_cols",
                group_shapes(len(members)),
                (*chip, far_faces, near_faces, *after),
                8,
                1.6,
                specs=[VMEM] * 4 + [ANY] * len(after),
            )
            for members, after in zip(CHIP_MEMBERS, ((), beside))
        ]
        late_fars = late_far(chip_cols[0][1:])
        thin_other = swap(thin, "gx", 2)
        cross_other = across(cross, [(i, i ^ 2) for i in range(gx)], side_steps(gy)[0])
        packed = gathered(
            "gather_late",
            (thin_other, cross_other, both, both_side[0]),
            (chip_cols[1][1], late_fars[0]),
        )
        near_packed = swap(packed, "gx", 1)
        nears = [near_packed]
        other_features, other_seeds = call(
            other_cols_kernel,
            "other_cols",
            group_shapes(len(OTHER_MEMBERS)),
            (early, near_early, packed),
            8,
            3,
            specs=[VMEM] * 2 + [ANY],
        )
        members = [both, both_side[0], thin_other, cross_other, near_packed]
        taps = 2 + (chunk - 2) // C
        own_part, *sent = call(
            group_terms_kernel,
            "group_terms",
            (
                shape((2 * chunk, cols), jnp.float32),
                *[shape((2 * chunk, cols))] * (deeps - 1),
            ),
            (
                *members,
                *chip_cols[0],
                *chip_cols[1],
                other_features,
                other_seeds,
            ),
            12,
            3.5,
            [pltpu.VMEM((deeps, taps * C, cols), jnp.float32)],
        )
        token = sent[0]
        grads = over_z(own_part, sent)
        first_grad, second_grad = grads[:chunk], grads[chunk:]
    else:
        far_faces = jnp.concatenate(fars, axis=0)
        nears = [swap(cells, "gx", 1) for cells in (both, *both_side)]
        late_fars = late_far(())

        def summed(kernel, name, cells):
            keep, send = call(
                kernel,
                name,
                (
                    shape((gx // 2, chunk, C), jnp.float32),
                    shape((gx // 2, chunk, C), jnp.float32),
                ),
                (both, cells),
                24,
                4,
                [pltpu.VMEM((TAPS * C, C), jnp.float32)],
            )
            keep = keep.reshape(deeps, 2, chunk, C)
            got = swap(send, "gx", 1).reshape(keep.shape)

            def part(i):
                return piece(keep, i, 1) + piece(got, i, 1)

            total = part(half) + swap(part(1 - half).astype(jnp.bfloat16), "gx", 2).astype(
                jnp.float32
            )
            total = total.reshape(deeps, chunk, gy, C // gy)
            total = piece(total, iy, 2) + sum(
                swap(piece(total, iy ^ m, 2).astype(jnp.bfloat16), "gy", m).astype(jnp.float32)
                for m in range(1, gy)
            )
            total = over_z(
                piece(total, deep, 0),
                [piece(total, deep ^ m, 0).astype(jnp.bfloat16) for m in range(1, deeps)],
            )
            return total, send

        feature_cols, seed_cols = call(
            functools.partial(chip_cols_kernel, sides, ((0, 0),)),
            "own_cols",
            (shape((1, *columns.shape)),) * 2,
            (*chip, far_faces, far_faces),
            8,
            1,
        )
        feature_cols, seed_cols = feature_cols[0], seed_cols[0]
        second_grad, token = summed(second_terms_kernel, "second_terms", seed_cols)
        first_grad, _ = summed(first_terms_kernel, "first_terms", feature_cols)

    late = [chip[0], both, *both_side, *nears, *late_fars]
    result = shape((slots, 64, C), jnp.float32)
    output, input_grad = call(
        functools.partial(last_kernel, sides),
        "last_layer",
        (result, result),
        (*late, first_weight, second_weight, source, target, token),
        12,
        0.1,
        [pltpu.VMEM(columns.shape, jnp.bfloat16)] * 2,
        [VMEM] * (len(late) + 4) + [ANY],
    )
    return (
        output.reshape(features.shape),
        input_grad.reshape(features.shape),
        first_grad,
        second_grad,
    )


def solution(mesh):
    placed = (
        P("gx", "gy", None, None, None),
        P("gx", "gy", None),
        P("gx", "gy"),
        P(),
        P(),
        P("gx", "gy", None, None, None),
    )
    return jax.shard_map(
        per_device,
        mesh=mesh,
        in_specs=placed,
        out_specs=(
            P("gx", "gy", None, None, None),
            P("gx", "gy", None, None, None),
            P("gx", "gy"),
            P("gx", "gy"),
        ),
        check_vma=False,
    )
```

```python
import functools
import math

import jax
import jax.numpy as jnp
from jax import lax
from jax.experimental import pallas as pl
from jax.experimental.pallas import tpu as pltpu
from jax.sharding import PartitionSpec as P

C = 256
TAPS = 27
PLANE = 16
META = 16
LANES = 512
STEP_Y = 64.0
STEP_X = 4096.0
NOWHERE = -1.0e7
VMEM = pl.BlockSpec(memory_space=pltpu.MemorySpace.VMEM)
HBM = pl.BlockSpec(memory_space=pltpu.MemorySpace.HBM)
ANY = pl.BlockSpec(memory_space=pl.ANY)


def params(mib):
    return pltpu.CompilerParams(vmem_limit_bytes=mib * 2**20)


def dot(lhs, rhs, dims=((1,), (0,))):
    return lax.dot_general(lhs, rhs, (dims, ((), ())), preferred_element_type=jnp.float32)


def iota(shape, dim):
    return lax.broadcasted_iota(jnp.int32, shape, dim)


def place_codes(meta, offset, absent=NOWHERE):
    rows = meta.astype(jnp.float32)
    parts = []
    for half in range(2):
        x, y, z, live = (rows[4 * half + i : 4 * half + i + 1] for i in range(4))
        parts.append(jnp.where(live > 0.5, x * STEP_X + y * STEP_Y + z + offset, absent))
    return jnp.concatenate(parts, axis=1)


def source_codes(metas, offsets, width):
    lane = iota((1, LANES), 1)
    total = jnp.full((1, LANES), NOWHERE, jnp.float32)
    for place, (meta, offset) in enumerate(zip(metas, offsets)):
        inside = (lane >= place * width) & (lane < (place + 1) * width)
        total = jnp.where(inside, place_codes(meta, offset), total)
    return total


def target_codes(meta, width):
    codes = place_codes(meta, 0.0, 3 * NOWHERE)
    own = iota((width, LANES), 0) == iota((width, LANES), 1)
    column = jnp.sum(jnp.where(own, codes, 0.0), axis=1, keepdims=True)
    return jnp.concatenate(
        [column + ((s // 3 - 1) * STEP_Y + (s % 3 - 1)) for s in range(9)], axis=0
    )


def selectors(before, after, target, sides, width):
    middle = (1 + sides) * width
    return tuple(
        (codes == target + step).astype(jnp.float32).astype(jnp.bfloat16)
        for codes, step in (
            (before[:, : 2 * middle], -STEP_X),
            (before[:, :middle], 0.0),
            (after[:, : 2 * middle], STEP_X),
        )
    )


def fill(cols_ref, tiles, faces, odd, chosen, width, columns=slice(None)):
    def load(source, plane):
        ref, first, paired = source[:3]
        if paired:
            at = first + plane % 2 * width
            return ref[at : at + width, plane // 2 * (C // 2) : (plane // 2 + 1) * (C // 2)]
        return ref[first + plane * width : first + (plane + 1) * width, columns]

    for plane in range(6):
        if plane in (0, 5):
            start = 3 if plane == 0 else 0
            pieces = [load(tile, start) for tile in tiles]
            for near, far in faces:
                if far is None:
                    pieces.append(load(near, start))
                    continue
                near, far = load(near, start), load(far, far[3])
                pieces.append(jnp.where(odd, near, far) if plane == 0 else jnp.where(odd, far, near))
        else:
            pieces = [load(tile, plane - 1) for tile in tiles]
        select = chosen[0 if plane == 0 else 2 if plane == 5 else 1]
        moved = dot(select, jnp.concatenate(pieces, axis=0)).astype(jnp.bfloat16)
        for shift in range(9):
            cols_ref[shift, plane * width : (plane + 1) * width, :] = moved[
                shift * width : (shift + 1) * width
            ]


def tap_rows(cols_ref, tap, width, columns=slice(None)):
    start = tap // 9 * width
    return cols_ref[tap % 9, start : start + 4 * width, columns]


def conv(cols_ref, weight_ref, width):
    total = None
    for tap in range(TAPS):
        term = dot(tap_rows(cols_ref, tap, width), weight_ref[tap * C : (tap + 1) * C, :])
        total = term if total is None else total + term
    return total


def conv_back(cols_ref, weight_ref, width):
    total = None
    for tap in range(TAPS):
        weight = weight_ref[(26 - tap) * C : (27 - tap) * C, :]
        term = dot(tap_rows(cols_ref, tap, width), weight, ((1,), (1,)))
        total = term if total is None else total + term
    return total


def live_rows(meta, width):
    codes = place_codes(meta, 0.0)
    own = iota((width, LANES), 0) == iota((width, LANES), 1)
    column = jnp.sum(jnp.where(own, codes, 0.0), axis=1, keepdims=True)
    return jnp.concatenate([column] * 4, axis=0) > 0.5 * NOWHERE


def near_row(width):
    return pl.multiple_of((lax.axis_index("gx") % 2) * (3 * width), PLANE)


def side_offsets(sides):
    if sides == 2:
        return [-8 * STEP_Y, 8 * STEP_Y]
    return [(1 - 2 * lax.axis_index("gy")).astype(jnp.float32) * (8 * STEP_Y)]


def pack_kernel(features, cotangent, coords, counts, *refs):
    own_ref, face_ref, place_ref, live_ref, sems = refs
    slots = features.shape[2]
    width = slots * PLANE
    copies = [
        pltpu.make_async_copy(coords.at[0], place_ref, sems.at[0]),
        pltpu.make_async_copy(counts, live_ref, sems.at[1]),
    ]
    for field, ref in enumerate((features, cotangent)):
        planes = own_ref.at[pl.ds(field * 4 * width, 4 * width)].reshape(4, slots, PLANE, C)
        for slot in range(slots):
            copies.append(
                pltpu.make_async_copy(
                    ref.at[0, 0, slot].reshape(4, PLANE, C),
                    planes.at[:, slot],
                    sems.at[len(copies)],
                )
            )
    for copy in copies:
        copy.start()
    for copy in copies:
        copy.wait()
    lane = iota((1, LANES), 1)
    lane_slot = (lane // PLANE) % slots
    position = jnp.zeros((1, LANES), jnp.int32)
    for slot in range(slots):
        position = jnp.where(lane_slot == slot, place_ref[0, slot], position)
    values = [
        position // 16,
        4 * (position // 8 % 2) + lane % PLANE // 4,
        4 * (position % 8) + lane % 4,
        (lane_slot < live_ref[0, 0]).astype(jnp.int32),
    ]
    rows = [v[:, h * C : (h + 1) * C] for h in range(2) for v in values]
    rows.append(jnp.zeros((META - 8, C), jnp.int32))
    meta = jnp.concatenate(rows, axis=0).astype(jnp.float32).astype(jnp.bfloat16)
    own_ref[8 * width :, :] = meta
    at = near_row(width)
    face_ref[:width, :] = own_ref[pl.ds(at, width), :]
    face_ref[width : 2 * width, :] = own_ref[pl.ds(pl.multiple_of(4 * width + at, PLANE), width), :]
    face_ref[2 * width :, :] = meta


class Around:
    def __init__(self, tiles, fars, sides, rows):
        self.tiles, self.fars, self.sides = tiles, fars, sides
        self.rows, self.width = rows, rows // 8

    def order(self, s):
        return [s] + [other for other in range(1 + self.sides) if other != s]

    def odd(self, j):
        return (lax.axis_index("gx") + j) % 2 == 1

    def codes(self, j, s):
        def meta(ref, start):
            return ref[start : start + 8, :]

        def tile_meta(j, o):
            ref, first, thin = self.tiles[j][o]
            return meta(ref, first + (self.rows * 3 // 4 if thin else self.rows))

        order = self.order(s)
        metas = [tile_meta(j, o) for o in order]
        offsets = side_offsets(self.sides)
        offsets = [0.0] + ([-o for o in offsets] if s else offsets)
        befores, afters = [], []
        for o in order:
            near = tile_meta(j ^ 1, o)
            if self.fars is None:
                far = jnp.zeros_like(near)
            else:
                ref, first, *side = self.fars[j][o]
                places = 3 * self.width + side[0] * META if side else 2 * self.width
                far = meta(ref, first + places)
            befores.append(jnp.where(self.odd(j), near, far))
            afters.append(jnp.where(self.odd(j), far, near))
        before, after = (
            source_codes(metas + beyond, offsets + [o + step for o in offsets], self.width)
            for beyond, step in ((befores, -2 * STEP_X), (afters, 2 * STEP_X))
        )
        return before, after, target_codes(metas[0], self.width)

    def sources(self, j, s, field):
        def tile(j, o):
            ref, first, thin = self.tiles[j][o]
            return ref, first + field * 4 * self.width, thin and field == 1

        order = self.order(s)
        faces = []
        for o in order:
            far = None
            if self.fars is not None:
                ref, first, *side = self.fars[j][o]
                far = (ref, first + field * self.width, False, 0)
                if side and field:
                    far = (ref, first + 2 * self.width, True, 2 * side[0])
                elif side:
                    far = (ref, first + side[0] * self.width, False, 0)
            faces.append((tile(j ^ 1, o), far))
        return [tile(j, o) for o in order], faces, self.odd(j)


def chip_places(refs, sides, rows):
    return [[(ref, s * (rows + META), False) for s in range(1 + sides)] for ref in refs]


def main_kernel(sides, *refs):
    tiles, refs = refs[:2], refs[2:]
    first, second, pre_ref, back_ref, feature_cols, seed_cols = refs
    rows = 2 * pre_ref.shape[0]
    width = rows // 8
    around = Around(chip_places(tiles, sides, rows), None, sides, rows)
    chosen = selectors(*around.codes(0, 0), sides, width)
    fill(feature_cols, *around.sources(0, 0, 0), chosen, width)
    fill(seed_cols, *around.sources(0, 0, 1), chosen, width)
    pre_ref[...] = conv(feature_cols, first, width)
    back_ref[...] = conv_back(seed_cols, second, width)


def layer_kernel(sides, *refs):
    tiles, refs = refs[:2], refs[2:]
    fars, refs = refs[: 1 + sides], refs[1 + sides :]
    first, second, pre_main, back_main = refs[:4]
    both_ref, slim_ref, cross_ref, source_ref, target_ref, pre_ref, back_ref = refs[-7:]
    rows = both_ref.shape[0]
    width = rows // 8
    around = Around(chip_places(tiles, sides, rows), [[(ref, 0) for ref in fars]], sides, rows)
    before, after, target = around.codes(0, 0)
    source_ref[0:1, :] = before
    source_ref[1:2, :] = after
    target_ref[...] = target
    odd = around.odd(0)
    codes = jnp.where(odd, after, before)[:, : 2 * (1 + sides) * width]
    chosen = (codes == target + jnp.where(odd, STEP_X, -STEP_X)).astype(jnp.float32)
    chosen = chosen.astype(jnp.bfloat16)
    nothing = jnp.zeros(((1 + sides) * width, C), jnp.bfloat16)
    at = near_row(width)

    def add(total_ref, main_ref, field, weight):
        pieces = [nothing] + [ref[field * width : (field + 1) * width, :] for ref in fars]
        moved = dot(chosen, jnp.concatenate(pieces, axis=0)).astype(jnp.bfloat16)
        more = sum(weight(shift, moved[shift * width : (shift + 1) * width]) for shift in range(9))
        total_ref[...] = main_ref[...]
        total_ref[pl.ds(at, width), :] = total_ref[pl.ds(at, width), :] + more

    def tap(weight_ref, index):
        return weight_ref[pl.ds(pl.multiple_of(index * C, C), C), :]

    add(
        pre_ref,
        pre_main,
        0,
        lambda shift, cells: dot(cells, tap(first, jnp.where(odd, 18, 0) + shift)),
    )
    add(
        back_ref,
        back_main,
        1,
        lambda shift, cells: dot(cells, tap(second, jnp.where(odd, 8, 26) - shift), ((1,), (1,))),
    )
    pre_first = pre_ref[...]
    live = live_rows(tiles[0][rows : rows + 8, :], width)
    sigmoid = 1.0 / (1.0 + jnp.exp(-pre_first))
    hidden = jnp.where(live, pre_first * sigmoid, 0.0)
    both_ref[: 4 * width, :] = hidden.astype(jnp.bfloat16)
    slope = jnp.where(live, sigmoid * (1.0 + pre_first * (1.0 - sigmoid)), 0.0)
    both_ref[4 * width :, :] = (back_ref[...] * slope).astype(jnp.bfloat16)
    if sides == 1:
        slim(both_ref, slim_ref, lax.axis_index("gy"))
        slim(both_ref, cross_ref, 1 - lax.axis_index("gy"))
    else:
        slim_ref[...] = jnp.zeros(slim_ref.shape, slim_ref.dtype)
        cross_ref[...] = jnp.zeros(cross_ref.shape, cross_ref.dtype)


def join_kernel(count, *refs):
    joined_ref, slim_ref = refs[-2:]
    gather_kernel(count, *refs[:count], joined_ref)
    if count == 2:
        size = slim_ref.shape[0] // 2
        for i in range(2):
            slim(refs[i], slim_ref.at[pl.ds(i * size, size)], lax.axis_index("gy"))
    else:
        slim_ref[...] = jnp.zeros(slim_ref.shape, slim_ref.dtype)


def slim(tile_ref, slim_ref, half):
    rows = tile_ref.shape[0] // (8 * PLANE) * 4 * PLANE
    columns = pl.ds(pl.multiple_of(half * (C // 2), 128), C // 2)
    slim_ref[:rows, :] = tile_ref[:rows, :]
    slim_ref[rows : rows + rows // 2, : C // 2] = tile_ref[rows : rows + rows // 2, columns]
    slim_ref[rows : rows + rows // 2, C // 2 :] = tile_ref[rows + rows // 2 : 2 * rows, columns]
    if slim_ref.shape[0] > rows + rows // 2:
        slim_ref[rows + rows // 2 :, :] = tile_ref[2 * rows :, :]


def slim_faces_kernel(far, side_far, _, slim_ref):
    width = (far.shape[0] - META) // 2
    columns = my_columns(C // 2)
    for s, ref in enumerate((far, side_far)):
        slim_ref[s * width : (s + 1) * width, :] = ref[:width, :]
        slim_ref[2 * width : 3 * width, s * (C // 2) : (s + 1) * (C // 2)] = ref[
            width : 2 * width, columns
        ]
        at = 3 * width + s * META
        slim_ref[at : at + META, :] = ref[2 * width :, :]


def gather_kernel(count, *refs):
    packed_ref = refs[-1]
    at = 0
    for ref in refs[:count]:
        packed_ref[at : at + ref.shape[0], :] = ref[...]
        at += ref.shape[0]


def face_kernel(both_ref, *refs):
    face_ref = refs[-1]
    width = both_ref.shape[0] // 8
    at = near_row(width)
    face_ref[:width, :] = both_ref[pl.ds(at, width), :]
    face_ref[width:, :] = both_ref[pl.ds(pl.multiple_of(4 * width + at, PLANE), width), :]


def my_columns(cols):
    if cols == C:
        return slice(None)
    return pl.ds(pl.multiple_of(lax.axis_index("gy") * cols, 128), cols)


def store_terms(keep_ref, send_ref, total_ref):
    core = lax.axis_index("gx") % 2
    pairs, rows = keep_ref.shape[0], keep_ref.shape[1]
    for i in range(pairs):
        keep_at = pl.multiple_of((2 * i + core) * rows, 8)
        send_at = pl.multiple_of((2 * i + 1 - core) * rows, 8)
        keep_ref[i] = total_ref[pl.ds(keep_at, rows), :]
        send_ref[i] = total_ref[pl.ds(send_at, rows), :]


def second_terms_kernel(both_ref, cols_ref, keep_ref, send_ref, total_ref):
    rows = both_ref.shape[0] // 2
    hidden = both_ref[:rows, :].astype(jnp.float32).T.astype(jnp.bfloat16)
    for tap in range(TAPS):
        total_ref[tap * C : (tap + 1) * C, :] = dot(hidden, tap_rows(cols_ref, 26 - tap, rows // 4))
    store_terms(keep_ref, send_ref, total_ref)


def first_terms_kernel(both_ref, cols_ref, keep_ref, send_ref, total_ref):
    rows = both_ref.shape[0] // 2
    grad = both_ref[rows:, :]
    for tap in range(TAPS):
        total_ref[tap * C : (tap + 1) * C, :] = dot(
            tap_rows(cols_ref, tap, rows // 4), grad, ((0,), (0,))
        )
    store_terms(keep_ref, send_ref, total_ref)


def group_cols(around, members, feature_ref, seed_ref):
    columns = my_columns(seed_ref.shape[3])
    for index, (j, s) in enumerate(members):
        chosen = selectors(*around.codes(j, s), around.sides, around.width)
        fill(feature_ref.at[index], *around.sources(j, s, 0), chosen, around.width)
        fill(seed_ref.at[index], *around.sources(j, s, 1), chosen, around.width, columns)


CHIP_MEMBERS = (((0, 0), (0, 1)), ((1, 0), (1, 1)))
OTHER_MEMBERS = ((2, 0), (2, 1), (3, 0), (3, 1))


def chip_cols_kernel(sides, members, *refs):
    tiles, (far, near_far), (feature_ref, seed_ref) = refs[:2], refs[2:4], refs[-2:]
    rows = feature_ref.shape[2] // 6 * 8
    face = rows // 4 + META
    fars = [[(ref, s * face) for s in range(1 + sides)] for ref in (far, near_far)]
    around = Around(chip_places(tiles, sides, rows), fars, sides, rows)
    group_cols(around, members, feature_ref, seed_ref)


def other_cols_kernel(packed, near_packed, _, feature_ref, seed_ref):
    width = feature_ref.shape[2] // 6
    rows = 8 * width
    thin = 6 * width + META
    tiles = [[(ref, s * thin, True) for s in range(2)] for ref in (packed, near_packed)]
    fars = [[(ref, 2 * thin, s) for s in range(2)] for ref in (packed, near_packed)]
    around = Around([None, None] + tiles, [None, None] + fars, 1, rows)
    group_cols(around, OTHER_MEMBERS, feature_ref, seed_ref)


def group_terms(cols_of, fields, first, top, out_refs, total_ref):
    own_ref, send_refs = out_refs[0], out_refs[1:]
    chunk, cols = own_ref.shape[0] // 2, own_ref.shape[1]
    deep = lax.axis_index("gx") // 4
    row = lax.axis_index("gx") % 4
    taps = total_ref.shape[1] // C
    width = fields[0].shape[0] // 4
    starts = [((deep ^ m) * 4 + row) * chunk for m in range(1 + len(send_refs))]

    def rows(tap):
        tap = jnp.minimum(tap, TAPS - 1)
        tap = tap if first else TAPS - 1 - tap
        at = pl.multiple_of(tap // 9 * width, PLANE)
        return jnp.concatenate(
            [cols_of(i, tap % 9, pl.ds(at, 4 * width)) for i in range(len(fields))], axis=0
        )

    operand = jnp.concatenate(fields, axis=0).astype(jnp.float32).T.astype(jnp.bfloat16)
    wanted = [(m, i) for m in range(len(starts)) for i in range(taps)]
    if first:
        for m, i in wanted:
            result = dot(operand, rows(starts[m] // C + i))
            total_ref[m, i * C : (i + 1) * C, :] = result.T
    else:
        step = max(1, C // cols)
        for at in range(0, len(wanted), step):
            part = wanted[at : at + step]
            result = dot(
                operand, jnp.concatenate([rows(starts[m] // C + i) for m, i in part], axis=1)
            )
            for place, (m, i) in enumerate(part):
                total_ref[m, i * C : (i + 1) * C, :] = result[:, place * cols : (place + 1) * cols]
    for m, start in enumerate(starts):
        at = pl.multiple_of(start % C, 16)
        if m == 0:
            own_ref[top : top + chunk, :] = total_ref[m, pl.ds(at, chunk), :]
        else:
            send_refs[m - 1][top : top + chunk, :] = total_ref[m, pl.ds(at, chunk), :].astype(
                jnp.bfloat16
            )


def group_terms_kernel(*refs):
    both, thins, packed, refs = refs[:2], refs[2:4], refs[4], refs[5:]
    groups, refs = refs[:6], refs[6:]
    out_refs, total_ref = refs[:-1], refs[-1]
    rows = both[0].shape[0] // 2
    chunk = out_refs[0].shape[0] // 2
    columns = my_columns(out_refs[0].shape[1])
    thin_rows = thins[0].shape[0]
    both = [(ref, 0) for ref in both]
    both += [(packed, 2 * thin_rows), (packed, 2 * thin_rows + 2 * rows)]
    thins = [(ref, 0) for ref in thins] + [(packed, 0), (packed, thin_rows)]

    def group(part, tile, shift, at):
        place, index = (tile // 2, tile % 2) if tile < 4 else (2, tile - 4)
        return groups[part + 2 * place][index, shift, at, :]

    features_of, seeds_of = functools.partial(group, 0), functools.partial(group, 1)
    grads = [ref[at + rows : at + 2 * rows, columns] for ref, at in both]
    for ref, at in thins:
        halves = ref[at + rows : at + rows + rows // 2, :]
        grads.append(jnp.concatenate([halves[:, : C // 2], halves[:, C // 2 :]], axis=0))
    hiddens = [ref[at : at + rows, :] for ref, at in (*both, *thins)]
    group_terms(features_of, grads, True, 0, out_refs, total_ref)
    group_terms(seeds_of, hiddens, False, chunk, out_refs, total_ref)


def last_kernel(sides, *refs):
    own_ref, refs = refs[0], refs[1:]
    tiles, refs = refs[: 1 + sides], refs[1 + sides :]
    count = 1 if sides == 1 else 1 + sides
    nears, refs = refs[:count], refs[count:]
    fars, refs = refs[: 1 + sides], refs[1 + sides :]
    first, second, source_ref, target_ref, _, output_ref, input_ref = refs[:7]
    hidden_cols_ref, grad_cols_ref = refs[7:]
    width = tiles[0].shape[0] // 8
    slots = output_ref.shape[0]
    chosen = selectors(source_ref[0:1, :], source_ref[1:2, :], target_ref[...], sides, width)
    live = live_rows(own_ref[8 * width : 8 * width + 8, :], width)
    rows = tiles[0].shape[0]
    if sides == 1:
        near_at = nears[0].shape[0] - 2 * rows
        nears = [(nears[0], near_at, False), (nears[0], near_at + rows, False)]
    else:
        nears = [(ref, 0, False) for ref in nears]
    around = Around(
        [[(ref, 0, False) for ref in tiles], nears],
        [[(ref, 0) for ref in fars]],
        sides,
        rows,
    )

    def put(ref, total):
        total = jnp.where(live, total, 0.0)
        for x in range(4):
            for slot in range(slots):
                start = x * width + slot * PLANE
                ref[slot, x * PLANE : (x + 1) * PLANE, :] = total[start : start + PLANE]

    fill(hidden_cols_ref, *around.sources(0, 0, 0), chosen, width)
    fill(grad_cols_ref, *around.sources(0, 0, 1), chosen, width)
    put(output_ref, conv(hidden_cols_ref, second, width))
    put(input_ref, conv_back(grad_cols_ref, first, width))


def swap(cells, axis, bit):
    return lax.ppermute(cells, axis, [(i, i ^ bit) for i in range(lax.axis_size(axis))])


def side_steps(count):
    if count == 2:
        return [[(0, 1), (1, 0)]]
    ends = count - 1
    return [[(i, i + 1) for i in range(ends)], [(i + 1, i) for i in range(ends)]]


def far_steps(count):
    pairs = [(i, i + 1) for i in range(1, count - 1, 2)]
    return pairs + [(b, a) for a, b in pairs]


def from_sides(cells):
    return [lax.ppermute(cells, "gy", step) for step in side_steps(lax.axis_size("gy"))]


def across(face, gx_steps, gy_steps):
    gy = lax.axis_size("gy")
    return lax.ppermute(
        face, ("gx", "gy"), [(a * gy + c, b * gy + d) for a, b in gx_steps for c, d in gy_steps]
    )


def from_far(face):
    far = lax.ppermute(face, "gx", far_steps(lax.axis_size("gx")))
    return [far, *from_sides(far)]


def piece(cells, index, axis):
    return lax.dynamic_index_in_dim(cells, index, axis, keepdims=False)


def per_device(features, block_coords, block_counts, first_weight, second_weight, cotangent):
    gx, gy = lax.axis_size("gx"), lax.axis_size("gy")
    iy, ix = lax.axis_index("gy"), lax.axis_index("gx")
    slots = features.shape[2]
    width = slots * PLANE
    rows = 8 * width
    half, deep = ix // 2 % 2, ix // 4
    deeps = gx // 4
    grouped = gy == 2
    sides = 1 if grouped else 2
    chunk = TAPS * C // gx

    def shape(dims, kind=jnp.bfloat16):
        return jax.ShapeDtypeStruct(dims, kind)

    def call(kernel, name, outs, args, mib, micros, scratch=(), specs=None):
        return pl.pallas_call(
            kernel,
            out_shape=outs,
            in_specs=specs or [VMEM] * len(args),
            out_specs=(VMEM,) * len(outs),
            scratch_shapes=list(scratch),
            compiler_params=params(mib),
            cost_estimate=pl.CostEstimate(
                flops=int(micros * 1.1e9), bytes_accessed=2**20, transcendentals=0
            ),
            name=name,
        )(*args)

    own, face = call(
        pack_kernel,
        "pack",
        (
            shape((rows + META, C)),
            shape((2 * width + META, C)),
        ),
        (features, cotangent, block_coords, block_counts),
        60,
        3,
        [
            pltpu.SMEM((1, slots), jnp.int32),
            pltpu.SMEM((1, 1), jnp.int32),
            pltpu.SemaphoreType.DMA((2 + 2 * slots,)),
        ],
        [HBM] * 4,
    )
    side = from_sides(own)
    field = (4 * width, C)
    fars = from_far(face)
    def gathered(name, cells, after, micros=0.5):
        return call(
            functools.partial(gather_kernel, len(cells)),
            name,
            (shape((sum(part.shape[0] for part in cells), C)),),
            (*cells, *after),
            8,
            micros,
            specs=[VMEM] * len(cells) + [ANY] * len(after),
        )[0]

    parts = [own, *side]
    chip, thins = call(
        functools.partial(join_kernel, len(parts)),
        "join",
        (
            shape((len(parts) * (rows + META), C)),
            shape((2 * (6 * width + META), C)),
        ),
        (*parts, fars[0]),
        8,
        3,
        specs=[VMEM] * len(parts) + [ANY],
    )
    chip = [chip, swap(chip, "gx", 1)]
    columns = shape((9, 6 * width, C))
    main = call(
        functools.partial(main_kernel, sides),
        "first_convs",
        (shape(field, jnp.float32),) * 2,
        (*chip, first_weight, second_weight),
        12,
        3,
        [pltpu.VMEM(columns.shape, jnp.bfloat16)] * 2,
    )
    both, thin, cross, source, target = call(
        functools.partial(layer_kernel, sides),
        "layer",
        (
            shape((rows, C)),
            shape((6 * width, C)),
            shape((6 * width, C)),
            shape((2, LANES), jnp.float32),
            shape((9 * width, 1), jnp.float32),
        ),
        (*chip, *fars, first_weight, second_weight, *main),
        8,
        1,
        [pltpu.VMEM(field, jnp.float32)] * 2,
    )
    both_side = from_sides(both)

    def late_far(after):
        (late_face,) = call(
            face_kernel,
            "face",
            (shape((2 * width, C)),),
            (both, *after),
            8,
            0.3,
            specs=[VMEM] + [ANY] * len(after),
        )
        return from_far(late_face)

    grad_scale = 1.0 / math.sqrt(64 * slots * gx * gy)

    def over_z(own_part, sent):
        got = [swap(cells, "gx", 4 * m) for m, cells in enumerate(sent, 1)]
        return (own_part + sum(cells.astype(jnp.float32) for cells in got)) * grad_scale

    if grouped:
        cols = C // 2

        def group_shapes(count):
            return shape((count, *columns.shape)), shape((count, *columns.shape[:2], cols))

        far_faces = gathered("far_faces", fars, main[:1])
        near_faces = swap(far_faces, "gx", 1)
        (slim_faces,) = call(
            slim_faces_kernel,
            "slim_faces",
            (shape((3 * width + 2 * META, C)),),
            (*fars, main[0]),
            8,
            0.5,
            specs=[VMEM] * 2 + [ANY],
        )
        beside = [swap(cells, "gx", 2) for cells in (thins, slim_faces)]
        chip_cols = [
            call(
                functools.partial(chip_cols_kernel, 1, members),
                "chip_cols",
                group_shapes(len(members)),
                (*chip, far_faces, near_faces, *after),
                8,
                1.6,
                specs=[VMEM] * 4 + [ANY] * len(after),
            )
            for members, after in zip(CHIP_MEMBERS, ((), beside))
        ]
        late_fars = late_far(chip_cols[0][1:])
        early = gathered("gather_early", beside, chip_cols[0][1:])
        near_early = swap(early, "gx", 1)
        thin_other = swap(thin, "gx", 2)
        cross_other = across(cross, [(i, i ^ 2) for i in range(gx)], side_steps(gy)[0])
        packed = gathered(
            "gather_late",
            (thin_other, cross_other, both, both_side[0]),
            (chip_cols[1][1], late_fars[0]),
        )
        near_packed = swap(packed, "gx", 1)
        nears = [near_packed]
        other_features, other_seeds = call(
            other_cols_kernel,
            "other_cols",
            group_shapes(len(OTHER_MEMBERS)),
            (early, near_early, packed),
            8,
            3,
            specs=[VMEM] * 2 + [ANY],
        )
        members = [both, both_side[0], thin_other, cross_other, near_packed]
        taps = 2 + (chunk - 2) // C
        own_part, *sent = call(
            group_terms_kernel,
            "group_terms",
            (
                shape((2 * chunk, cols), jnp.float32),
                *[shape((2 * chunk, cols))] * (deeps - 1),
            ),
            (
                *members,
                *chip_cols[0],
                *chip_cols[1],
                other_features,
                other_seeds,
            ),
            12,
            3.5,
            [pltpu.VMEM((deeps, taps * C, cols), jnp.float32)],
        )
        token = sent[0]
        grads = over_z(own_part, sent)
        first_grad, second_grad = grads[:chunk], grads[chunk:]
    else:
        far_faces = jnp.concatenate(fars, axis=0)
        nears = [swap(cells, "gx", 1) for cells in (both, *both_side)]
        late_fars = late_far(())

        def summed(kernel, name, cells):
            keep, send = call(
                kernel,
                name,
                (
                    shape((gx // 2, chunk, C), jnp.float32),
                    shape((gx // 2, chunk, C), jnp.float32),
                ),
                (both, cells),
                24,
                4,
                [pltpu.VMEM((TAPS * C, C), jnp.float32)],
            )
            keep = keep.reshape(deeps, 2, chunk, C)
            got = swap(send, "gx", 1).reshape(keep.shape)

            def part(i):
                return piece(keep, i, 1) + piece(got, i, 1)

            total = part(half) + swap(part(1 - half).astype(jnp.bfloat16), "gx", 2).astype(
                jnp.float32
            )
            total = total.reshape(deeps, chunk, gy, C // gy)
            total = piece(total, iy, 2) + sum(
                swap(piece(total, iy ^ m, 2).astype(jnp.bfloat16), "gy", m).astype(jnp.float32)
                for m in range(1, gy)
            )
            total = over_z(
                piece(total, deep, 0),
                [piece(total, deep ^ m, 0).astype(jnp.bfloat16) for m in range(1, deeps)],
            )
            return total, send

        feature_cols, seed_cols = call(
            functools.partial(chip_cols_kernel, sides, ((0, 0),)),
            "own_cols",
            (shape((1, *columns.shape)),) * 2,
            (*chip, far_faces, far_faces),
            8,
            1,
        )
        feature_cols, seed_cols = feature_cols[0], seed_cols[0]
        second_grad, token = summed(second_terms_kernel, "second_terms", seed_cols)
        first_grad, _ = summed(first_terms_kernel, "first_terms", feature_cols)

    late = [chip[0], both, *both_side, *nears, *late_fars]
    result = shape((slots, 64, C), jnp.float32)
    output, input_grad = call(
        functools.partial(last_kernel, sides),
        "last_layer",
        (result, result),
        (*late, first_weight, second_weight, source, target, token),
        12,
        0.1,
        [pltpu.VMEM(columns.shape, jnp.bfloat16)] * 2,
        [VMEM] * (len(late) + 4) + [ANY],
    )
    return (
        output.reshape(features.shape),
        input_grad.reshape(features.shape),
        first_grad,
        second_grad,
    )


def solution(mesh):
    placed = (
        P("gx", "gy", None, None, None),
        P("gx", "gy", None),
        P("gx", "gy"),
        P(),
        P(),
        P("gx", "gy", None, None, None),
    )
    return jax.shard_map(
        per_device,
        mesh=mesh,
        in_specs=placed,
        out_specs=(
            P("gx", "gy", None, None, None),
            P("gx", "gy", None, None, None),
            P("gx", "gy"),
            P("gx", "gy"),
        ),
        check_vma=False,
    )
```

```python
import functools
import math

import jax
import jax.numpy as jnp
from jax import lax
from jax.experimental import pallas as pl
from jax.experimental.pallas import tpu as pltpu
from jax.sharding import PartitionSpec as P

C = 256
TAPS = 27
PLANE = 16
META = 16
LANES = 512
STEP_Y = 64.0
STEP_X = 4096.0
NOWHERE = -1.0e7
VMEM = pl.BlockSpec(memory_space=pltpu.MemorySpace.VMEM)
HBM = pl.BlockSpec(memory_space=pltpu.MemorySpace.HBM)
ANY = pl.BlockSpec(memory_space=pl.ANY)


def params(mib):
    return pltpu.CompilerParams(vmem_limit_bytes=mib * 2**20)


def dot(lhs, rhs, dims=((1,), (0,))):
    return lax.dot_general(lhs, rhs, (dims, ((), ())), preferred_element_type=jnp.float32)


def iota(shape, dim):
    return lax.broadcasted_iota(jnp.int32, shape, dim)


def place_codes(meta, offset, absent=NOWHERE):
    rows = meta.astype(jnp.float32)
    parts = []
    for half in range(2):
        x, y, z, live = (rows[4 * half + i : 4 * half + i + 1] for i in range(4))
        parts.append(jnp.where(live > 0.5, x * STEP_X + y * STEP_Y + z + offset, absent))
    return jnp.concatenate(parts, axis=1)


def source_codes(metas, offsets, width):
    lane = iota((1, LANES), 1)
    total = jnp.full((1, LANES), NOWHERE, jnp.float32)
    for place, (meta, offset) in enumerate(zip(metas, offsets)):
        inside = (lane >= place * width) & (lane < (place + 1) * width)
        total = jnp.where(inside, place_codes(meta, offset), total)
    return total


def target_codes(meta, width):
    codes = place_codes(meta, 0.0, 3 * NOWHERE)
    own = iota((width, LANES), 0) == iota((width, LANES), 1)
    column = jnp.sum(jnp.where(own, codes, 0.0), axis=1, keepdims=True)
    return jnp.concatenate(
        [column + ((s // 3 - 1) * STEP_Y + (s % 3 - 1)) for s in range(9)], axis=0
    )


def selectors(before, after, target, sides, width):
    middle = (1 + sides) * width
    return tuple(
        (codes == target + step).astype(jnp.float32).astype(jnp.bfloat16)
        for codes, step in (
            (before[:, : 2 * middle], -STEP_X),
            (before[:, :middle], 0.0),
            (after[:, : 2 * middle], STEP_X),
        )
    )


def fill(cols_ref, tiles, faces, odd, chosen, width, columns=slice(None)):
    def load(source, plane):
        ref, first, paired = source[:3]
        if paired:
            at = first + plane % 2 * width
            return ref[at : at + width, plane // 2 * (C // 2) : (plane // 2 + 1) * (C // 2)]
        return ref[first + plane * width : first + (plane + 1) * width, columns]

    for plane in range(6):
        if plane in (0, 5):
            start = 3 if plane == 0 else 0
            pieces = [load(tile, start) for tile in tiles]
            for near, far in faces:
                if far is None:
                    pieces.append(load(near, start))
                    continue
                near, far = load(near, start), load(far, far[3])
                pieces.append(jnp.where(odd, near, far) if plane == 0 else jnp.where(odd, far, near))
        else:
            pieces = [load(tile, plane - 1) for tile in tiles]
        select = chosen[0 if plane == 0 else 2 if plane == 5 else 1]
        moved = dot(select, jnp.concatenate(pieces, axis=0)).astype(jnp.bfloat16)
        for shift in range(9):
            cols_ref[shift, plane * width : (plane + 1) * width, :] = moved[
                shift * width : (shift + 1) * width
            ]


def tap_rows(cols_ref, tap, width, columns=slice(None)):
    start = tap // 9 * width
    return cols_ref[tap % 9, start : start + 4 * width, columns]


def conv(cols_ref, weight_ref, width):
    total = None
    for tap in range(TAPS):
        term = dot(tap_rows(cols_ref, tap, width), weight_ref[tap * C : (tap + 1) * C, :])
        total = term if total is None else total + term
    return total


def conv_back(cols_ref, weight_ref, width):
    total = None
    for tap in range(TAPS):
        weight = weight_ref[(26 - tap) * C : (27 - tap) * C, :]
        term = dot(tap_rows(cols_ref, tap, width), weight, ((1,), (1,)))
        total = term if total is None else total + term
    return total


def live_rows(meta, width):
    codes = place_codes(meta, 0.0)
    own = iota((width, LANES), 0) == iota((width, LANES), 1)
    column = jnp.sum(jnp.where(own, codes, 0.0), axis=1, keepdims=True)
    return jnp.concatenate([column] * 4, axis=0) > 0.5 * NOWHERE


def near_row(width):
    return pl.multiple_of((lax.axis_index("gx") % 2) * (3 * width), PLANE)


def side_offsets(sides):
    if sides == 2:
        return [-8 * STEP_Y, 8 * STEP_Y]
    return [(1 - 2 * lax.axis_index("gy")).astype(jnp.float32) * (8 * STEP_Y)]


def pack_kernel(features, cotangent, coords, counts, *refs):
    own_ref, face_ref, place_ref, live_ref, sems = refs
    slots = features.shape[2]
    width = slots * PLANE
    copies = [
        pltpu.make_async_copy(coords.at[0], place_ref, sems.at[0]),
        pltpu.make_async_copy(counts, live_ref, sems.at[1]),
    ]
    for field, ref in enumerate((features, cotangent)):
        planes = own_ref.at[pl.ds(field * 4 * width, 4 * width)].reshape(4, slots, PLANE, C)
        for slot in range(slots):
            copies.append(
                pltpu.make_async_copy(
                    ref.at[0, 0, slot].reshape(4, PLANE, C),
                    planes.at[:, slot],
                    sems.at[len(copies)],
                )
            )
    for copy in copies:
        copy.start()
    for copy in copies:
        copy.wait()
    lane = iota((1, LANES), 1)
    lane_slot = (lane // PLANE) % slots
    position = jnp.zeros((1, LANES), jnp.int32)
    for slot in range(slots):
        position = jnp.where(lane_slot == slot, place_ref[0, slot], position)
    values = [
        position // 16,
        4 * (position // 8 % 2) + lane % PLANE // 4,
        4 * (position % 8) + lane % 4,
        (lane_slot < live_ref[0, 0]).astype(jnp.int32),
    ]
    rows = [v[:, h * C : (h + 1) * C] for h in range(2) for v in values]
    rows.append(jnp.zeros((META - 8, C), jnp.int32))
    meta = jnp.concatenate(rows, axis=0).astype(jnp.float32).astype(jnp.bfloat16)
    own_ref[8 * width :, :] = meta
    at = near_row(width)
    face_ref[:width, :] = own_ref[pl.ds(at, width), :]
    face_ref[width : 2 * width, :] = own_ref[pl.ds(pl.multiple_of(4 * width + at, PLANE), width), :]
    face_ref[2 * width :, :] = meta


class Around:
    def __init__(self, tiles, fars, sides, rows):
        self.tiles, self.fars, self.sides = tiles, fars, sides
        self.rows, self.width = rows, rows // 8

    def order(self, s):
        return [s] + [other for other in range(1 + self.sides) if other != s]

    def odd(self, j):
        return (lax.axis_index("gx") + j) % 2 == 1

    def codes(self, j, s):
        def meta(ref, start):
            return ref[start : start + 8, :]

        def tile_meta(j, o):
            ref, first, thin = self.tiles[j][o]
            return meta(ref, first + (self.rows * 3 // 4 if thin else self.rows))

        order = self.order(s)
        metas = [tile_meta(j, o) for o in order]
        offsets = side_offsets(self.sides)
        offsets = [0.0] + ([-o for o in offsets] if s else offsets)
        befores, afters = [], []
        for o in order:
            near = tile_meta(j ^ 1, o)
            if self.fars is None:
                far = jnp.zeros_like(near)
            else:
                ref, first, *side = self.fars[j][o]
                places = 3 * self.width + side[0] * META if side else 2 * self.width
                far = meta(ref, first + places)
            befores.append(jnp.where(self.odd(j), near, far))
            afters.append(jnp.where(self.odd(j), far, near))
        before, after = (
            source_codes(metas + beyond, offsets + [o + step for o in offsets], self.width)
            for beyond, step in ((befores, -2 * STEP_X), (afters, 2 * STEP_X))
        )
        return before, after, target_codes(metas[0], self.width)

    def sources(self, j, s, field):
        def tile(j, o):
            ref, first, thin = self.tiles[j][o]
            return ref, first + field * 4 * self.width, thin and field == 1

        order = self.order(s)
        faces = []
        for o in order:
            far = None
            if self.fars is not None:
                ref, first, *side = self.fars[j][o]
                far = (ref, first + field * self.width, False, 0)
                if side and field:
                    far = (ref, first + 2 * self.width, True, 2 * side[0])
                elif side:
                    far = (ref, first + side[0] * self.width, False, 0)
            faces.append((tile(j ^ 1, o), far))
        return [tile(j, o) for o in order], faces, self.odd(j)


def chip_places(refs, sides, rows):
    return [[(ref, s * (rows + META), False) for s in range(1 + sides)] for ref in refs]


def main_kernel(sides, *refs):
    tiles, refs = refs[:2], refs[2:]
    first, second, pre_ref, back_ref, feature_cols, seed_cols = refs
    rows = 2 * pre_ref.shape[0]
    width = rows // 8
    around = Around(chip_places(tiles, sides, rows), None, sides, rows)
    chosen = selectors(*around.codes(0, 0), sides, width)
    fill(feature_cols, *around.sources(0, 0, 0), chosen, width)
    fill(seed_cols, *around.sources(0, 0, 1), chosen, width)
    pre_ref[...] = conv(feature_cols, first, width)
    back_ref[...] = conv_back(seed_cols, second, width)


def layer_kernel(sides, *refs):
    tiles, refs = refs[:2], refs[2:]
    fars, refs = refs[: 1 + sides], refs[1 + sides :]
    first, second, pre_main, back_main = refs[:4]
    both_ref, slim_ref, cross_ref, source_ref, target_ref, pre_ref, back_ref = refs[-7:]
    rows = both_ref.shape[0]
    width = rows // 8
    around = Around(chip_places(tiles, sides, rows), [[(ref, 0) for ref in fars]], sides, rows)
    before, after, target = around.codes(0, 0)
    source_ref[0:1, :] = before
    source_ref[1:2, :] = after
    target_ref[...] = target
    odd = around.odd(0)
    codes = jnp.where(odd, after, before)[:, : 2 * (1 + sides) * width]
    chosen = (codes == target + jnp.where(odd, STEP_X, -STEP_X)).astype(jnp.float32)
    chosen = chosen.astype(jnp.bfloat16)
    nothing = jnp.zeros(((1 + sides) * width, C), jnp.bfloat16)
    at = near_row(width)

    def add(total_ref, main_ref, field, weight):
        pieces = [nothing] + [ref[field * width : (field + 1) * width, :] for ref in fars]
        moved = dot(chosen, jnp.concatenate(pieces, axis=0)).astype(jnp.bfloat16)
        more = sum(weight(shift, moved[shift * width : (shift + 1) * width]) for shift in range(9))
        total_ref[...] = main_ref[...]
        total_ref[pl.ds(at, width), :] = total_ref[pl.ds(at, width), :] + more

    def tap(weight_ref, index):
        return weight_ref[pl.ds(pl.multiple_of(index * C, C), C), :]

    add(
        pre_ref,
        pre_main,
        0,
        lambda shift, cells: dot(cells, tap(first, jnp.where(odd, 18, 0) + shift)),
    )
    add(
        back_ref,
        back_main,
        1,
        lambda shift, cells: dot(cells, tap(second, jnp.where(odd, 8, 26) - shift), ((1,), (1,))),
    )
    pre_first = pre_ref[...]
    live = live_rows(tiles[0][rows : rows + 8, :], width)
    sigmoid = 1.0 / (1.0 + jnp.exp(-pre_first))
    hidden = jnp.where(live, pre_first * sigmoid, 0.0)
    both_ref[: 4 * width, :] = hidden.astype(jnp.bfloat16)
    slope = jnp.where(live, sigmoid * (1.0 + pre_first * (1.0 - sigmoid)), 0.0)
    both_ref[4 * width :, :] = (back_ref[...] * slope).astype(jnp.bfloat16)
    if sides == 1:
        slim(both_ref, slim_ref, lax.axis_index("gy"))
        slim(both_ref, cross_ref, 1 - lax.axis_index("gy"))
    else:
        slim_ref[...] = jnp.zeros(slim_ref.shape, slim_ref.dtype)
        cross_ref[...] = jnp.zeros(cross_ref.shape, cross_ref.dtype)


def join_kernel(count, *refs):
    joined_ref, slim_ref = refs[-2:]
    gather_kernel(count, *refs[:count], joined_ref)
    if count == 2:
        size = slim_ref.shape[0] // 2
        for i in range(2):
            slim(refs[i], slim_ref.at[pl.ds(i * size, size)], lax.axis_index("gy"))
    else:
        slim_ref[...] = jnp.zeros(slim_ref.shape, slim_ref.dtype)


def slim(tile_ref, slim_ref, half):
    rows = tile_ref.shape[0] // (8 * PLANE) * 4 * PLANE
    columns = pl.ds(pl.multiple_of(half * (C // 2), 128), C // 2)
    slim_ref[:rows, :] = tile_ref[:rows, :]
    slim_ref[rows : rows + rows // 2, : C // 2] = tile_ref[rows : rows + rows // 2, columns]
    slim_ref[rows : rows + rows // 2, C // 2 :] = tile_ref[rows + rows // 2 : 2 * rows, columns]
    if slim_ref.shape[0] > rows + rows // 2:
        slim_ref[rows + rows // 2 :, :] = tile_ref[2 * rows :, :]


def faces_kernel(far, side_far, _, faces_ref, slim_ref):
    gather_kernel(2, far, side_far, faces_ref)
    width = (far.shape[0] - META) // 2
    columns = my_columns(C // 2)
    for s, ref in enumerate((far, side_far)):
        slim_ref[s * width : (s + 1) * width, :] = ref[:width, :]
        slim_ref[2 * width : 3 * width, s * (C // 2) : (s + 1) * (C // 2)] = ref[
            width : 2 * width, columns
        ]
        at = 3 * width + s * META
        slim_ref[at : at + META, :] = ref[2 * width :, :]


def gather_kernel(count, *refs):
    packed_ref = refs[-1]
    at = 0
    for ref in refs[:count]:
        packed_ref[at : at + ref.shape[0], :] = ref[...]
        at += ref.shape[0]


def face_kernel(both_ref, *refs):
    face_ref = refs[-1]
    width = both_ref.shape[0] // 8
    at = near_row(width)
    face_ref[:width, :] = both_ref[pl.ds(at, width), :]
    face_ref[width:, :] = both_ref[pl.ds(pl.multiple_of(4 * width + at, PLANE), width), :]


def my_columns(cols):
    if cols == C:
        return slice(None)
    return pl.ds(pl.multiple_of(lax.axis_index("gy") * cols, 128), cols)


def store_terms(keep_ref, send_ref, total_ref):
    core = lax.axis_index("gx") % 2
    pairs, rows = keep_ref.shape[0], keep_ref.shape[1]
    for i in range(pairs):
        keep_at = pl.multiple_of((2 * i + core) * rows, 8)
        send_at = pl.multiple_of((2 * i + 1 - core) * rows, 8)
        keep_ref[i] = total_ref[pl.ds(keep_at, rows), :]
        send_ref[i] = total_ref[pl.ds(send_at, rows), :]


def second_terms_kernel(both_ref, cols_ref, keep_ref, send_ref, total_ref):
    rows = both_ref.shape[0] // 2
    hidden = both_ref[:rows, :].astype(jnp.float32).T.astype(jnp.bfloat16)
    for tap in range(TAPS):
        total_ref[tap * C : (tap + 1) * C, :] = dot(hidden, tap_rows(cols_ref, 26 - tap, rows // 4))
    store_terms(keep_ref, send_ref, total_ref)


def first_terms_kernel(both_ref, cols_ref, keep_ref, send_ref, total_ref):
    rows = both_ref.shape[0] // 2
    grad = both_ref[rows:, :]
    for tap in range(TAPS):
        total_ref[tap * C : (tap + 1) * C, :] = dot(
            tap_rows(cols_ref, tap, rows // 4), grad, ((0,), (0,))
        )
    store_terms(keep_ref, send_ref, total_ref)


def group_cols(around, members, feature_ref, seed_ref):
    columns = my_columns(seed_ref.shape[3])
    for index, (j, s) in enumerate(members):
        chosen = selectors(*around.codes(j, s), around.sides, around.width)
        fill(feature_ref.at[index], *around.sources(j, s, 0), chosen, around.width)
        fill(seed_ref.at[index], *around.sources(j, s, 1), chosen, around.width, columns)


CHIP_MEMBERS = (((0, 0), (0, 1)), ((1, 0), (1, 1)))
OTHER_MEMBERS = ((2, 0), (2, 1), (3, 0), (3, 1))


def chip_cols_kernel(sides, members, *refs):
    tiles, (far, near_far), (feature_ref, seed_ref) = refs[:2], refs[2:4], refs[-2:]
    rows = feature_ref.shape[2] // 6 * 8
    face = rows // 4 + META
    fars = [[(ref, s * face) for s in range(1 + sides)] for ref in (far, near_far)]
    around = Around(chip_places(tiles, sides, rows), fars, sides, rows)
    group_cols(around, members, feature_ref, seed_ref)


def other_cols_kernel(packed, near_packed, _, feature_ref, seed_ref):
    width = feature_ref.shape[2] // 6
    rows = 8 * width
    thin = 6 * width + META
    tiles = [[(ref, s * thin, True) for s in range(2)] for ref in (packed, near_packed)]
    fars = [[(ref, 2 * thin, s) for s in range(2)] for ref in (packed, near_packed)]
    around = Around([None, None] + tiles, [None, None] + fars, 1, rows)
    group_cols(around, OTHER_MEMBERS, feature_ref, seed_ref)


def group_terms(cols_of, fields, first, top, out_refs, total_ref):
    own_ref, send_refs = out_refs[0], out_refs[1:]
    chunk, cols = own_ref.shape[0] // 2, own_ref.shape[1]
    deep = lax.axis_index("gx") // 4
    row = lax.axis_index("gx") % 4
    taps = total_ref.shape[1] // C
    width = fields[0].shape[0] // 4
    starts = [((deep ^ m) * 4 + row) * chunk for m in range(1 + len(send_refs))]

    def rows(tap):
        tap = jnp.minimum(tap, TAPS - 1)
        tap = tap if first else TAPS - 1 - tap
        at = pl.multiple_of(tap // 9 * width, PLANE)
        return jnp.concatenate(
            [cols_of(i, tap % 9, pl.ds(at, 4 * width)) for i in range(len(fields))], axis=0
        )

    operand = jnp.concatenate(fields, axis=0).astype(jnp.float32).T.astype(jnp.bfloat16)
    wanted = [(m, i) for m in range(len(starts)) for i in range(taps)]
    if first:
        for m, i in wanted:
            result = dot(operand, rows(starts[m] // C + i))
            total_ref[m, i * C : (i + 1) * C, :] = result.T
    else:
        step = max(1, C // cols)
        for at in range(0, len(wanted), step):
            part = wanted[at : at + step]
            result = dot(
                operand, jnp.concatenate([rows(starts[m] // C + i) for m, i in part], axis=1)
            )
            for place, (m, i) in enumerate(part):
                total_ref[m, i * C : (i + 1) * C, :] = result[:, place * cols : (place + 1) * cols]
    for m, start in enumerate(starts):
        at = pl.multiple_of(start % C, 16)
        if m == 0:
            own_ref[top : top + chunk, :] = total_ref[m, pl.ds(at, chunk), :]
        else:
            send_refs[m - 1][top : top + chunk, :] = total_ref[m, pl.ds(at, chunk), :].astype(
                jnp.bfloat16
            )


def group_terms_kernel(*refs):
    both, thins, packed, refs = refs[:2], refs[2:4], refs[4], refs[5:]
    groups, refs = refs[:6], refs[6:]
    out_refs, total_ref = refs[:-1], refs[-1]
    rows = both[0].shape[0] // 2
    chunk = out_refs[0].shape[0] // 2
    columns = my_columns(out_refs[0].shape[1])
    thin_rows = thins[0].shape[0]
    both = [(ref, 0) for ref in both]
    both += [(packed, 2 * thin_rows), (packed, 2 * thin_rows + 2 * rows)]
    thins = [(ref, 0) for ref in thins] + [(packed, 0), (packed, thin_rows)]

    def group(part, tile, shift, at):
        place, index = (tile // 2, tile % 2) if tile < 4 else (2, tile - 4)
        return groups[part + 2 * place][index, shift, at, :]

    features_of, seeds_of = functools.partial(group, 0), functools.partial(group, 1)
    grads = [ref[at + rows : at + 2 * rows, columns] for ref, at in both]
    for ref, at in thins:
        halves = ref[at + rows : at + rows + rows // 2, :]
        grads.append(jnp.concatenate([halves[:, : C // 2], halves[:, C // 2 :]], axis=0))
    hiddens = [ref[at : at + rows, :] for ref, at in (*both, *thins)]
    group_terms(features_of, grads, True, 0, out_refs, total_ref)
    group_terms(seeds_of, hiddens, False, chunk, out_refs, total_ref)


def last_kernel(sides, *refs):
    own_ref, refs = refs[0], refs[1:]
    tiles, refs = refs[: 1 + sides], refs[1 + sides :]
    count = 1 if sides == 1 else 1 + sides
    nears, refs = refs[:count], refs[count:]
    fars, refs = refs[: 1 + sides], refs[1 + sides :]
    first, second, source_ref, target_ref, _, output_ref, input_ref = refs[:7]
    hidden_cols_ref, grad_cols_ref = refs[7:]
    width = tiles[0].shape[0] // 8
    slots = output_ref.shape[0]
    chosen = selectors(source_ref[0:1, :], source_ref[1:2, :], target_ref[...], sides, width)
    live = live_rows(own_ref[8 * width : 8 * width + 8, :], width)
    rows = tiles[0].shape[0]
    if sides == 1:
        near_at = nears[0].shape[0] - 2 * rows
        nears = [(nears[0], near_at, False), (nears[0], near_at + rows, False)]
    else:
        nears = [(ref, 0, False) for ref in nears]
    around = Around(
        [[(ref, 0, False) for ref in tiles], nears],
        [[(ref, 0) for ref in fars]],
        sides,
        rows,
    )

    def put(ref, total):
        total = jnp.where(live, total, 0.0)
        for x in range(4):
            for slot in range(slots):
                start = x * width + slot * PLANE
                ref[slot, x * PLANE : (x + 1) * PLANE, :] = total[start : start + PLANE]

    fill(hidden_cols_ref, *around.sources(0, 0, 0), chosen, width)
    fill(grad_cols_ref, *around.sources(0, 0, 1), chosen, width)
    put(output_ref, conv(hidden_cols_ref, second, width))
    put(input_ref, conv_back(grad_cols_ref, first, width))


def swap(cells, axis, bit):
    return lax.ppermute(cells, axis, [(i, i ^ bit) for i in range(lax.axis_size(axis))])


def side_steps(count):
    if count == 2:
        return [[(0, 1), (1, 0)]]
    ends = count - 1
    return [[(i, i + 1) for i in range(ends)], [(i + 1, i) for i in range(ends)]]


def far_steps(count):
    pairs = [(i, i + 1) for i in range(1, count - 1, 2)]
    return pairs + [(b, a) for a, b in pairs]


def from_sides(cells):
    return [lax.ppermute(cells, "gy", step) for step in side_steps(lax.axis_size("gy"))]


def across(face, gx_steps, gy_steps):
    gy = lax.axis_size("gy")
    return lax.ppermute(
        face, ("gx", "gy"), [(a * gy + c, b * gy + d) for a, b in gx_steps for c, d in gy_steps]
    )


def from_far(face):
    far = lax.ppermute(face, "gx", far_steps(lax.axis_size("gx")))
    return [far, *from_sides(far)]


def piece(cells, index, axis):
    return lax.dynamic_index_in_dim(cells, index, axis, keepdims=False)


def per_device(features, block_coords, block_counts, first_weight, second_weight, cotangent):
    gx, gy = lax.axis_size("gx"), lax.axis_size("gy")
    iy, ix = lax.axis_index("gy"), lax.axis_index("gx")
    slots = features.shape[2]
    width = slots * PLANE
    rows = 8 * width
    half, deep = ix // 2 % 2, ix // 4
    deeps = gx // 4
    grouped = gy == 2
    sides = 1 if grouped else 2
    chunk = TAPS * C // gx

    def shape(dims, kind=jnp.bfloat16):
        return jax.ShapeDtypeStruct(dims, kind)

    def call(kernel, name, outs, args, mib, micros, scratch=(), specs=None):
        return pl.pallas_call(
            kernel,
            out_shape=outs,
            in_specs=specs or [VMEM] * len(args),
            out_specs=(VMEM,) * len(outs),
            scratch_shapes=list(scratch),
            compiler_params=params(mib),
            cost_estimate=pl.CostEstimate(
                flops=int(micros * 1.1e9), bytes_accessed=2**20, transcendentals=0
            ),
            name=name,
        )(*args)

    own, face = call(
        pack_kernel,
        "pack",
        (
            shape((rows + META, C)),
            shape((2 * width + META, C)),
        ),
        (features, cotangent, block_coords, block_counts),
        60,
        3,
        [
            pltpu.SMEM((1, slots), jnp.int32),
            pltpu.SMEM((1, 1), jnp.int32),
            pltpu.SemaphoreType.DMA((2 + 2 * slots,)),
        ],
        [HBM] * 4,
    )
    side = from_sides(own)
    field = (4 * width, C)
    fars = from_far(face)
    def gathered(name, cells, after, micros=0.5):
        return call(
            functools.partial(gather_kernel, len(cells)),
            name,
            (shape((sum(part.shape[0] for part in cells), C)),),
            (*cells, *after),
            8,
            micros,
            specs=[VMEM] * len(cells) + [ANY] * len(after),
        )[0]

    parts = [own, *side]
    chip, thins = call(
        functools.partial(join_kernel, len(parts)),
        "join",
        (
            shape((len(parts) * (rows + META), C)),
            shape((2 * (6 * width + META), C)),
        ),
        (*parts, fars[0]),
        8,
        3,
        specs=[VMEM] * len(parts) + [ANY],
    )
    chip = [chip, swap(chip, "gx", 1)]
    columns = shape((9, 6 * width, C))
    main = call(
        functools.partial(main_kernel, sides),
        "first_convs",
        (shape(field, jnp.float32),) * 2,
        (*chip, first_weight, second_weight),
        12,
        3,
        [pltpu.VMEM(columns.shape, jnp.bfloat16)] * 2,
    )
    both, thin, cross, source, target = call(
        functools.partial(layer_kernel, sides),
        "layer",
        (
            shape((rows, C)),
            shape((6 * width, C)),
            shape((6 * width, C)),
            shape((2, LANES), jnp.float32),
            shape((9 * width, 1), jnp.float32),
        ),
        (*chip, *fars, first_weight, second_weight, *main),
        8,
        1,
        [pltpu.VMEM(field, jnp.float32)] * 2,
    )
    both_side = from_sides(both)

    def late_far(after):
        (late_face,) = call(
            face_kernel,
            "face",
            (shape((2 * width, C)),),
            (both, *after),
            8,
            0.3,
            specs=[VMEM] + [ANY] * len(after),
        )
        return from_far(late_face)

    grad_scale = 1.0 / math.sqrt(64 * slots * gx * gy)

    def over_z(own_part, sent):
        got = [swap(cells, "gx", 4 * m) for m, cells in enumerate(sent, 1)]
        return (own_part + sum(cells.astype(jnp.float32) for cells in got)) * grad_scale

    if grouped:
        cols = C // 2

        def group_shapes(count):
            return shape((count, *columns.shape)), shape((count, *columns.shape[:2], cols))

        far_faces, slim_faces = call(
            faces_kernel,
            "far_faces",
            (shape((2 * (2 * width + META), C)), shape((3 * width + 2 * META, C))),
            (*fars, main[0]),
            8,
            0.5,
            specs=[VMEM] * 2 + [ANY],
        )
        near_faces = swap(far_faces, "gx", 1)
        beside = [swap(cells, "gx", 2) for cells in (thins, slim_faces)]
        chip_cols = [
            call(
                functools.partial(chip_cols_kernel, 1, members),
                "chip_cols",
                group_shapes(len(members)),
                (*chip, far_faces, near_faces, *after),
                8,
                1.6,
                specs=[VMEM] * 4 + [ANY] * len(after),
            )
            for members, after in zip(CHIP_MEMBERS, ((), beside))
        ]
        late_fars = late_far(chip_cols[0][1:])
        early = gathered("gather_early", beside, chip_cols[0][1:])
        near_early = swap(early, "gx", 1)
        thin_other = swap(thin, "gx", 2)
        cross_other = across(cross, [(i, i ^ 2) for i in range(gx)], side_steps(gy)[0])
        packed = gathered(
            "gather_late",
            (thin_other, cross_other, both, both_side[0]),
            (chip_cols[1][1], late_fars[0]),
        )
        near_packed = swap(packed, "gx", 1)
        nears = [near_packed]
        other_features, other_seeds = call(
            other_cols_kernel,
            "other_cols",
            group_shapes(len(OTHER_MEMBERS)),
            (early, near_early, packed),
            8,
            3,
            specs=[VMEM] * 2 + [ANY],
        )
        members = [both, both_side[0], thin_other, cross_other, near_packed]
        taps = 2 + (chunk - 2) // C
        own_part, *sent = call(
            group_terms_kernel,
            "group_terms",
            (
                shape((2 * chunk, cols), jnp.float32),
                *[shape((2 * chunk, cols))] * (deeps - 1),
            ),
            (
                *members,
                *chip_cols[0],
                *chip_cols[1],
                other_features,
                other_seeds,
            ),
            12,
            3.5,
            [pltpu.VMEM((deeps, taps * C, cols), jnp.float32)],
        )
        token = sent[0]
        grads = over_z(own_part, sent)
        first_grad, second_grad = grads[:chunk], grads[chunk:]
    else:
        far_faces = jnp.concatenate(fars, axis=0)
        nears = [swap(cells, "gx", 1) for cells in (both, *both_side)]
        late_fars = late_far(())

        def summed(kernel, name, cells):
            keep, send = call(
                kernel,
                name,
                (
                    shape((gx // 2, chunk, C), jnp.float32),
                    shape((gx // 2, chunk, C), jnp.float32),
                ),
                (both, cells),
                24,
                4,
                [pltpu.VMEM((TAPS * C, C), jnp.float32)],
            )
            keep = keep.reshape(deeps, 2, chunk, C)
            got = swap(send, "gx", 1).reshape(keep.shape)

            def part(i):
                return piece(keep, i, 1) + piece(got, i, 1)

            total = part(half) + swap(part(1 - half).astype(jnp.bfloat16), "gx", 2).astype(
                jnp.float32
            )
            total = total.reshape(deeps, chunk, gy, C // gy)
            total = piece(total, iy, 2) + sum(
                swap(piece(total, iy ^ m, 2).astype(jnp.bfloat16), "gy", m).astype(jnp.float32)
                for m in range(1, gy)
            )
            total = over_z(
                piece(total, deep, 0),
                [piece(total, deep ^ m, 0).astype(jnp.bfloat16) for m in range(1, deeps)],
            )
            return total, send

        feature_cols, seed_cols = call(
            functools.partial(chip_cols_kernel, sides, ((0, 0),)),
            "own_cols",
            (shape((1, *columns.shape)),) * 2,
            (*chip, far_faces, far_faces),
            8,
            1,
        )
        feature_cols, seed_cols = feature_cols[0], seed_cols[0]
        second_grad, token = summed(second_terms_kernel, "second_terms", seed_cols)
        first_grad, _ = summed(first_terms_kernel, "first_terms", feature_cols)

    late = [chip[0], both, *both_side, *nears, *late_fars]
    result = shape((slots, 64, C), jnp.float32)
    output, input_grad = call(
        functools.partial(last_kernel, sides),
        "last_layer",
        (result, result),
        (*late, first_weight, second_weight, source, target, token),
        12,
        0.1,
        [pltpu.VMEM(columns.shape, jnp.bfloat16)] * 2,
        [VMEM] * (len(late) + 4) + [ANY],
    )
    return (
        output.reshape(features.shape),
        input_grad.reshape(features.shape),
        first_grad,
        second_grad,
    )


def solution(mesh):
    placed = (
        P("gx", "gy", None, None, None),
        P("gx", "gy", None),
        P("gx", "gy"),
        P(),
        P(),
        P("gx", "gy", None, None, None),
    )
    return jax.shard_map(
        per_device,
        mesh=mesh,
        in_specs=placed,
        out_specs=(
            P("gx", "gy", None, None, None),
            P("gx", "gy", None, None, None),
            P("gx", "gy"),
            P("gx", "gy"),
        ),
        check_vma=False,
    )
```
